32 devices in a mesh: dp: 8 (over z, x), seq: 4 (over y, core).
Axes of the slice: x: 2, y: 2, z: 4, core: 2. Of those that a mesh axis runs over, the one named last changes fastest.
Arguments:
- block_input: bfloat16 [2, 4096, 1024], P(None, ('dp', 'seq')), may hold values from -6 to 6
- positions: int32 [2, 4096], P(None, ('dp', 'seq')), may hold values from 0 to 249, as said below
- out_grad: bfloat16 [2, 4096, 1024], P(None, ('dp', 'seq')), may hold values from -6 to 6
- qkv_weight: bfloat16 [1024, 3072], P(('dp', 'seq')), may hold values from -0.1875 to 0.1875
- out_weight: bfloat16 [1024, 1024], P(('dp', 'seq')), may hold values from -1 to 1
- gate_weight: bfloat16 [1024, 4096], P(('dp', 'seq')), may hold values from -0.1875 to 0.1875
- up_weight: bfloat16 [1024, 4096], P(('dp', 'seq')), may hold values from -0.1875 to 0.1875
- down_weight: bfloat16 [4096, 1024], P(None, ('dp', 'seq')), may hold values from -0.125 to 0.125
- norm1_gain: bfloat16 [1024], P(('dp', 'seq')), may hold values from 0.5 to 1.5
- norm1_shift: bfloat16 [1024], P(('dp', 'seq')), may hold values from -2 to 2
- norm2_gain: bfloat16 [1024], P(('dp', 'seq')), may hold values from 0.5 to 1.5
- norm2_shift: bfloat16 [1024], P(('dp', 'seq')), may hold values from -2 to 2
- attn_scale: bfloat16 [1024], P(('dp', 'seq')), may hold values from 0.5 to 2
- mlp_scale: bfloat16 [1024], P(('dp', 'seq')), may hold values from 0.5 to 2
Outputs:
- output: bfloat16 [2, 4096, 1024], P(None, ('dp', 'seq'))
- input_grad: bfloat16 [2, 4096, 1024], P(None, ('dp', 'seq'))
- grad_qkv_weight: float32 [1024, 3072], P(('dp', 'seq'))
- grad_out_weight: float32 [1024, 1024], P(('dp', 'seq'))
- grad_gate_weight: float32 [1024, 4096], P(('dp', 'seq'))
- grad_up_weight: float32 [1024, 4096], P(('dp', 'seq'))
- grad_down_weight: float32 [4096, 1024], P(None, ('dp', 'seq'))
- grad_norm1_gain: float32 [1024], P(('dp', 'seq'))
- grad_norm1_shift: float32 [1024], P(('dp', 'seq'))
- grad_norm2_gain: float32 [1024], P(('dp', 'seq'))
- grad_norm2_shift: float32 [1024], P(('dp', 'seq'))
- grad_attn_scale: float32 [1024], P(('dp', 'seq'))
- grad_mlp_scale: float32 [1024], P(('dp', 'seq'))
The draws below stay inside these ranges and needn't reach their ends.
Inputs may be any that keep to these rules, and one draw needn't show every extreme that they name: Within a clip positions count up by one from 0; clips have 125 or 250 frames, laid end to end along the frames of a micro-batch; the clip of a micro-batch's first frame may begin before it, and the last clip may be cut.
All inputs are finite; a program needn't handle non-finite values.
Results may differ from the reference program's by a relative error of at most 0.02.
Values may be sent and summed in bfloat16 or wider, within the bound.
A program may use at most 512 MiB of HBM per device.

```python
import math
import jax
import jax.numpy as jnp
from jax import lax

D = 1024
H = 16
HD = 64
FF = 4096
WINDOW = 128
LONG_CLIP = 250
SHORT_CLIP = 125
MICRO = 2
GROUP = 512
FRAMES = 4096
N_DP = 8


def draw_positions(key, part):
    key = jax.random.fold_in(key, 7)
    count = FRAMES // SHORT_CLIP + 2

    def one_row(row_key):
        pick_key, shift_key = jax.random.split(row_key)
        longer = jax.random.randint(pick_key, (count,), 0, 2, dtype=jnp.int32)
        lengths = SHORT_CLIP + longer * (LONG_CLIP - SHORT_CLIP)
        ends = jnp.cumsum(lengths).astype(jnp.int32)
        offset = jax.random.randint(shift_key, (), 0, SHORT_CLIP, dtype=jnp.int32)
        frames = jnp.arange(FRAMES, dtype=jnp.int32) + offset
        which = jnp.searchsorted(ends, frames, side='right').astype(jnp.int32)
        begins = jnp.concatenate([jnp.zeros((1,), jnp.int32), ends])
        return (frames - begins[which]).astype(jnp.int32)
    return jax.vmap(one_row)(jax.random.split(key, MICRO))


def with_spikes(values, own_key, source, target, parts, factor):
    owner, partner = [(jnp.arange(values.shape[axis_at]) // (values.shape[axis_at] // parts)).reshape([-1 if axis == axis_at else 1 for axis in range(values.ndim)]) for axis_at in (source, target)]
    chosen = jax.random.permutation(own_key, parts)[partner]
    strong = (owner == chosen) | (owner == (partner + parts // 2) % parts)
    return jnp.where(strong, factor * values, values)


def levels(stream_key, shape, shards, least, largest):
    level, own = 1.0, jax.random.fold_in(stream_key, 6)
    for position, parts in shards:
        draws = jnp.exp(jax.random.uniform(jax.random.fold_in(own, position), (parts,), jnp.float32, least / len(shards), largest / len(shards)))
        level = level * jnp.repeat(draws, shape[position] // parts).reshape([-1 if axis == position else 1 for axis in range(len(shape))])
    return level


def scatter_about(rng, shape, deviation, bound, shards=(), held_as=jnp.bfloat16):
    values = jax.random.normal(rng, shape, jnp.float32) * deviation
    if len(shards) > 0:
        values = levels(rng, shape, shards, -0.22, 0.18) * values
    return jnp.clip(values, min=-bound, max=bound).astype(held_as)


def noise_with(key, shape, scale, most, cuts, heavy, kind=jnp.bfloat16):
    values = scale * jax.random.normal(key, shape, jnp.float32)
    if cuts:
        values = values * levels(key, shape, cuts, -0.22, 0.18)
    return jnp.clip(with_spikes(values, jax.random.fold_in(key, 3), *heavy), -most, most).astype(kind)


def setup_inputs(seed: int = 0) -> dict:
    key_list = jax.random.split(jax.random.key(seed), 15)
    return {
        "block_input": scatter_about(key_list[0], (MICRO, FRAMES, D), 1.0, 6.0, ((1, 32),)),
        "positions": draw_positions(jax.random.fold_in(key_list[14], 71), 0),
        "out_grad": noise_with(key_list[2], (MICRO, FRAMES, D), 1.0, 6.0, ((1, 32),), (1, 2, 32, 2.75)),
        "qkv_weight": scatter_about(key_list[3], (D, 3 * D), D ** -0.5, 0.1875, ((0, 32),)),
        "out_weight": scatter_about(key_list[4], (D, D), (D // 32) ** -0.5, 1.0, ((0, 32),)),
        "gate_weight": scatter_about(key_list[5], (D, FF), D ** -0.5, 0.1875, ((0, 32),)),
        "up_weight": scatter_about(key_list[6], (D, FF), D ** -0.5, 0.1875, ((0, 32),)),
        "down_weight": scatter_about(key_list[7], (FF, D), (FF // 2) ** -0.5, 0.125, ((1, 32),)),
        "norm1_gain": jnp.clip(1.0 + 0.1 * jax.random.normal(key_list[8], (D,), jnp.float32), 0.5, 1.5).astype(jnp.bfloat16),
        "norm1_shift": scatter_about(key_list[9], (D,), 0.3, 2.0, ((0, 32),)),
        "norm2_gain": jnp.clip(1.0 + 0.1 * jax.random.normal(key_list[10], (D,), jnp.float32), 0.5, 1.5).astype(jnp.bfloat16),
        "norm2_shift": scatter_about(key_list[11], (D,), 0.3, 2.0, ((0, 32),)),
        "attn_scale": jnp.clip(jnp.exp(math.log(2.0) - 1.3862944 * jax.random.uniform(key_list[12], (D,), jnp.float32) ** levels(key_list[12], (D,), ((0, 32),), -0.2, 0.2)), 0.5, 2.0).astype(jnp.bfloat16),
        "mlp_scale": jnp.clip(jnp.exp(math.log(2.0) - 1.3862944 * jax.random.uniform(key_list[13], (D,), jnp.float32) ** levels(key_list[13], (D,), ((0, 32),), -0.2, 0.2)), 0.5, 2.0).astype(jnp.bfloat16),
    }


EPSILON = 1e-05
NEGATIVE = -1e+30
HIGHEST = lax.Precision.HIGHEST

@jax.custom_vjp
def low(v):
    return lax.optimization_barrier(v.astype(jnp.bfloat16)).astype(jnp.float32)

@jax.custom_vjp
def low_back(v):
    return v

def low_keep(v):
    return (low(v), None)

def low_pass(kept, grad):
    return (grad,)

def back_keep(v):
    return (v, None)

def back_low(kept, grad):
    return (low(grad),)
low.defvjp(low_keep, low_pass)
low_back.defvjp(back_keep, back_low)

def layer_norm(values, gain, shift):
    center = values - lax.optimization_barrier(jnp.mean(values, axis=-1, keepdims=True))
    inverse = lax.rsqrt(lax.optimization_barrier(jnp.mean(center * center, axis=-1, keepdims=True)) + EPSILON)
    return center * inverse * gain + shift

def angles_of(places, size):
    inverse = 10000.0 ** (-(jnp.arange(size // 2, dtype=jnp.float32) * (2.0 / size)))
    return places.astype(jnp.float32)[:, None] * inverse[None, :]

def rotate(values, angles):
    half = values.shape[-1] // 2
    cosine = jnp.cos(angles)[:, None, :]
    sine = jnp.sin(angles)[:, None, :]
    first_half = values[..., :half]
    second_half = values[..., half:]
    return jnp.concatenate([first_half * cosine - second_half * sine, second_half * cosine + first_half * sine], axis=-1)

def attend(query, keyset, valueset, starts):
    length = query.shape[0]
    size = min(512, length)
    count = length // size
    padding = jnp.zeros((WINDOW,) + keyset.shape[1:], jnp.float32)
    keys_padded = jnp.concatenate([padding, keyset], axis=0)
    values_padded = jnp.concatenate([padding, valueset], axis=0)
    factor = HD ** (-0.5)

    def block(index):
        first = index * size
        block_query = lax.dynamic_slice_in_dim(query, first, size, 0)
        block_keys = lax.dynamic_slice_in_dim(keys_padded, first, size + WINDOW, 0)
        block_values = lax.dynamic_slice_in_dim(values_padded, first, size + WINDOW, 0)
        begin = lax.dynamic_slice_in_dim(starts, first, size, 0)
        here = first + jnp.arange(size, dtype=jnp.int32)
        there = first - WINDOW + jnp.arange(size + WINDOW, dtype=jnp.int32)
        allowed = (there[None, :] >= begin[:, None]) & (there[None, :] <= here[:, None]) & (here[:, None] - there[None, :] < WINDOW)
        raw = low_back(jnp.einsum('qhd,khd->hqk', block_query, block_keys, precision=HIGHEST))
        scores = jnp.where(allowed[None], raw * factor, NEGATIVE)
        top = lax.optimization_barrier(jnp.max(scores, axis=-1, keepdims=True))
        exponent = jnp.exp(scores - top)
        probs = exponent / lax.optimization_barrier(jnp.sum(exponent, axis=-1, keepdims=True))
        return jnp.einsum('hqk,khd->qhd', low(probs), block_values, precision=HIGHEST)
    outcome = lax.map(jax.checkpoint(block), jnp.arange(count, dtype=jnp.int32))
    return outcome.reshape(query.shape)

def forward(params, values, places):
    qkv_weight, out_weight, gate_weight, up_weight, down_weight, gain1, shift1, gain2, shift2, scale1, scale2 = params
    length = values.shape[0]
    normed1 = low(layer_norm(values, gain1, shift1))
    projected = low_back(jnp.dot(normed1, qkv_weight, precision=HIGHEST))
    angles = angles_of(places, HD)
    query = low(low_back(rotate(projected[:, :D].reshape(length, H, HD), angles)))
    keyset = low(low_back(rotate(projected[:, D:2 * D].reshape(length, H, HD), angles)))
    valueset = low(low_back(projected[:, 2 * D:].reshape(length, H, HD)))
    starts = jnp.maximum(jnp.arange(length, dtype=jnp.int32) - places, 0)
    attended = low(low_back(attend(query, keyset, valueset, starts).reshape(length, D)))
    attn = low_back(jnp.dot(attended, out_weight, precision=HIGHEST))
    mid = values + scale1 * attn
    normed2 = low(layer_norm(mid, gain2, shift2))
    gate = low_back(jnp.dot(normed2, gate_weight, precision=HIGHEST))
    up = low_back(jnp.dot(normed2, up_weight, precision=HIGHEST))
    hidden = low(jax.nn.silu(gate) * up)
    branch = low_back(jnp.dot(hidden, down_weight, precision=HIGHEST))
    return mid + scale2 * branch

def reference(block_input, positions, out_grad, qkv_weight, out_weight, gate_weight, up_weight, down_weight, norm1_gain, norm1_shift, norm2_gain, norm2_shift, attn_scale, mlp_scale):
    params = tuple((item.astype(jnp.float32) for item in (qkv_weight, out_weight, gate_weight, up_weight, down_weight, norm1_gain, norm1_shift, norm2_gain, norm2_shift, attn_scale, mlp_scale)))
    count = MICRO * N_DP
    inputs = block_input.astype(jnp.float32).reshape(count, GROUP, D)
    places = positions.reshape(count, GROUP)
    cotangents = out_grad.astype(jnp.float32).reshape(count, GROUP, D)

    def one_group(totals, item):
        block, where_at, cotangent = item

        def apply(weights, values):
            return forward(weights, values, where_at)
        result, pull = jax.vjp(apply, params, block)
        grads, grad_block = pull(cotangent)
        totals = tuple((first_term + second_term for first_term, second_term in zip(totals, grads)))
        return (totals, (result.astype(jnp.bfloat16), grad_block.astype(jnp.bfloat16)))
    zeros = tuple((jnp.zeros(item.shape, jnp.float32) for item in params))
    totals, (results, grads_in) = lax.scan(one_group, zeros, (inputs, places, cotangents))
    output = results.reshape(block_input.shape)
    input_grad = grads_in.reshape(block_input.shape)
    return (output, input_grad, totals[0], totals[1], totals[2], totals[3], totals[4], totals[5], totals[6], totals[7], totals[8], totals[9], totals[10])
```

```python
import jax
import jax.numpy as jnp
import ml_dtypes
import numpy as np
from jax import lax
from jax.experimental import pallas as pl
from jax.experimental.pallas import tpu as pltpu
from jax.sharding import PartitionSpec as P

H = 16
HD = 64
WINDOW = 128


EPSILON = 1e-05
NEGATIVE = -1e30


def normalize(values, gain, shift):
    center = values - jnp.mean(values, axis=-1, keepdims=True)
    inverse = lax.rsqrt(jnp.mean(center * center, axis=-1, keepdims=True) + EPSILON)
    unit = center * inverse
    return (unit * gain + shift, unit, inverse)


def normalize_back(incoming, unit, inverse, gain):
    scaled = incoming * gain
    middle = (
        scaled
        - jnp.mean(scaled, axis=-1, keepdims=True)
        - unit * jnp.mean(scaled * unit, axis=-1, keepdims=True)
    )
    return (inverse * middle, jnp.sum(incoming * unit, axis=0), jnp.sum(incoming, axis=0))


def angles_of(places, size):
    inverse = 10000.0 ** (-(jnp.arange(size // 2, dtype=jnp.float32) * (2.0 / size)))
    return places.astype(jnp.float32)[:, None] * inverse[None, :]


def rotate(values, angles):
    half = values.shape[-1] // 2
    cosine = jnp.cos(angles)[:, None, :]
    sine = jnp.sin(angles)[:, None, :]
    first_half = values[..., :half]
    second_half = values[..., half:]
    return jnp.concatenate(
        [first_half * cosine - second_half * sine, second_half * cosine + first_half * sine],
        axis=-1,
    )


def unrotate(values, angles):
    half = values.shape[-1] // 2
    cosine = jnp.cos(angles)[:, None, :]
    sine = jnp.sin(angles)[:, None, :]
    first_half = values[..., :half]
    second_half = values[..., half:]
    return jnp.concatenate(
        [first_half * cosine + second_half * sine, second_half * cosine - first_half * sine],
        axis=-1,
    )


def pack_shards(shards):
    return jnp.concatenate([item.reshape(1, -1) for item in shards], axis=1)


def unpack_gathered(whole, shards):
    devices = whole.shape[0]
    result = []
    offset = 0
    for number, item in enumerate(shards):
        count = item.size
        piece = whole[:, offset : offset + count]
        offset = offset + count
        if number == 4:
            rows, cols = item.shape
            result.append(
                piece.reshape(devices, rows, cols).transpose(1, 0, 2).reshape(rows, devices * cols)
            )
        elif item.ndim == 2:
            result.append(piece.reshape(devices * item.shape[0], item.shape[1]))
        else:
            result.append(piece.reshape(-1))
    return tuple(result)


def pack_grads(totals, devices):
    pieces = []
    for number, item in enumerate(totals):
        if number == 4:
            rows, cols = item.shape
            pieces.append(
                item.reshape(rows, devices, cols // devices).transpose(1, 0, 2).reshape(devices, -1)
            )
        else:
            pieces.append(item.reshape(devices, -1))
    return jnp.concatenate(pieces, axis=1)


def unpack_summed(summed, shards):
    flat = summed.reshape(-1)
    result = []
    offset = 0
    for item in shards:
        count = item.size
        result.append(flat[offset : offset + count].reshape(item.shape))
        offset = offset + count
    return tuple(result)


def block_scores(query, keys_padded, values_padded, starts, first, size):
    block_query = lax.dynamic_slice_in_dim(query, first, size, 0)
    block_keys = lax.dynamic_slice_in_dim(keys_padded, first, size + WINDOW, 0)
    block_values = lax.dynamic_slice_in_dim(values_padded, first, size + WINDOW, 0)
    begin = lax.dynamic_slice_in_dim(starts, first, size, 0)
    here = first + jnp.arange(size, dtype=jnp.int32)
    there = first - WINDOW + jnp.arange(size + WINDOW, dtype=jnp.int32)
    allowed = (
        (there[None, :] >= begin[:, None])
        & (there[None, :] <= here[:, None])
        & (here[:, None] - there[None, :] < WINDOW)
    )
    raw = jnp.einsum("qhd,khd->hqk", block_query, block_keys, preferred_element_type=jnp.float32)
    scores = jnp.where(allowed[None], raw * HD ** (-0.5), NEGATIVE)
    return (scores, block_query, block_keys, block_values)


def attend_forward(query, keys_padded, values_padded, starts):
    length = query.shape[0]
    size = min(512, length)
    count = length // size

    def step(carry, index):
        scores, block_query, block_keys, block_values = block_scores(
            query, keys_padded, values_padded, starts, index * size, size
        )
        top = jnp.max(scores, axis=-1, keepdims=True)
        exponent = jnp.exp(scores - top)
        total = jnp.sum(exponent, axis=-1, keepdims=True)
        probs = (exponent / total).astype(jnp.bfloat16)
        outcome = jnp.einsum(
            "hqk,khd->qhd", probs, block_values, preferred_element_type=jnp.float32
        )
        return (carry, (outcome, (top + jnp.log(total))[..., 0]))

    unused, (outcomes, logs) = lax.scan(step, 0, jnp.arange(count, dtype=jnp.int32))
    return (outcomes.reshape(query.shape), logs)


def attend_backward(query, keys_padded, values_padded, starts, logs, grad_out):
    length = query.shape[0]
    size = min(512, length)
    count = length // size

    def step(carry, index):
        grad_query, grad_keys, grad_values = carry
        first = index * size
        scores, block_query, block_keys, block_values = block_scores(
            query, keys_padded, values_padded, starts, first, size
        )
        probs = jnp.exp(scores - logs[index][..., None])
        grad_block = lax.dynamic_slice_in_dim(grad_out, first, size, 0)
        grad_probs = jnp.einsum(
            "qhd,khd->hqk", grad_block, block_values, preferred_element_type=jnp.float32
        )
        inner = jnp.sum(probs * grad_probs, axis=-1, keepdims=True)
        grad_scores = (probs * (grad_probs - inner) * HD ** (-0.5)).astype(jnp.bfloat16)
        query_part = jnp.einsum(
            "hqk,khd->qhd", grad_scores, block_keys, preferred_element_type=jnp.float32
        )
        keys_part = jnp.einsum(
            "hqk,qhd->khd", grad_scores, block_query, preferred_element_type=jnp.float32
        )
        values_part = jnp.einsum(
            "hqk,qhd->khd",
            probs.astype(jnp.bfloat16),
            grad_block,
            preferred_element_type=jnp.float32,
        )
        grad_query = lax.dynamic_update_slice_in_dim(grad_query, query_part, first, 0)
        grad_keys = lax.dynamic_update_slice_in_dim(
            grad_keys,
            lax.dynamic_slice_in_dim(grad_keys, first, size + WINDOW, 0) + keys_part,
            first,
            0,
        )
        grad_values = lax.dynamic_update_slice_in_dim(
            grad_values,
            lax.dynamic_slice_in_dim(grad_values, first, size + WINDOW, 0) + values_part,
            first,
            0,
        )
        return ((grad_query, grad_keys, grad_values), None)

    start_state = (
        jnp.zeros(query.shape, jnp.float32),
        jnp.zeros(keys_padded.shape, jnp.float32),
        jnp.zeros(values_padded.shape, jnp.float32),
    )
    (grad_query, grad_keys, grad_values), unused = lax.scan(
        step, start_state, jnp.arange(count, dtype=jnp.int32)
    )
    return (grad_query, grad_keys, grad_values)


def attention_forward(query, keyset, valueset, places):
    rows, heads, depth = query.shape
    width = heads * depth
    parts = lax.axis_size("seq")
    slab = width // parts
    local = slab // depth
    packed = jnp.stack(
        [query.reshape(rows, width), keyset.reshape(rows, width), valueset], axis=1
    ).reshape(rows, 3, parts, slab)
    moved = lax.all_to_all(packed, "seq", split_axis=2, concat_axis=0, tiled=True)
    group = moved.shape[0]
    every = lax.all_gather(places, "seq", axis=0, tiled=True)
    starts = jnp.maximum(jnp.arange(group, dtype=jnp.int32) - every, 0)
    padding = jnp.zeros((WINDOW, local, depth), jnp.bfloat16)
    head_query = moved[:, 0, 0].reshape(group, local, depth)
    keys_padded = jnp.concatenate([padding, moved[:, 1, 0].reshape(group, local, depth)], axis=0)
    values_padded = jnp.concatenate([padding, moved[:, 2, 0].reshape(group, local, depth)], axis=0)
    outcome, logs = attend_forward(head_query, keys_padded, values_padded, starts)
    sent = outcome.astype(jnp.bfloat16).reshape(group, 1, slab)
    attended = lax.all_to_all(sent, "seq", split_axis=0, concat_axis=1, tiled=True).reshape(
        rows, width
    )
    return (attended, (head_query, keys_padded, values_padded, starts, logs))


def attention_backward(kept, grad_attended, rows, width):
    head_query, keys_padded, values_padded, starts, logs = kept
    depth = head_query.shape[-1]
    parts = lax.axis_size("seq")
    slab = width // parts
    local = slab // depth
    came = lax.all_to_all(
        grad_attended.reshape(rows, parts, slab), "seq", split_axis=1, concat_axis=0, tiled=True
    )
    group = came.shape[0]
    grad_out = came.reshape(group, local, depth)
    grad_query, grad_keys, grad_values = attend_backward(
        head_query, keys_padded, values_padded, starts, logs, grad_out
    )
    packed = (
        jnp.stack([grad_query, grad_keys[WINDOW:], grad_values[WINDOW:]], axis=1)
        .astype(jnp.bfloat16)
        .reshape(group, 3, 1, slab)
    )
    back = lax.all_to_all(packed, "seq", split_axis=0, concat_axis=2, tiled=True).reshape(
        rows, 3, width
    )
    return (back[:, 0], back[:, 1], back[:, 2])


def forward_micro(weights, block, places):
    (
        qkv_weight,
        out_weight,
        gate_weight,
        up_weight,
        down_weight,
        gain1,
        shift1,
        gain2,
        shift2,
        scale1,
        scale2,
    ) = weights
    rows, width = block.shape
    start_in = block.astype(jnp.float32)
    normed1, unit1, inverse1 = normalize(start_in, gain1, shift1)
    acted1 = normed1.astype(jnp.bfloat16)
    projected = jnp.dot(acted1, qkv_weight, preferred_element_type=jnp.float32)
    angles = angles_of(places, HD)
    query = rotate(projected[:, :width].reshape(rows, H, HD), angles).astype(jnp.bfloat16)
    keyset = rotate(projected[:, width : 2 * width].reshape(rows, H, HD), angles).astype(
        jnp.bfloat16
    )
    valueset = projected[:, 2 * width :].astype(jnp.bfloat16)
    attended, kept = attention_forward(query, keyset, valueset, places)
    attn = jnp.dot(attended, out_weight, preferred_element_type=jnp.float32)
    mid = start_in + scale1 * attn
    normed2, unit2, inverse2 = normalize(mid, gain2, shift2)
    acted2 = normed2.astype(jnp.bfloat16)
    gate = jnp.dot(acted2, gate_weight, preferred_element_type=jnp.float32)
    up_value = jnp.dot(acted2, up_weight, preferred_element_type=jnp.float32)
    hidden = (jax.nn.silu(gate) * up_value).astype(jnp.bfloat16)
    branch = jnp.dot(hidden, down_weight, preferred_element_type=jnp.float32)
    result = (mid + scale2 * branch).astype(jnp.bfloat16)
    saved = (
        acted1,
        unit1,
        inverse1,
        angles,
        kept,
        attended,
        attn,
        unit2,
        inverse2,
        acted2,
        gate,
        up_value,
        hidden,
        branch,
    )
    return (result, saved)


def backward_micro(weights, saved, cotangent):
    (
        qkv_weight,
        out_weight,
        gate_weight,
        up_weight,
        down_weight,
        gain1,
        shift1,
        gain2,
        shift2,
        scale1,
        scale2,
    ) = weights
    (
        acted1,
        unit1,
        inverse1,
        angles,
        kept,
        attended,
        attn,
        unit2,
        inverse2,
        acted2,
        gate,
        up_value,
        hidden,
        branch,
    ) = saved
    rows, width = attended.shape
    flow = cotangent.astype(jnp.float32)
    grad_branch = (scale2 * flow).astype(jnp.bfloat16)
    grad_scale2 = jnp.sum(flow * branch, axis=0)
    grad_down = jnp.einsum("rf,rd->fd", hidden, grad_branch, preferred_element_type=jnp.float32)
    grad_hidden = jnp.einsum(
        "rd,fd->rf", grad_branch, down_weight, preferred_element_type=jnp.float32
    )
    sigmoid_gate = jax.nn.sigmoid(gate)
    grad_gate = (
        grad_hidden * up_value * sigmoid_gate * (1.0 + gate * (1.0 - sigmoid_gate))
    ).astype(jnp.bfloat16)
    grad_up = (grad_hidden * gate * sigmoid_gate).astype(jnp.bfloat16)
    grad_gate_w = jnp.einsum("rd,rf->df", acted2, grad_gate, preferred_element_type=jnp.float32)
    grad_up_w = jnp.einsum("rd,rf->df", acted2, grad_up, preferred_element_type=jnp.float32)
    grad_acted2 = jnp.einsum(
        "rf,df->rd", grad_gate, gate_weight, preferred_element_type=jnp.float32
    ) + jnp.einsum("rf,df->rd", grad_up, up_weight, preferred_element_type=jnp.float32)
    grad_mid, grad_gain2, grad_shift2 = normalize_back(grad_acted2, unit2, inverse2, gain2)
    grad_mid = flow + grad_mid
    grad_scale1 = jnp.sum(grad_mid * attn, axis=0)
    grad_attn = (scale1 * grad_mid).astype(jnp.bfloat16)
    grad_out_w = jnp.einsum("rd,re->de", attended, grad_attn, preferred_element_type=jnp.float32)
    grad_attended = jnp.einsum(
        "re,de->rd", grad_attn, out_weight, preferred_element_type=jnp.float32
    ).astype(jnp.bfloat16)
    grad_query, grad_keys, grad_values = attention_backward(kept, grad_attended, rows, width)
    query_plain = unrotate(grad_query.astype(jnp.float32).reshape(rows, H, HD), angles).reshape(
        rows, width
    )
    keys_plain = unrotate(grad_keys.astype(jnp.float32).reshape(rows, H, HD), angles).reshape(
        rows, width
    )
    grad_projected = jnp.concatenate(
        [query_plain, keys_plain, grad_values.astype(jnp.float32)], axis=1
    ).astype(jnp.bfloat16)
    grad_qkv_w = jnp.einsum("rd,re->de", acted1, grad_projected, preferred_element_type=jnp.float32)
    grad_acted1 = jnp.einsum(
        "re,de->rd", grad_projected, qkv_weight, preferred_element_type=jnp.float32
    )
    grad_first, grad_gain1, grad_shift1 = normalize_back(grad_acted1, unit1, inverse1, gain1)
    grad_input = (grad_mid + grad_first).astype(jnp.bfloat16)
    terms = (
        grad_qkv_w,
        grad_out_w,
        grad_gate_w,
        grad_up_w,
        grad_down,
        grad_gain1,
        grad_shift1,
        grad_gain2,
        grad_shift2,
        grad_scale1,
        grad_scale2,
    )
    return (grad_input, terms)


def body(
    block_input,
    positions,
    out_grad,
    qkv_weight,
    out_weight,
    gate_weight,
    up_weight,
    down_weight,
    norm1_gain,
    norm1_shift,
    norm2_gain,
    norm2_shift,
    attn_scale,
    mlp_scale,
):
    shards = (
        qkv_weight,
        out_weight,
        gate_weight,
        up_weight,
        down_weight,
        norm1_gain,
        norm1_shift,
        norm2_gain,
        norm2_shift,
        attn_scale,
        mlp_scale,
    )
    devices = lax.axis_size(("dp", "seq"))
    outer = lax.axis_size("dp")
    inner = lax.axis_size("seq")
    packed = pack_shards(shards)
    totals = None
    results = []
    grads_in = []
    for index in range(block_input.shape[0]):
        weights = unpack_gathered(lax.all_gather(packed, ("dp", "seq"), axis=0, tiled=True), shards)
        result, saved = forward_micro(weights, block_input[index], positions[index])
        backward_weights = unpack_gathered(
            lax.all_gather(packed, ("dp", "seq"), axis=0, tiled=True), shards
        )
        grad_input, terms = backward_micro(backward_weights, saved, out_grad[index])
        if totals is None:
            totals = terms
        else:
            totals = tuple(
                (first_term + second_term for first_term, second_term in zip(totals, terms))
            )
        results.append(result)
        grads_in.append(grad_input)
    laid = pack_grads(totals, devices)
    laid = laid.reshape(outer, inner, laid.shape[1])
    partial_sum = lax.psum_scatter(laid.astype(jnp.bfloat16), "dp", scatter_dimension=0, tiled=True)
    summed = lax.psum_scatter(partial_sum, "seq", scatter_dimension=1, tiled=True).astype(
        jnp.float32
    )
    return (jnp.stack(results), jnp.stack(grads_in)) + unpack_summed(summed, shards)


VMEM_BYTES = 64 * 1024 * 1024
BF = jnp.bfloat16
F32 = jnp.float32
MESH = pl.DeviceIdType.MESH
TEAM = 8
PLACES = 256
RELATIONS = [(1, 0, 0), (0, 1, 0), (1, 1, 0), (0, 0, 1), (1, 0, 1), (0, 1, 1), (1, 1, 1)]
ROW_TEAM = (1, 3, 5)
LEG = (None, 0)


def trig_table():
    inverse = 10000.0 ** (-(np.arange(HD // 2, dtype=np.float64) * (2.0 / HD)))
    angles = np.arange(PLACES, dtype=np.float64)[:, None] * inverse[None, :]
    values = np.concatenate([np.cos(angles), np.sin(angles)] * 2, axis=1).astype(np.float32)
    high = values.astype(ml_dtypes.bfloat16)
    rest = (values - high.astype(np.float32)).astype(ml_dtypes.bfloat16)
    return np.concatenate([high, rest], axis=1)


def dot(a, b):
    return lax.dot_general(a, b, (((1,), (0,)), ((), ())), preferred_element_type=F32)


def dot_rows(a, b):
    return lax.dot_general(a, b, (((1,), (1,)), ((), ())), preferred_element_type=F32)


def dot_cols(a, b):
    return lax.dot_general(a, b, (((0,), (0,)), ((), ())), preferred_element_type=F32)


def sigmoid(v):
    return 0.5 * jnp.tanh(0.5 * v) + 0.5


def unit_of(values):
    center = values - jnp.mean(values, axis=-1, keepdims=True)
    inverse = lax.rsqrt(jnp.mean(center * center, axis=-1, keepdims=True) + EPSILON)
    return center * inverse, inverse


def layer_kernel(
    x_ref, g_ref, vec_ref, table_ref, qkv_ref, out_ref, gate_ref, up_ref, down_ref,
    y_ref, dx_ref, vg_ref, fin_a, fin_m, zq_ref, zo_ref, zg_ref, zd_ref,
    vec_all, vecs, gacc, gv_in, gv_z, gv_send, gv_all,
    pack_a, pack_m, w0, w1, w2, outw,
    n1, n2, db, da, qkv, att, probs, dqs, dkv, hid, dgu,
    send_a, recv_c, recv_d, send_b, send_a0, recv_c0, recv_d0,
    stage_q, stage_o, stage_g, stage_d, own_q, own_o, own_g, own_d, gout, gsend,
    side_q, side_o, keep_q, send_q, relay_g, relay_d, relay_q, relay_o,
    mid, attn, trig, pos,
    vec_ss, vec_rs, wr_ss, wr_rs, wa_ss, wa_rs, w_ss, w_rs, o_ss, o_rs, ga_ss, ga_rs, ag_ss, ag_rs,
    ra_ss, ra_rs, rs_ss, rs_rs, go_ss, go_rs, sx_ss, sx_rs, z_ss, z_rs, f_ss, f_rs,
    gv_ss, gv_rs, loc_sem,
):
    dp = lax.axis_index("dp")
    sq = lax.axis_index("seq")
    z, xi, y, c = dp // 2, dp % 2, sq // 2, sq % 2
    me = xi * 4 + sq
    chip = xi * 2 + y

    def copy(src, dst, ss, rs, device):
        return pltpu.make_async_remote_copy(
            src_ref=src, dst_ref=dst, send_sem=ss, recv_sem=rs,
            device_id=device, device_id_type=MESH,
        )

    def span(start, size):
        return pl.ds(pl.multiple_of(start, size), size)

    def team(k):
        kx, ky, kc = RELATIONS[k]
        xx, yy, cc = (xi + kx) % 2, (y + ky) % 2, (c + kc) % 2
        return (z * 2 + xx, yy * 2 + cc), xx * 4 + yy * 2 + cc

    def level(j):
        zz = (z + j) % 4
        return (zz * 2 + xi, sq), zz

    teams = [team(k) for k in range(7)]
    levels = [level(j) for j in range(1, 4)]
    sources = [(z + 4 - j) % 4 for j in range(1, 4)]
    across, beside, sibling = teams[0][0], teams[1][0], teams[3][0]
    chips = [(1 - xi) * 2 + y, xi * 2 + (1 - y), (1 - xi) * 2 + (1 - y)]

    pending = []
    pack_sends = []
    barrier = pltpu.get_barrier_semaphore()
    for device, _ in teams + levels:
        pl.semaphore_signal(barrier, inc=1, device_id=device, device_id_type=MESH)

    for t in range(4):
        for b in range(3):
            pack_a[32 * t : 32 * t + 32, 256 * b : 256 * b + 256] = qkv_ref[
                :, 1024 * b + 256 * t : 1024 * b + 256 * t + 256
            ]
        pack_a[32 * t : 32 * t + 32, 768:1024] = out_ref[:, 256 * t : 256 * t + 256]
    lane = lax.broadcasted_iota(jnp.int32, (8, 128), 1)
    sub = lax.broadcasted_iota(jnp.int32, (8, 128), 0)
    vec_all[z, me] = jnp.where((sub >= 6) | (lane // 32 == me % 4), vec_ref[...], 0.0)
    gacc[...] = jnp.zeros_like(gacc)
    pl.semaphore_wait(barrier, 10)

    def begin(item):
        item.start()
        pending.append(item)

    for k, (device, _) in enumerate(teams):
        begin(copy(vec_all.at[z, me], vec_all.at[z, me], vec_ss.at[k], vec_rs.at[k], device))

    my_rows = span((z * 8 + me) * 32, 32)
    w0[my_rows, :] = pack_a[span(sq * 32, 32), :]
    for i, k in enumerate(ROW_TEAM):
        device, g = teams[k]
        begin(
            copy(pack_a.at[span((g % 4) * 32, 32), :], w0.at[my_rows, :], wr_ss.at[i], wr_rs.at[i],
                 device)
        )
    for t in range(TEAM):
        pack_m[32 * t : 32 * t + 32, 0:512] = gate_ref[:, 512 * t : 512 * t + 512]
        pack_m[32 * t : 32 * t + 32, 512:1024] = up_ref[:, 512 * t : 512 * t + 512]
        pack_m[32 * t : 32 * t + 32, 1024:1536] = down_ref[:, 512 * t : 512 * t + 512]

    jumps = [z == 3, None, z == 0]
    passes = (z == 1) | (z == 2)

    def rise(ref, piece, ss, rs, base):
        for j in (1, 0, 2):
            item = copy(
                ref.at[piece(z)], ref.at[piece(z)], ss.at[base + j], rs.at[base + j], levels[j][0]
            )
            if jumps[j] is None:
                begin(item)
            else:
                pl.when(jnp.logical_not(jumps[j]))(item.start)
                pending.append((jumps[j], item))

    def rise_pass(ref, piece, ss, rs, base):
        arrived = ref.at[piece(sources[1])]
        copy(arrived, arrived, ss.at[base + 1], rs.at[base + 1], levels[1][0]).wait_recv()
        slot = jnp.where(z == 1, 0, 2)
        end = jnp.where(z == 1, 0, 3)
        item = copy(arrived, arrived, ss.at[base + 3], rs.at[base + slot], (end * 2 + xi, sq))
        pl.when(passes)(item.start)
        pending.append((jnp.logical_not(passes), item))

    def rise_wait(ref, piece, ss, rs, base, j):
        arrived = ref.at[piece(sources[j])]
        copy(arrived, arrived, ss.at[base + j], rs.at[base + j], levels[j][0]).wait_recv()

    groups = [(w1, 0, 1024), (w2, 1024, 512)]

    def level_rows(zz):
        return span(zz * 256, 256)

    def weights_out(n):
        ref, first, width = groups[n]
        ref[my_rows, :] = pack_m[span(me * 32, 32), first : first + width]
        for k, (device, g) in enumerate(teams):
            item = copy(
                pack_m.at[span(g * 32, 32), pl.ds(first, width)],
                ref.at[my_rows, :], w_ss.at[n, k], w_rs.at[n, k], device,
            )
            item.start()
            pack_sends.append(item)

    def weights_up(n):
        ref = groups[n][0]
        for k, (device, g) in enumerate(teams):
            rows = span((z * 8 + g) * 32, 32)
            copy(ref.at[rows, :], ref.at[rows, :], w_ss.at[n, k], w_rs.at[n, k], device).wait_recv()
        rise(ref, level_rows, w_ss.at[n], w_rs.at[n], 7)

    def weights_pass(n):
        rise_pass(groups[n][0], level_rows, w_ss.at[n], w_rs.at[n], 7)

    def weights_in(n):
        for j in (0, 2):
            rise_wait(groups[n][0], level_rows, w_ss.at[n], w_rs.at[n], 7, j)

    halves = [pl.ds(0, 768), pl.ds(768, 256)]

    def slab(n, zz, xx):
        return span((zz * 2 + xx) * 128, 128), halves[n]

    def slab_up(n):
        rise(w0, lambda zz: slab(n, zz, xi), wa_ss.at[n], wa_rs.at[n], 0)
        mine = w0.at[slab(n, z, xi)]
        begin(copy(mine, mine, wa_ss.at[n, 4], wa_rs.at[n, 4], across))

    def slab_pass(n):
        rise_pass(w0, lambda zz: slab(n, zz, xi), wa_ss.at[n], wa_rs.at[n], 0)
        for j in (1, 0, 2):
            if j != 1:
                rise_wait(w0, lambda zz: slab(n, zz, xi), wa_ss.at[n], wa_rs.at[n], 0, j)
            block = w0.at[slab(n, sources[j], xi)]
            begin(copy(block, block, wa_ss.at[n, 5 + j], wa_rs.at[n, 5 + j], across))

    def slab_in(n):
        for j in range(4):
            block = w0.at[slab(n, z if j == 0 else sources[j - 1], 1 - xi)]
            copy(block, block, wa_ss.at[n, 4 + j], wa_rs.at[n, 4 + j], across).wait_recv()

    for k, (device, g) in enumerate(teams):
        copy(vec_all.at[z, g], vec_all.at[z, g], vec_ss.at[k], vec_rs.at[k], device).wait_recv()
    for j, (device, _) in enumerate(levels):
        begin(copy(vec_all.at[z], vec_all.at[z], vec_ss.at[7 + j], vec_rs.at[7 + j], device))
    for i, k in enumerate(ROW_TEAM):
        device, g = teams[k]
        rows = w0.at[span((z * 8 + g) * 32, 32), :]
        copy(rows, rows, wr_ss.at[i], wr_rs.at[i], device).wait_recv()
    slab_up(0)
    for j in range(3):
        block = vec_all.at[sources[j]]
        copy(block, block, vec_ss.at[7 + j], vec_rs.at[7 + j], levels[j][0]).wait_recv()
    for k in range(8):
        total = vec_all[k // 2, 4 * (k % 2)]
        for j in range(1, 4):
            total = total + vec_all[k // 2, 4 * (k % 2) + j]
        vecs[:, 128 * k : 128 * k + 128] = total

    def vector(n):
        return vecs[n : n + 1, :]

    def row_rows(m, cc, yy):
        return span(m * 512 + cc * 256 + yy * 128, 128)

    def row_start(ref, e, m):
        block = ref.at[row_rows(m, c, y), :]
        begin(copy(block, block, ga_ss.at[e, m, 0], ga_rs.at[e, m, 0], beside))
        begin(copy(block, block, ga_ss.at[e, m, 1], ga_rs.at[e, m, 1], sibling))

    def row_pass(ref, e, m):
        block = ref.at[row_rows(m, c, 1 - y), :]
        copy(block, block, ga_ss.at[e, m, 0], ga_rs.at[e, m, 0], beside).wait_recv()
        begin(copy(block, block, ga_ss.at[e, m, 2], ga_rs.at[e, m, 2], sibling))

    def row_end(ref, e, m):
        for which, yy in ((1, y), (2, 1 - y)):
            block = ref.at[row_rows(m, 1 - c, yy), :]
            copy(block, block, ga_ss.at[e, m, which], ga_rs.at[e, m, which], sibling).wait_recv()

    def slot_rows(m, cc, place):
        return span(m * 1024 + cc * 512 + place * 128, 128)

    def gather_start(ref, e, m):
        block = ref.at[slot_rows(m, c, chip), :]
        for r in (0, 1, 3):
            begin(copy(block, block, ag_ss.at[e, m, r], ag_rs.at[e, m, r], teams[r][0]))

    def gather_hand(ref, e, m, r):
        block = ref.at[slot_rows(m, c, chips[r]), :]
        copy(block, block, ag_ss.at[e, m, r], ag_rs.at[e, m, r], teams[r][0]).wait_recv()
        begin(copy(block, block, ag_ss.at[e, m, 4 + r], ag_rs.at[e, m, 4 + r], sibling))

    def gather_pass(ref, e, m, last):
        first = 1 - last
        gather_hand(ref, e, m, first)
        block = ref.at[slot_rows(m, c, chips[first]), :]
        begin(copy(block, block, ag_ss.at[e, m, 2], ag_rs.at[e, m, 2], teams[last][0]))
        gather_hand(ref, e, m, last)

    def gather_far(ref, e, m):
        gather_hand(ref, e, m, 2)

    def gather_end(ref, e, m):
        for r in range(4):
            place = chip if r == 3 else chips[r]
            which = 3 if r == 3 else 4 + r
            block = ref.at[slot_rows(m, 1 - c, place), :]
            copy(block, block, ag_ss.at[e, m, which], ag_rs.at[e, m, which], sibling).wait_recv()

    for m in range(2):
        unit, _ = unit_of(x_ref[m].astype(F32))
        n1[row_rows(m, c, y), :] = (unit * vector(0) + vector(1)).astype(BF)
        row_start(n1, 0, m)
    for m in range(2):
        db[slot_rows(m, c, chip), :] = (g_ref[m].astype(F32) * vector(5)).astype(BF)
    gather_start(db, 0, 0)

    def make_trig(index, carry):
        m, slot = index // 4, index % 4
        cc, yy = slot // 2, slot % 2
        row = vec_all[z, xi * 4 + yy * 2 + cc, pl.ds(6 + m, 1), :]
        places = jnp.transpose(jnp.broadcast_to(row, (128, 128)))
        rows = span(index * 128, 128)
        pos[rows, :] = places
        hits = lax.broadcasted_iota(jnp.int32, (128, PLACES), 1).astype(F32) == jnp.concatenate(
            [places, places], axis=1
        )
        both = dot(hits.astype(F32).astype(BF), table_ref[...])
        trig[rows, :] = both[:, :128] + both[:, 128:]
        return carry

    lax.fori_loop(0, 8, make_trig, 0)
    weights_out(0)

    def expand(rows, count):
        both = trig[rows, :]
        front = lax.broadcasted_iota(jnp.int32, (count, 128), 1) % 64 < 32
        cosine = jnp.where(front, both, pltpu.roll(both, 32, 1))
        sine = jnp.where(front, -pltpu.roll(both, 96, 1), both)
        return front, cosine, sine

    def swap(values, front):
        return jnp.where(front, pltpu.roll(values, 96, 1), pltpu.roll(values, 32, 1))

    slab_pass(0)
    slab_up(1)
    row_pass(n1, 0, 0)
    row_pass(n1, 0, 1)
    gather_pass(db, 0, 0, 1)
    weights_out(1)
    weights_up(0)
    slab_in(0)

    first_head = lax.broadcasted_iota(jnp.int32, (128, 128), 1) < 64

    def split_heads(values):
        zero = jnp.zeros_like(values)
        return jnp.concatenate(
            [jnp.where(first_head, values, zero), jnp.where(first_head, zero, values)], axis=0
        )

    def join_heads(values):
        return jnp.where(first_head, values[:128], values[128:])

    def project(m):
        def step(i, carry):
            rows = span(m * 512 + i * 256, 256)
            raw = dot(n1[rows, :], w0[:, 0:768])
            front, cosine, sine = expand(rows, 256)
            for b in range(4):
                part = raw[:, 128 * b : 128 * b + 128]
                qkv[rows, 128 * b : 128 * b + 128] = (
                    part * cosine + swap(part, front) * sine
                ).astype(BF)
            qkv[rows, 512:768] = raw[:, 512:768].astype(BF)
            return carry

        lax.fori_loop(0, 2, step, 0)

    def block_rows(m, s):
        return span(m * 512 + (s % 2) * 256 + (s // 2) * 128, 128)

    def pair(b, p):
        return slice(256 * b + 128 * p, 256 * b + 128 * p + 128)

    def attend(m):
        def step(s, carry):
            rows = block_rows(m, s)
            before = block_rows(m, jnp.maximum(s - 1, 0))
            r = lax.broadcasted_iota(jnp.int32, (128, 256), 0)
            k = lax.broadcasted_iota(jnp.int32, (128, 256), 1)
            back = r + 128 - k
            places = pos[rows, :]
            limit = jnp.minimum(jnp.concatenate([places, places], axis=1).astype(jnp.int32), 127)
            limit = jnp.minimum(limit, s * 128 + r)
            allowed = (back >= 0) & (back <= limit)
            allowed = jnp.concatenate([allowed, allowed], axis=0)
            for p in range(2):
                query = split_heads(qkv[rows, pair(0, p)])
                keys = jnp.concatenate([qkv[before, pair(1, p)], qkv[rows, pair(1, p)]], axis=0)
                held = jnp.concatenate([qkv[before, pair(2, p)], qkv[rows, pair(2, p)]], axis=0)
                scores = dot_rows(query, keys) * (HD ** -0.5)
                scores = jnp.where(allowed, scores, NEGATIVE)
                top = jnp.max(scores, axis=-1, keepdims=True)
                exponent = jnp.exp(scores - top)
                total = jnp.sum(exponent, axis=-1, keepdims=True)
                share = (exponent / total).astype(BF)
                probs[(m * 4 + s) * 2 + p] = share
                att[rows, pair(0, p)] = join_heads(dot(share, held)).astype(BF)
            return carry

        lax.fori_loop(0, 4, step, 0)

    def row_send(e, m):
        return copy(
            send_a0.at[m, span((1 - y) * 128, 128), :], recv_d0.at[m], ra_ss.at[e, m, 1],
            ra_rs.at[e, m, 1], beside,
        )

    def row_scatter(e, m, compute):
        hand = copy(send_b.at[m], recv_c0.at[m], ra_ss.at[e, m, 0], ra_rs.at[e, m, 0], sibling)

        def step(j, carry):
            part = compute(pl.multiple_of(m * 512 + ((c + 1 + j) % 2) * 256, 256))

            @pl.when(j == 0)
            def _():
                send_b[m] = part.astype(BF)
                hand.start()

            @pl.when(j == 1)
            def _():
                hand.wait_recv()
                send_a0[m] = (part + recv_c0[m].astype(F32)).astype(BF)
                row_send(e, m).start()

            return carry

        lax.fori_loop(0, 2, step, 0)
        hand.wait_send()

    def row_scatter_end(e, m):
        row_send(e, m).wait()
        return send_a0[m, span(y * 128, 128), :].astype(F32) + recv_d0[m].astype(F32)

    def scatter(e, m, compute):
        def step(j, carry):
            cc = (c + 1 + j // 2) % 2
            xx = (xi + 1 + j % 2) % 2
            part = compute(pl.multiple_of(m * 1024 + cc * 512 + xx * 256, 256))
            there = span(xx * 256, 256)

            @pl.when(j < 2)
            def _():
                send_b[j] = part.astype(BF)
                copy(
                    send_b.at[j], recv_c.at[e, m, there, :], rs_ss.at[e, m, j], rs_rs.at[e, m, j],
                    sibling,
                ).start()

            @pl.when(j >= 2)
            def _():
                copy(
                    send_b.at[j - 2], recv_c.at[e, m, there, :], rs_ss.at[e, m, j - 2],
                    rs_rs.at[e, m, j - 2], sibling,
                ).wait_recv()
                send_a[m, there, :] = (
                    part + recv_c[e, m, there, :].astype(F32)
                ).astype(BF)

            @pl.when(j == 2)
            def _():
                scatter_send(e, m, 2).start()
                if LEG[e] != 1:
                    scatter_send(e, m, 0).start()

            @pl.when(j == 3)
            def _():
                if LEG[e] != 0:
                    scatter_send(e, m, 1).start()

            return carry

        lax.fori_loop(0, 4, step, 0)
        for j in range(2):
            copy(
                send_b.at[j], recv_c.at[e, m, pl.ds(0, 256), :], rs_ss.at[e, m, j],
                rs_rs.at[e, m, j], sibling,
            ).wait_send()

    def scatter_send(e, m, r):
        rows = span(chips[r] * 128, 128)
        return copy(
            send_a.at[m, rows, :], recv_d.at[e, m, r], rs_ss.at[e, m, 2 + r],
            rs_rs.at[e, m, 2 + r], teams[r if r < 2 or LEG[e] is None else LEG[e]][0],
        )

    def scatter_pass(e, m):
        r = 1 - LEG[e]
        rows = span(chips[r] * 128, 128)
        scatter_send(e, m, 2).wait_recv()
        send_a[m, rows, :] = (
            send_a[m, rows, :].astype(F32) + recv_d[e, m, 2].astype(F32)
        ).astype(BF)
        scatter_send(e, m, r).start()

    def scatter_end(e, m):
        direct = LEG[e] is None
        for r in range(3):
            if r < 2 or direct:
                scatter_send(e, m, r).wait()
            else:
                scatter_send(e, m, r).wait_send()
        total = send_a[m, span(chip * 128, 128), :].astype(F32)
        for r in range(3 if direct else 2):
            total = total + recv_d[e, m, r].astype(F32)
        return total

    def outwards(row):
        return dot(att[pl.ds(row, 256), :], outw[...])

    row_end(n1, 0, 0)
    project(0)
    slab_pass(1)
    attend(0)
    slab_in(1)
    for i, k in enumerate(ROW_TEAM):
        device, g = teams[k]
        begin(
            copy(
                w0.at[span((g % 4) * 256, 256), pl.ds(768, 256)],
                outw.at[:, span(sq * 256, 256)], o_ss.at[i], o_rs.at[i], device,
            )
        )
    outw[:, span(sq * 256, 256)] = w0[span(sq * 256, 256), 768:1024]
    gather_start(db, 0, 1)
    row_end(n1, 0, 1)
    project(1)
    for i, k in enumerate(ROW_TEAM):
        device, g = teams[k]
        copy(
            w0.at[span((g % 4) * 256, 256), pl.ds(768, 256)],
            outw.at[:, span((g % 4) * 256, 256)], o_ss.at[i], o_rs.at[i], device,
        ).wait_recv()
    row_scatter(0, 0, outwards)
    weights_up(1)
    attend(1)
    row_scatter(0, 1, outwards)

    def second_norm(m):
        total = row_scatter_end(0, m)
        attn[m] = total
        middle = x_ref[m].astype(F32) + vector(4) * total
        mid[m] = middle
        unit, _ = unit_of(middle)
        n2[slot_rows(m, c, chip), :] = (unit * vector(2) + vector(3)).astype(BF)

    gather_far(db, 0, 0)
    second_norm(0)
    gather_start(n2, 1, 0)
    gather_pass(db, 0, 1, 0)
    weights_pass(0)
    second_norm(1)
    gather_start(n2, 1, 1)
    gather_pass(n2, 1, 0, 0)
    gather_far(db, 0, 1)
    gather_far(n2, 1, 0)
    gather_pass(n2, 1, 1, 1)
    weights_pass(1)

    def mlp(row):
        rows = pl.ds(row, 256)
        both = dot(n2[rows, :], w1[...])
        d_hidden = dot(db[rows, :], w2[...])
        gate, up = both[:, :512], both[:, 512:]
        sig = sigmoid(gate)
        silu = gate * sig
        hid[rows, :] = (silu * up).astype(BF)
        dgu[rows, 0:512] = (d_hidden * up * sig * (1.0 + gate * (1.0 - sig))).astype(BF)
        dgu[rows, 512:1024] = (d_hidden * silu).astype(BF)
        return dot_rows(dgu[rows, :], w1[...])

    weights_in(0)
    weights_in(1)
    gather_end(db, 0, 0)
    gather_end(n2, 1, 0)
    scatter(0, 0, mlp)
    gather_far(n2, 1, 1)
    gather_end(db, 0, 1)
    gather_end(n2, 1, 1)
    scatter(0, 1, mlp)

    turned = (z == 0) | (z == 2)
    at_end = (z == 0) | (z == 3)

    def target(i):
        inner = jnp.where(i == 3, 1, jnp.where(i == 0, 0, i + 1))
        plain = jnp.where(at_end, i, inner)
        return jnp.where(turned, 3 - plain, plain)

    def descend(n, i, stage, arrive, relay):
        zz = target(i)

        @pl.when(at_end & (i == 0))
        def _():
            via = jnp.where(z == 0, 1, 2)
            copy(stage.at[i], relay, z_ss.at[n, i], z_rs.at[n, 3], (via * 2 + xi, sq)).start()

        @pl.when(jnp.logical_not(at_end & (i == 0)) & (at_end | (i < 2)))
        def _():
            slot = (zz + 3 - z) % 4
            copy(
                stage.at[i], arrive.at[slot], z_ss.at[n, i], z_rs.at[n, slot], (zz * 2 + xi, sq)
            ).start()

    def descend_pass(n, stage, arrive, relay):
        @pl.when(passes)
        def _():
            zz = target(2)
            slot = (zz + 3 - z) % 4
            copy(stage.at[2], relay, z_ss.at[n, 2], z_rs.at[n, 3], levels[0][0]).wait_recv()
            stage[2] = (stage[2].astype(F32) + relay[...].astype(F32)).astype(BF)
            copy(
                stage.at[2], arrive.at[slot], z_ss.at[n, 2], z_rs.at[n, slot], (zz * 2 + xi, sq)
            ).start()

    def weight_grad(n, left, right, stage, own, arrive, relay):
        def step(i, carry):
            part = dot_cols(left[:, span(target(i) * 256, 256)], right[...])

            @pl.when(i < 3)
            def _():
                stage[i] = part.astype(BF)
                descend(n, i, stage, arrive, relay)

            @pl.when(i == 3)
            def _():
                own[...] = part.astype(own.dtype)

            return carry

        lax.fori_loop(0, 4, step, 0)

    weight_grad(0, n2, dgu, stage_g, own_g, zg_ref, relay_g)

    def norm_back(grad, values, gain, row):
        unit, inverse = unit_of(values)
        gacc[row : row + 1, :] += jnp.sum(grad * unit, axis=0, keepdims=True)
        gacc[row + 1 : row + 2, :] += jnp.sum(grad, axis=0, keepdims=True)
        scaled = grad * gain
        return inverse * (
            scaled
            - jnp.mean(scaled, axis=-1, keepdims=True)
            - unit * jnp.mean(scaled * unit, axis=-1, keepdims=True)
        )

    def second_norm_back(m):
        grad = scatter_end(0, m)
        d_mid = g_ref[m].astype(F32) + norm_back(grad, mid[m], vector(2), 2)
        gacc[4:5, :] += jnp.sum(d_mid * attn[m], axis=0, keepdims=True)
        attn[m] = d_mid
        da[row_rows(m, c, y), :] = (vector(4) * d_mid).astype(BF)
        row_start(da, 1, m)

    second_norm_back(0)
    weight_grad(1, db, hid, stage_d, own_d, zd_ref, relay_d)

    def downwards(row):
        return dot_rows(hid[pl.ds(row, 256), :], w2[...])

    def attend_back(m):
        def step(s, carry):
            rows = block_rows(m, s)
            before = block_rows(m, jnp.maximum(s - 1, 0))
            d_att = dot_rows(da[rows, :], outw[...]).astype(BF)
            here = span(s * 128, 128)
            prior = span(jnp.maximum(s - 1, 0) * 128, 128)
            for p in range(2):
                d_heads = split_heads(d_att[:, 128 * p : 128 * p + 128])
                query = split_heads(qkv[rows, pair(0, p)])
                keys = jnp.concatenate([qkv[before, pair(1, p)], qkv[rows, pair(1, p)]], axis=0)
                held = jnp.concatenate([qkv[before, pair(2, p)], qkv[rows, pair(2, p)]], axis=0)
                share = probs[(m * 4 + s) * 2 + p]
                weights = share.astype(F32)
                d_probs = dot_rows(d_heads, held)
                inner = jnp.sum(weights * d_probs, axis=-1, keepdims=True)
                d_scores = (weights * (d_probs - inner) * (HD ** -0.5)).astype(BF)
                dqs[here, pair(0, p)] = join_heads(dot(d_scores, keys))
                d_keys = dot_cols(d_scores, query)
                d_held = dot_cols(share, d_heads)
                dkv[prior, pair(0, p)] += d_keys[:128]
                dkv[prior, pair(1, p)] += d_held[:128]
                dkv[here, pair(0, p)] = d_keys[128:]
                dkv[here, pair(1, p)] = d_held[128:]
            return carry

        lax.fori_loop(0, 4, step, 0)

        def finish(s, carry):
            rows = block_rows(m, s)
            here = span(s * 128, 128)
            front, cosine, sine = expand(rows, 128)
            for b in range(4):
                part = dqs[here, 128 * b : 128 * b + 128] if b < 2 else dkv[here, pair(0, b - 2)]
                qkv[rows, 128 * b : 128 * b + 128] = (
                    part * cosine - swap(part, front) * sine
                ).astype(BF)
            qkv[rows, 512:768] = dkv[here, 256:512].astype(BF)
            return carry

        lax.fori_loop(0, 4, finish, 0)

    def inwards(row):
        return dot_rows(qkv[pl.ds(row, 256), :], w0[:, 0:768])

    dkv[...] = jnp.zeros_like(dkv)
    scatter(1, 0, downwards)
    row_pass(da, 1, 0)
    second_norm_back(1)
    row_end(da, 1, 0)
    attend_back(0)
    row_scatter(1, 0, inwards)
    scatter_pass(1, 0)
    scatter(1, 1, downwards)
    row_pass(da, 1, 1)
    row_end(da, 1, 1)
    part = dot_cols(att[...], da[...])
    for u in range(4):
        gsend[u] = part[:, 256 * u : 256 * u + 256].astype(BF)
    gout[span(sq * 256, 256), :] = gsend[sq]
    for i, k in enumerate(ROW_TEAM):
        device, g = teams[k]
        begin(
            copy(gsend.at[g % 4], gout.at[span(sq * 256, 256), :], go_ss.at[i], go_rs.at[i], device)
        )

    attend_back(1)
    row_scatter(1, 1, inwards)
    def mine_of(values):
        return jnp.where(xi == 0, values[:128], values[128:])

    def other_of(values):
        return jnp.where(xi == 0, values[128:], values[:128])

    for i, k in enumerate(ROW_TEAM):
        device, g = teams[k]
        theirs = span((g % 4) * 256, 256)
        copy(gsend.at[g % 4], gout.at[theirs, :], go_ss.at[i], go_rs.at[i], device).wait_recv()
    for j in range(4):
        zz = target(j)
        begin(
            copy(
                gout.at[span((zz * 2 + 1 - xi) * 128, 128), :], side_o.at[j], sx_ss.at[1, j],
                sx_rs.at[1, j], across,
            )
        )

    def qkv_grad(j, carry):
        part = dot_cols(n1[:, span(target(j) * 256, 256)], qkv[...])
        send_q[j] = other_of(part).astype(BF)
        copy(send_q.at[j], side_q.at[j], sx_ss.at[0, j], sx_rs.at[0, j], across).start()
        keep_q[j] = mine_of(part).astype(BF)
        return carry

    lax.fori_loop(0, 4, qkv_grad, 0)


    def summed(n, i, mine, side, stage, own, arrive, relay):
        copy(side.at[i], side.at[i], sx_ss.at[n, i], sx_rs.at[n, i], across).wait_recv()
        total = mine + side[i].astype(F32)
        if i < 3:
            stage[i] = total.astype(BF)
            descend(2 + n, i, stage, arrive, relay)
        else:
            own[...] = total

    def sum_q(i):
        summed(0, i, keep_q[i].astype(F32), side_q, stage_q, own_q, zq_ref, relay_q)

    def sum_o(i):
        part = gout[span((target(i) * 2 + xi) * 128, 128), :].astype(F32)
        summed(1, i, part, side_o, stage_o, own_o, zo_ref, relay_o)

    def summed_levels(n, stage, own, arrive):
        for i in range(3):
            copy(stage.at[i], arrive.at[i], z_ss.at[n, i], z_rs.at[n, i], levels[0][0]).wait_send()
        loads = [pltpu.make_async_copy(arrive.at[j], stage.at[j], loc_sem.at[j]) for j in range(3)]
        absent = [z == 0, None, z == 3]
        for j in range(3):
            def load(j=j):
                copy(
                    stage.at[j], arrive.at[j], z_ss.at[n, j], z_rs.at[n, j], levels[0][0]
                ).wait_recv()
                loads[j].start()

            def clear(j=j):
                stage[j] = jnp.zeros(stage.shape[1:], BF)

            if absent[j] is None:
                load()
            else:
                pl.when(jnp.logical_not(absent[j]))(load)
                pl.when(absent[j])(clear)
        for j in range(3):
            if absent[j] is None:
                loads[j].wait()
            else:
                pl.when(jnp.logical_not(absent[j]))(loads[j].wait)
        total = own[...].astype(F32)
        for j in range(3):
            total = total + stage[j].astype(F32)
        return total.astype(BF)

    def last_copies(n, pack, first, width, fin, people, who):
        found = []
        for i, k in enumerate(people):
            device, g = teams[k]
            found.append(
                copy(
                    pack.at[span((g % who) * 32, 32), pl.ds(first, width)],
                    fin.at[me % who, :, pl.ds(first, width)], f_ss.at[n, i], f_rs.at[n, i], device,
                )
            )
        return found

    def finals(n, first, width, stage, own, arrive, pack, fin, people, who):
        pack[:, first : first + width] = summed_levels(n, stage, own, arrive)
        stay = pltpu.make_async_copy(
            pack.at[span((me % who) * 32, 32), pl.ds(first, width)],
            fin.at[me % who, :, pl.ds(first, width)], loc_sem.at[3],
        )
        stay.start()
        for item in last_copies(n, pack, first, width, fin, people, who):
            item.start()
        stay.wait()

    plans = [
        (0, 0, 1024, stage_g, own_g, zg_ref, pack_m, fin_m, range(7), 8),
        (1, 1024, 512, stage_d, own_d, zd_ref, pack_m, fin_m, range(7), 8),
        (3, 768, 256, stage_o, own_o, zo_ref, pack_a, fin_a, ROW_TEAM, 4),
        (2, 0, 768, stage_q, own_q, zq_ref, pack_a, fin_a, ROW_TEAM, 4),
    ]
    def first_norm_back(m):
        grad = row_scatter_end(1, m)
        back = norm_back(grad, x_ref[m].astype(F32), vector(0), 0)
        dx_ref[m] = (attn[m] + back).astype(BF)

    def result(m):
        branch = scatter_end(1, m)
        gacc[5:6, :] += jnp.sum(g_ref[m].astype(F32) * branch, axis=0, keepdims=True)
        y_ref[m] = (mid[m] + vector(5) * branch).astype(BF)

    descend_pass(0, stage_g, zg_ref, relay_g)
    for i in range(4):
        sum_o(i)
    sum_q(0)
    scatter_pass(1, 1)
    sum_q(1)
    descend_pass(1, stage_d, zd_ref, relay_d)
    first_norm_back(0)
    sum_q(2)
    descend_pass(3, stage_o, zo_ref, relay_o)
    first_norm_back(1)
    sum_q(3)
    result(0)
    result(1)
    for k in range(8):
        gv_send[k] = gacc[:, 128 * k : 128 * k + 128]
    for k, (device, g) in enumerate(teams):
        begin(copy(gv_send.at[g], gv_in.at[k], gv_ss.at[k], gv_rs.at[k], device))

    descend_pass(2, stage_q, zq_ref, relay_q)
    for item in pack_sends:
        item.wait_send()
    finals(*plans[0])
    for item in pending:
        if isinstance(item, tuple):
            pl.when(jnp.logical_not(item[0]))(item[1].wait_send)
        else:
            item.wait_send()
    for j in range(4):
        copy(send_q.at[j], side_q.at[j], sx_ss.at[0, j], sx_rs.at[0, j], across).wait_send()
    for k, (device, g) in enumerate(teams):
        copy(gv_send.at[g], gv_in.at[k], gv_ss.at[k], gv_rs.at[k], device).wait_recv()
    total = gv_send[me]
    for k in range(7):
        total = total + gv_in[k]
    gv_z[0] = total
    level_sends = []
    for j, (device, _) in enumerate(levels):
        item = copy(gv_z.at[0], gv_z.at[1 + j], gv_ss.at[7 + j], gv_rs.at[7 + j], device)
        item.start()
        level_sends.append(item)
    finals(*plans[1])
    for item in level_sends:
        item.wait()
    gv_all[me] = gv_z[0] + gv_z[1] + gv_z[2] + gv_z[3]
    for k, (device, g) in enumerate(teams):
        copy(gv_all.at[me], gv_all.at[me], gv_ss.at[10 + k], gv_rs.at[10 + k], device).start()
    finals(*plans[2])
    finals(*plans[3])
    for k, (device, g) in enumerate(teams):
        copy(gv_all.at[g], gv_all.at[g], gv_ss.at[10 + k], gv_rs.at[10 + k], device).wait()
    vg_ref[...] = gv_all[z * 2 + me // 4]
    for n, first, width, _, _, _, pack, fin, people, who in plans:
        for item in last_copies(n, pack, first, width, fin, people, who):
            item.wait()


def layer_fast(
    block_input,
    positions,
    out_grad,
    qkv_weight,
    out_weight,
    gate_weight,
    up_weight,
    down_weight,
    norm1_gain,
    norm1_shift,
    norm2_gain,
    norm2_shift,
    attn_scale,
    mlp_scale,
):
    vectors = jnp.stack(
        [norm1_gain, norm1_shift, norm2_gain, norm2_shift, attn_scale, mlp_scale]
    ).astype(F32)
    packed = jnp.concatenate([jnp.tile(vectors, (1, 4)), positions.astype(F32)], axis=0)
    vmem, anywhere = pl.BlockSpec(memory_space=pltpu.VMEM), pl.BlockSpec(memory_space=pl.ANY)
    dma = pltpu.SemaphoreType.DMA
    scratch = [
        pltpu.VMEM((4, 8, 8, 128), F32), pltpu.VMEM((8, 1024), F32), pltpu.VMEM((8, 1024), F32),
        pltpu.VMEM((7, 8, 128), F32), pltpu.VMEM((4, 8, 128), F32), pltpu.VMEM((8, 8, 128), F32),
        pltpu.VMEM((8, 8, 128), F32),
        pltpu.VMEM((128, 1024), BF), pltpu.VMEM((256, 1536), BF), pltpu.VMEM((1024, 1024), BF),
        pltpu.VMEM((1024, 1024), BF), pltpu.VMEM((1024, 512), BF), pltpu.VMEM((256, 1024), BF),
        pltpu.VMEM((1024, 1024), BF), pltpu.VMEM((2048, 1024), BF), pltpu.VMEM((2048, 1024), BF),
        pltpu.VMEM((1024, 1024), BF),
        pltpu.VMEM((1024, 768), BF), pltpu.VMEM((1024, 256), BF), pltpu.VMEM((16, 256, 256), BF),
        pltpu.VMEM((512, 256), F32), pltpu.VMEM((512, 512), F32),
        pltpu.VMEM((2048, 512), BF), pltpu.VMEM((2048, 1024), BF),
        pltpu.VMEM((2, 512, 1024), BF), pltpu.VMEM((2, 2, 512, 1024), BF),
        pltpu.VMEM((2, 2, 3, 128, 1024), BF), pltpu.VMEM((2, 256, 1024), BF),
        pltpu.VMEM((2, 256, 1024), BF), pltpu.VMEM((2, 256, 1024), BF),
        pltpu.VMEM((2, 128, 1024), BF),
        pltpu.VMEM((3, 128, 768), BF), pltpu.VMEM((3, 128, 256), BF),
        pltpu.VMEM((3, 256, 1024), BF), pltpu.VMEM((3, 256, 512), BF),
        pltpu.VMEM((128, 768), F32), pltpu.VMEM((128, 256), F32),
        pltpu.VMEM((256, 1024), BF), pltpu.VMEM((256, 512), BF),
        pltpu.VMEM((1024, 256), BF), pltpu.VMEM((4, 256, 256), BF),
        pltpu.VMEM((4, 128, 768), BF), pltpu.VMEM((4, 128, 256), BF),
        pltpu.VMEM((4, 128, 768), BF), pltpu.VMEM((4, 128, 768), BF),
        pltpu.VMEM((256, 1024), BF), pltpu.VMEM((256, 512), BF), pltpu.VMEM((128, 768), BF),
        pltpu.VMEM((128, 256), BF),
        pltpu.VMEM((2, 128, 1024), F32), pltpu.VMEM((2, 128, 1024), F32),
        pltpu.VMEM((1024, 128), F32), pltpu.VMEM((1024, 128), F32),
        dma((10,)), dma((10,)), dma((3,)), dma((3,)), dma((2, 8)), dma((2, 8)), dma((2, 11)), dma((2, 11)),
        dma((3,)), dma((3,)), dma((2, 2, 3)), dma((2, 2, 3)), dma((2, 2, 7)), dma((2, 2, 7)),
        dma((2, 2, 2)), dma((2, 2, 2)), dma((2, 2, 5)), dma((2, 2, 5)), dma((3,)), dma((3,)),
        dma((2, 4)), dma((2, 4)), dma((4, 4)), dma((4, 4)), dma((4, 7)), dma((4, 7)),
        dma((17,)), dma((17,)), dma((4,)),
    ]
    y, dx, vg, fin_a, fin_m = pl.pallas_call(
        layer_kernel,
        out_shape=(
            jax.ShapeDtypeStruct((2, 128, 1024), BF),
            jax.ShapeDtypeStruct((2, 128, 1024), BF),
            jax.ShapeDtypeStruct((8, 128), F32),
            jax.ShapeDtypeStruct((4, 32, 1024), BF),
            jax.ShapeDtypeStruct((8, 32, 1536), BF),
            jax.ShapeDtypeStruct((3, 128, 768), BF),
            jax.ShapeDtypeStruct((3, 128, 256), BF),
            jax.ShapeDtypeStruct((3, 256, 1024), BF),
            jax.ShapeDtypeStruct((3, 256, 512), BF),
        ),
        in_specs=[vmem] * 9,
        out_specs=(vmem, vmem, vmem) + (anywhere,) * 6,
        scratch_shapes=scratch,
        compiler_params=pltpu.CompilerParams(
            collective_id=0, has_side_effects=True, vmem_limit_bytes=VMEM_BYTES
        ),
        cost_estimate=pl.CostEstimate(
            flops=26_000_000_000, bytes_accessed=8_000_000, transcendentals=4_000_000
        ),
        name="layer",
    )(
        block_input, out_grad, packed, jnp.asarray(trig_table()), qkv_weight, out_weight,
        gate_weight, up_weight, down_weight.T,
    )[:5]
    fin_a, fin_m = fin_a.astype(F32), fin_m.astype(F32)
    grad_qkv = (
        fin_a[:, :, 0:768].reshape(4, 32, 3, 256).transpose(1, 2, 0, 3).reshape(32, 3072)
    )
    grad_out = fin_a[:, :, 768:1024].transpose(1, 0, 2).reshape(32, 1024)
    grad_gate = fin_m[:, :, 0:512].transpose(1, 0, 2).reshape(32, 4096)
    grad_up = fin_m[:, :, 512:1024].transpose(1, 0, 2).reshape(32, 4096)
    grad_down = fin_m[:, :, 1024:1536].transpose(0, 2, 1).reshape(4096, 32)
    part = lax.axis_index(("dp", "seq")) % 4
    vg = lax.dynamic_index_in_dim(vg.reshape(8, 4, 32), part, 1, keepdims=False)
    return (y, dx, grad_qkv, grad_out, grad_gate, grad_up, grad_down) + tuple(
        vg[i] for i in range(6)
    )


def fits(mesh):
    return mesh.shape["dp"] == 8 and mesh.shape["seq"] == 4


def solution(mesh):
    return jax.shard_map(
        layer_fast if fits(mesh) else body,
        mesh=mesh,
        in_specs=(
            P(None, ("dp", "seq"), None),
            P(None, ("dp", "seq")),
            P(None, ("dp", "seq"), None),
            P(("dp", "seq"), None),
            P(("dp", "seq"), None),
            P(("dp", "seq"), None),
            P(("dp", "seq"), None),
            P(None, ("dp", "seq")),
            P(("dp", "seq")),
            P(("dp", "seq")),
            P(("dp", "seq")),
            P(("dp", "seq")),
            P(("dp", "seq")),
            P(("dp", "seq")),
        ),
        out_specs=(
            P(None, ("dp", "seq"), None),
            P(None, ("dp", "seq"), None),
            P(("dp", "seq"), None),
            P(("dp", "seq"), None),
            P(("dp", "seq"), None),
            P(("dp", "seq"), None),
            P(None, ("dp", "seq")),
            P(("dp", "seq")),
            P(("dp", "seq")),
            P(("dp", "seq")),
            P(("dp", "seq")),
            P(("dp", "seq")),
            P(("dp", "seq")),
        ),
        check_vma=False,
    )
```

```python
import jax
import jax.numpy as jnp
import ml_dtypes
import numpy as np
from jax import lax
from jax.experimental import pallas as pl
from jax.experimental.pallas import tpu as pltpu
from jax.sharding import PartitionSpec as P

H = 16
HD = 64
WINDOW = 128


EPSILON = 1e-05
NEGATIVE = -1e30


def normalize(values, gain, shift):
    center = values - jnp.mean(values, axis=-1, keepdims=True)
    inverse = lax.rsqrt(jnp.mean(center * center, axis=-1, keepdims=True) + EPSILON)
    unit = center * inverse
    return (unit * gain + shift, unit, inverse)


def normalize_back(incoming, unit, inverse, gain):
    scaled = incoming * gain
    middle = (
        scaled
        - jnp.mean(scaled, axis=-1, keepdims=True)
        - unit * jnp.mean(scaled * unit, axis=-1, keepdims=True)
    )
    return (inverse * middle, jnp.sum(incoming * unit, axis=0), jnp.sum(incoming, axis=0))


def angles_of(places, size):
    inverse = 10000.0 ** (-(jnp.arange(size // 2, dtype=jnp.float32) * (2.0 / size)))
    return places.astype(jnp.float32)[:, None] * inverse[None, :]


def rotate(values, angles):
    half = values.shape[-1] // 2
    cosine = jnp.cos(angles)[:, None, :]
    sine = jnp.sin(angles)[:, None, :]
    first_half = values[..., :half]
    second_half = values[..., half:]
    return jnp.concatenate(
        [first_half * cosine - second_half * sine, second_half * cosine + first_half * sine],
        axis=-1,
    )


def unrotate(values, angles):
    half = values.shape[-1] // 2
    cosine = jnp.cos(angles)[:, None, :]
    sine = jnp.sin(angles)[:, None, :]
    first_half = values[..., :half]
    second_half = values[..., half:]
    return jnp.concatenate(
        [first_half * cosine + second_half * sine, second_half * cosine - first_half * sine],
        axis=-1,
    )


def pack_shards(shards):
    return jnp.concatenate([item.reshape(1, -1) for item in shards], axis=1)


def unpack_gathered(whole, shards):
    devices = whole.shape[0]
    result = []
    offset = 0
    for number, item in enumerate(shards):
        count = item.size
        piece = whole[:, offset : offset + count]
        offset = offset + count
        if number == 4:
            rows, cols = item.shape
            result.append(
                piece.reshape(devices, rows, cols).transpose(1, 0, 2).reshape(rows, devices * cols)
            )
        elif item.ndim == 2:
            result.append(piece.reshape(devices * item.shape[0], item.shape[1]))
        else:
            result.append(piece.reshape(-1))
    return tuple(result)


def pack_grads(totals, devices):
    pieces = []
    for number, item in enumerate(totals):
        if number == 4:
            rows, cols = item.shape
            pieces.append(
                item.reshape(rows, devices, cols // devices).transpose(1, 0, 2).reshape(devices, -1)
            )
        else:
            pieces.append(item.reshape(devices, -1))
    return jnp.concatenate(pieces, axis=1)


def unpack_summed(summed, shards):
    flat = summed.reshape(-1)
    result = []
    offset = 0
    for item in shards:
        count = item.size
        result.append(flat[offset : offset + count].reshape(item.shape))
        offset = offset + count
    return tuple(result)


def block_scores(query, keys_padded, values_padded, starts, first, size):
    block_query = lax.dynamic_slice_in_dim(query, first, size, 0)
    block_keys = lax.dynamic_slice_in_dim(keys_padded, first, size + WINDOW, 0)
    block_values = lax.dynamic_slice_in_dim(values_padded, first, size + WINDOW, 0)
    begin = lax.dynamic_slice_in_dim(starts, first, size, 0)
    here = first + jnp.arange(size, dtype=jnp.int32)
    there = first - WINDOW + jnp.arange(size + WINDOW, dtype=jnp.int32)
    allowed = (
        (there[None, :] >= begin[:, None])
        & (there[None, :] <= here[:, None])
        & (here[:, None] - there[None, :] < WINDOW)
    )
    raw = jnp.einsum("qhd,khd->hqk", block_query, block_keys, preferred_element_type=jnp.float32)
    scores = jnp.where(allowed[None], raw * HD ** (-0.5), NEGATIVE)
    return (scores, block_query, block_keys, block_values)


def attend_forward(query, keys_padded, values_padded, starts):
    length = query.shape[0]
    size = min(512, length)
    count = length // size

    def step(carry, index):
        scores, block_query, block_keys, block_values = block_scores(
            query, keys_padded, values_padded, starts, index * size, size
        )
        top = jnp.max(scores, axis=-1, keepdims=True)
        exponent = jnp.exp(scores - top)
        total = jnp.sum(exponent, axis=-1, keepdims=True)
        probs = (exponent / total).astype(jnp.bfloat16)
        outcome = jnp.einsum(
            "hqk,khd->qhd", probs, block_values, preferred_element_type=jnp.float32
        )
        return (carry, (outcome, (top + jnp.log(total))[..., 0]))

    unused, (outcomes, logs) = lax.scan(step, 0, jnp.arange(count, dtype=jnp.int32))
    return (outcomes.reshape(query.shape), logs)


def attend_backward(query, keys_padded, values_padded, starts, logs, grad_out):
    length = query.shape[0]
    size = min(512, length)
    count = length // size

    def step(carry, index):
        grad_query, grad_keys, grad_values = carry
        first = index * size
        scores, block_query, block_keys, block_values = block_scores(
            query, keys_padded, values_padded, starts, first, size
        )
        probs = jnp.exp(scores - logs[index][..., None])
        grad_block = lax.dynamic_slice_in_dim(grad_out, first, size, 0)
        grad_probs = jnp.einsum(
            "qhd,khd->hqk", grad_block, block_values, preferred_element_type=jnp.float32
        )
        inner = jnp.sum(probs * grad_probs, axis=-1, keepdims=True)
        grad_scores = (probs * (grad_probs - inner) * HD ** (-0.5)).astype(jnp.bfloat16)
        query_part = jnp.einsum(
            "hqk,khd->qhd", grad_scores, block_keys, preferred_element_type=jnp.float32
        )
        keys_part = jnp.einsum(
            "hqk,qhd->khd", grad_scores, block_query, preferred_element_type=jnp.float32
        )
        values_part = jnp.einsum(
            "hqk,qhd->khd",
            probs.astype(jnp.bfloat16),
            grad_block,
            preferred_element_type=jnp.float32,
        )
        grad_query = lax.dynamic_update_slice_in_dim(grad_query, query_part, first, 0)
        grad_keys = lax.dynamic_update_slice_in_dim(
            grad_keys,
            lax.dynamic_slice_in_dim(grad_keys, first, size + WINDOW, 0) + keys_part,
            first,
            0,
        )
        grad_values = lax.dynamic_update_slice_in_dim(
            grad_values,
            lax.dynamic_slice_in_dim(grad_values, first, size + WINDOW, 0) + values_part,
            first,
            0,
        )
        return ((grad_query, grad_keys, grad_values), None)

    start_state = (
        jnp.zeros(query.shape, jnp.float32),
        jnp.zeros(keys_padded.shape, jnp.float32),
        jnp.zeros(values_padded.shape, jnp.float32),
    )
    (grad_query, grad_keys, grad_values), unused = lax.scan(
        step, start_state, jnp.arange(count, dtype=jnp.int32)
    )
    return (grad_query, grad_keys, grad_values)


def attention_forward(query, keyset, valueset, places):
    rows, heads, depth = query.shape
    width = heads * depth
    parts = lax.axis_size("seq")
    slab = width // parts
    local = slab // depth
    packed = jnp.stack(
        [query.reshape(rows, width), keyset.reshape(rows, width), valueset], axis=1
    ).reshape(rows, 3, parts, slab)
    moved = lax.all_to_all(packed, "seq", split_axis=2, concat_axis=0, tiled=True)
    group = moved.shape[0]
    every = lax.all_gather(places, "seq", axis=0, tiled=True)
    starts = jnp.maximum(jnp.arange(group, dtype=jnp.int32) - every, 0)
    padding = jnp.zeros((WINDOW, local, depth), jnp.bfloat16)
    head_query = moved[:, 0, 0].reshape(group, local, depth)
    keys_padded = jnp.concatenate([padding, moved[:, 1, 0].reshape(group, local, depth)], axis=0)
    values_padded = jnp.concatenate([padding, moved[:, 2, 0].reshape(group, local, depth)], axis=0)
    outcome, logs = attend_forward(head_query, keys_padded, values_padded, starts)
    sent = outcome.astype(jnp.bfloat16).reshape(group, 1, slab)
    attended = lax.all_to_all(sent, "seq", split_axis=0, concat_axis=1, tiled=True).reshape(
        rows, width
    )
    return (attended, (head_query, keys_padded, values_padded, starts, logs))


def attention_backward(kept, grad_attended, rows, width):
    head_query, keys_padded, values_padded, starts, logs = kept
    depth = head_query.shape[-1]
    parts = lax.axis_size("seq")
    slab = width // parts
    local = slab // depth
    came = lax.all_to_all(
        grad_attended.reshape(rows, parts, slab), "seq", split_axis=1, concat_axis=0, tiled=True
    )
    group = came.shape[0]
    grad_out = came.reshape(group, local, depth)
    grad_query, grad_keys, grad_values = attend_backward(
        head_query, keys_padded, values_padded, starts, logs, grad_out
    )
    packed = (
        jnp.stack([grad_query, grad_keys[WINDOW:], grad_values[WINDOW:]], axis=1)
        .astype(jnp.bfloat16)
        .reshape(group, 3, 1, slab)
    )
    back = lax.all_to_all(packed, "seq", split_axis=0, concat_axis=2, tiled=True).reshape(
        rows, 3, width
    )
    return (back[:, 0], back[:, 1], back[:, 2])


def forward_micro(weights, block, places):
    (
        qkv_weight,
        out_weight,
        gate_weight,
        up_weight,
        down_weight,
        gain1,
        shift1,
        gain2,
        shift2,
        scale1,
        scale2,
    ) = weights
    rows, width = block.shape
    start_in = block.astype(jnp.float32)
    normed1, unit1, inverse1 = normalize(start_in, gain1, shift1)
    acted1 = normed1.astype(jnp.bfloat16)
    projected = jnp.dot(acted1, qkv_weight, preferred_element_type=jnp.float32)
    angles = angles_of(places, HD)
    query = rotate(projected[:, :width].reshape(rows, H, HD), angles).astype(jnp.bfloat16)
    keyset = rotate(projected[:, width : 2 * width].reshape(rows, H, HD), angles).astype(
        jnp.bfloat16
    )
    valueset = projected[:, 2 * width :].astype(jnp.bfloat16)
    attended, kept = attention_forward(query, keyset, valueset, places)
    attn = jnp.dot(attended, out_weight, preferred_element_type=jnp.float32)
    mid = start_in + scale1 * attn
    normed2, unit2, inverse2 = normalize(mid, gain2, shift2)
    acted2 = normed2.astype(jnp.bfloat16)
    gate = jnp.dot(acted2, gate_weight, preferred_element_type=jnp.float32)
    up_value = jnp.dot(acted2, up_weight, preferred_element_type=jnp.float32)
    hidden = (jax.nn.silu(gate) * up_value).astype(jnp.bfloat16)
    branch = jnp.dot(hidden, down_weight, preferred_element_type=jnp.float32)
    result = (mid + scale2 * branch).astype(jnp.bfloat16)
    saved = (
        acted1,
        unit1,
        inverse1,
        angles,
        kept,
        attended,
        attn,
        unit2,
        inverse2,
        acted2,
        gate,
        up_value,
        hidden,
        branch,
    )
    return (result, saved)


def backward_micro(weights, saved, cotangent):
    (
        qkv_weight,
        out_weight,
        gate_weight,
        up_weight,
        down_weight,
        gain1,
        shift1,
        gain2,
        shift2,
        scale1,
        scale2,
    ) = weights
    (
        acted1,
        unit1,
        inverse1,
        angles,
        kept,
        attended,
        attn,
        unit2,
        inverse2,
        acted2,
        gate,
        up_value,
        hidden,
        branch,
    ) = saved
    rows, width = attended.shape
    flow = cotangent.astype(jnp.float32)
    grad_branch = (scale2 * flow).astype(jnp.bfloat16)
    grad_scale2 = jnp.sum(flow * branch, axis=0)
    grad_down = jnp.einsum("rf,rd->fd", hidden, grad_branch, preferred_element_type=jnp.float32)
    grad_hidden = jnp.einsum(
        "rd,fd->rf", grad_branch, down_weight, preferred_element_type=jnp.float32
    )
    sigmoid_gate = jax.nn.sigmoid(gate)
    grad_gate = (
        grad_hidden * up_value * sigmoid_gate * (1.0 + gate * (1.0 - sigmoid_gate))
    ).astype(jnp.bfloat16)
    grad_up = (grad_hidden * gate * sigmoid_gate).astype(jnp.bfloat16)
    grad_gate_w = jnp.einsum("rd,rf->df", acted2, grad_gate, preferred_element_type=jnp.float32)
    grad_up_w = jnp.einsum("rd,rf->df", acted2, grad_up, preferred_element_type=jnp.float32)
    grad_acted2 = jnp.einsum(
        "rf,df->rd", grad_gate, gate_weight, preferred_element_type=jnp.float32
    ) + jnp.einsum("rf,df->rd", grad_up, up_weight, preferred_element_type=jnp.float32)
    grad_mid, grad_gain2, grad_shift2 = normalize_back(grad_acted2, unit2, inverse2, gain2)
    grad_mid = flow + grad_mid
    grad_scale1 = jnp.sum(grad_mid * attn, axis=0)
    grad_attn = (scale1 * grad_mid).astype(jnp.bfloat16)
    grad_out_w = jnp.einsum("rd,re->de", attended, grad_attn, preferred_element_type=jnp.float32)
    grad_attended = jnp.einsum(
        "re,de->rd", grad_attn, out_weight, preferred_element_type=jnp.float32
    ).astype(jnp.bfloat16)
    grad_query, grad_keys, grad_values = attention_backward(kept, grad_attended, rows, width)
    query_plain = unrotate(grad_query.astype(jnp.float32).reshape(rows, H, HD), angles).reshape(
        rows, width
    )
    keys_plain = unrotate(grad_keys.astype(jnp.float32).reshape(rows, H, HD), angles).reshape(
        rows, width
    )
    grad_projected = jnp.concatenate(
        [query_plain, keys_plain, grad_values.astype(jnp.float32)], axis=1
    ).astype(jnp.bfloat16)
    grad_qkv_w = jnp.einsum("rd,re->de", acted1, grad_projected, preferred_element_type=jnp.float32)
    grad_acted1 = jnp.einsum(
        "re,de->rd", grad_projected, qkv_weight, preferred_element_type=jnp.float32
    )
    grad_first, grad_gain1, grad_shift1 = normalize_back(grad_acted1, unit1, inverse1, gain1)
    grad_input = (grad_mid + grad_first).astype(jnp.bfloat16)
    terms = (
        grad_qkv_w,
        grad_out_w,
        grad_gate_w,
        grad_up_w,
        grad_down,
        grad_gain1,
        grad_shift1,
        grad_gain2,
        grad_shift2,
        grad_scale1,
        grad_scale2,
    )
    return (grad_input, terms)


def body(
    block_input,
    positions,
    out_grad,
    qkv_weight,
    out_weight,
    gate_weight,
    up_weight,
    down_weight,
    norm1_gain,
    norm1_shift,
    norm2_gain,
    norm2_shift,
    attn_scale,
    mlp_scale,
):
    shards = (
        qkv_weight,
        out_weight,
        gate_weight,
        up_weight,
        down_weight,
        norm1_gain,
        norm1_shift,
        norm2_gain,
        norm2_shift,
        attn_scale,
        mlp_scale,
    )
    devices = lax.axis_size(("dp", "seq"))
    outer = lax.axis_size("dp")
    inner = lax.axis_size("seq")
    packed = pack_shards(shards)
    totals = None
    results = []
    grads_in = []
    for index in range(block_input.shape[0]):
        weights = unpack_gathered(lax.all_gather(packed, ("dp", "seq"), axis=0, tiled=True), shards)
        result, saved = forward_micro(weights, block_input[index], positions[index])
        backward_weights = unpack_gathered(
            lax.all_gather(packed, ("dp", "seq"), axis=0, tiled=True), shards
        )
        grad_input, terms = backward_micro(backward_weights, saved, out_grad[index])
        if totals is None:
            totals = terms
        else:
            totals = tuple(
                (first_term + second_term for first_term, second_term in zip(totals, terms))
            )
        results.append(result)
        grads_in.append(grad_input)
    laid = pack_grads(totals, devices)
    laid = laid.reshape(outer, inner, laid.shape[1])
    partial_sum = lax.psum_scatter(laid.astype(jnp.bfloat16), "dp", scatter_dimension=0, tiled=True)
    summed = lax.psum_scatter(partial_sum, "seq", scatter_dimension=1, tiled=True).astype(
        jnp.float32
    )
    return (jnp.stack(results), jnp.stack(grads_in)) + unpack_summed(summed, shards)


VMEM_BYTES = 64 * 1024 * 1024
BF = jnp.bfloat16
F32 = jnp.float32
MESH = pl.DeviceIdType.MESH
TEAM = 8
PLACES = 256
RELATIONS = [(1, 0, 0), (0, 1, 0), (1, 1, 0), (0, 0, 1), (1, 0, 1), (0, 1, 1), (1, 1, 1)]
ROW_TEAM = (1, 3, 5)
LEG = (None, 0)


def trig_table():
    inverse = 10000.0 ** (-(np.arange(HD // 2, dtype=np.float64) * (2.0 / HD)))
    angles = np.arange(PLACES, dtype=np.float64)[:, None] * inverse[None, :]
    values = np.concatenate([np.cos(angles), np.sin(angles)] * 2, axis=1).astype(np.float32)
    high = values.astype(ml_dtypes.bfloat16)
    rest = (values - high.astype(np.float32)).astype(ml_dtypes.bfloat16)
    return np.concatenate([high, rest], axis=1)


def dot(a, b):
    return lax.dot_general(a, b, (((1,), (0,)), ((), ())), preferred_element_type=F32)


def dot_rows(a, b):
    return lax.dot_general(a, b, (((1,), (1,)), ((), ())), preferred_element_type=F32)


def dot_cols(a, b):
    return lax.dot_general(a, b, (((0,), (0,)), ((), ())), preferred_element_type=F32)


def sigmoid(v):
    return 0.5 * jnp.tanh(0.5 * v) + 0.5


def unit_of(values):
    center = values - jnp.mean(values, axis=-1, keepdims=True)
    inverse = lax.rsqrt(jnp.mean(center * center, axis=-1, keepdims=True) + EPSILON)
    return center * inverse, inverse


def layer_kernel(
    x_ref, g_ref, vec_ref, table_ref, qkv_ref, out_ref, gate_ref, up_ref, down_ref,
    y_ref, dx_ref, vg_ref, fin_a, fin_m, zq_ref, zo_ref, zg_ref, zd_ref,
    vec_all, vecs, gacc, gv_in, gv_z, gv_send, gv_all,
    pack_a, pack_m, w0, w1, w2, outw,
    n1, n2, db, da, qkv, att, probs, dqs, dkv, hid, dgu,
    send_a, recv_c, recv_d, send_b, send_a0, recv_c0, recv_d0,
    stage_q, stage_o, stage_g, stage_d, own_q, own_o, own_g, own_d, gout, gsend,
    side_q, side_o, keep_q, send_q, relay_g, relay_d, relay_q, relay_o,
    mid, attn, trig, pos,
    vec_ss, vec_rs, wr_ss, wr_rs, wa_ss, wa_rs, w_ss, w_rs, o_ss, o_rs, ga_ss, ga_rs, ag_ss, ag_rs,
    ra_ss, ra_rs, rs_ss, rs_rs, go_ss, go_rs, sx_ss, sx_rs, z_ss, z_rs, f_ss, f_rs,
    gv_ss, gv_rs, loc_sem,
):
    dp = lax.axis_index("dp")
    sq = lax.axis_index("seq")
    z, xi, y, c = dp // 2, dp % 2, sq // 2, sq % 2
    me = xi * 4 + sq
    chip = xi * 2 + y

    def copy(src, dst, ss, rs, device):
        return pltpu.make_async_remote_copy(
            src_ref=src, dst_ref=dst, send_sem=ss, recv_sem=rs,
            device_id=device, device_id_type=MESH,
        )

    def span(start, size):
        return pl.ds(pl.multiple_of(start, size), size)

    def team(k):
        kx, ky, kc = RELATIONS[k]
        xx, yy, cc = (xi + kx) % 2, (y + ky) % 2, (c + kc) % 2
        return (z * 2 + xx, yy * 2 + cc), xx * 4 + yy * 2 + cc

    def level(j):
        zz = (z + j) % 4
        return (zz * 2 + xi, sq), zz

    teams = [team(k) for k in range(7)]
    levels = [level(j) for j in range(1, 4)]
    sources = [(z + 4 - j) % 4 for j in range(1, 4)]
    across, beside, sibling = teams[0][0], teams[1][0], teams[3][0]
    chips = [(1 - xi) * 2 + y, xi * 2 + (1 - y), (1 - xi) * 2 + (1 - y)]

    pending = []
    pack_sends = []
    barrier = pltpu.get_barrier_semaphore()
    for device, _ in teams + levels:
        pl.semaphore_signal(barrier, inc=1, device_id=device, device_id_type=MESH)

    for t in range(4):
        for b in range(3):
            pack_a[32 * t : 32 * t + 32, 256 * b : 256 * b + 256] = qkv_ref[
                :, 1024 * b + 256 * t : 1024 * b + 256 * t + 256
            ]
        pack_a[32 * t : 32 * t + 32, 768:1024] = out_ref[:, 256 * t : 256 * t + 256]
    lane = lax.broadcasted_iota(jnp.int32, (8, 128), 1)
    sub = lax.broadcasted_iota(jnp.int32, (8, 128), 0)
    vec_all[z, me] = jnp.where((sub >= 6) | (lane // 32 == me % 4), vec_ref[...], 0.0)
    gacc[...] = jnp.zeros_like(gacc)
    pl.semaphore_wait(barrier, 10)

    def begin(item):
        item.start()
        pending.append(item)

    for k, (device, _) in enumerate(teams):
        begin(copy(vec_all.at[z, me], vec_all.at[z, me], vec_ss.at[k], vec_rs.at[k], device))

    my_rows = span((z * 8 + me) * 32, 32)
    w0[my_rows, :] = pack_a[span(sq * 32, 32), :]
    for i, k in enumerate(ROW_TEAM):
        device, g = teams[k]
        begin(
            copy(pack_a.at[span((g % 4) * 32, 32), :], w0.at[my_rows, :], wr_ss.at[i], wr_rs.at[i],
                 device)
        )
    for t in range(TEAM):
        pack_m[32 * t : 32 * t + 32, 0:512] = gate_ref[:, 512 * t : 512 * t + 512]
        pack_m[32 * t : 32 * t + 32, 512:1024] = up_ref[:, 512 * t : 512 * t + 512]
        pack_m[32 * t : 32 * t + 32, 1024:1536] = down_ref[:, 512 * t : 512 * t + 512]

    jumps = [z == 3, None, z == 0]
    passes = (z == 1) | (z == 2)

    def rise(ref, piece, ss, rs, base):
        for j in (1, 0, 2):
            item = copy(
                ref.at[piece(z)], ref.at[piece(z)], ss.at[base + j], rs.at[base + j], levels[j][0]
            )
            if jumps[j] is None:
                begin(item)
            else:
                pl.when(jnp.logical_not(jumps[j]))(item.start)
                pending.append((jumps[j], item))

    def rise_pass(ref, piece, ss, rs, base):
        arrived = ref.at[piece(sources[1])]
        copy(arrived, arrived, ss.at[base + 1], rs.at[base + 1], levels[1][0]).wait_recv()
        slot = jnp.where(z == 1, 0, 2)
        end = jnp.where(z == 1, 0, 3)
        item = copy(arrived, arrived, ss.at[base + 3], rs.at[base + slot], (end * 2 + xi, sq))
        pl.when(passes)(item.start)
        pending.append((jnp.logical_not(passes), item))

    def rise_wait(ref, piece, ss, rs, base, j):
        arrived = ref.at[piece(sources[j])]
        copy(arrived, arrived, ss.at[base + j], rs.at[base + j], levels[j][0]).wait_recv()

    groups = [(w1, 0, 1024), (w2, 1024, 512)]

    def level_rows(zz):
        return span(zz * 256, 256)

    def weights_out(n):
        ref, first, width = groups[n]
        ref[my_rows, :] = pack_m[span(me * 32, 32), first : first + width]
        for k, (device, g) in enumerate(teams):
            item = copy(
                pack_m.at[span(g * 32, 32), pl.ds(first, width)],
                ref.at[my_rows, :], w_ss.at[n, k], w_rs.at[n, k], device,
            )
            item.start()
            pack_sends.append(item)

    def weights_up(n):
        ref = groups[n][0]
        for k, (device, g) in enumerate(teams):
            rows = span((z * 8 + g) * 32, 32)
            copy(ref.at[rows, :], ref.at[rows, :], w_ss.at[n, k], w_rs.at[n, k], device).wait_recv()
        rise(ref, level_rows, w_ss.at[n], w_rs.at[n], 7)

    def weights_pass(n):
        rise_pass(groups[n][0], level_rows, w_ss.at[n], w_rs.at[n], 7)

    def weights_in(n):
        for j in (0, 2):
            rise_wait(groups[n][0], level_rows, w_ss.at[n], w_rs.at[n], 7, j)

    halves = [pl.ds(0, 768), pl.ds(768, 256)]

    def slab(n, zz, xx):
        return span((zz * 2 + xx) * 128, 128), halves[n]

    def slab_up(n):
        rise(w0, lambda zz: slab(n, zz, xi), wa_ss.at[n], wa_rs.at[n], 0)
        mine = w0.at[slab(n, z, xi)]
        begin(copy(mine, mine, wa_ss.at[n, 4], wa_rs.at[n, 4], across))

    def slab_pass(n):
        rise_pass(w0, lambda zz: slab(n, zz, xi), wa_ss.at[n], wa_rs.at[n], 0)
        for j in (1, 0, 2):
            if j != 1:
                rise_wait(w0, lambda zz: slab(n, zz, xi), wa_ss.at[n], wa_rs.at[n], 0, j)
            block = w0.at[slab(n, sources[j], xi)]
            begin(copy(block, block, wa_ss.at[n, 5 + j], wa_rs.at[n, 5 + j], across))

    def slab_in(n):
        for j in range(4):
            block = w0.at[slab(n, z if j == 0 else sources[j - 1], 1 - xi)]
            copy(block, block, wa_ss.at[n, 4 + j], wa_rs.at[n, 4 + j], across).wait_recv()

    for k, (device, g) in enumerate(teams):
        copy(vec_all.at[z, g], vec_all.at[z, g], vec_ss.at[k], vec_rs.at[k], device).wait_recv()
    for j, (device, _) in enumerate(levels):
        begin(copy(vec_all.at[z], vec_all.at[z], vec_ss.at[7 + j], vec_rs.at[7 + j], device))
    for i, k in enumerate(ROW_TEAM):
        device, g = teams[k]
        rows = w0.at[span((z * 8 + g) * 32, 32), :]
        copy(rows, rows, wr_ss.at[i], wr_rs.at[i], device).wait_recv()
    slab_up(0)
    weights_out(0)
    for j in range(3):
        block = vec_all.at[sources[j]]
        copy(block, block, vec_ss.at[7 + j], vec_rs.at[7 + j], levels[j][0]).wait_recv()
    for k in range(8):
        total = vec_all[k // 2, 4 * (k % 2)]
        for j in range(1, 4):
            total = total + vec_all[k // 2, 4 * (k % 2) + j]
        vecs[:, 128 * k : 128 * k + 128] = total

    def vector(n):
        return vecs[n : n + 1, :]

    def row_rows(m, cc, yy):
        return span(m * 512 + cc * 256 + yy * 128, 128)

    def row_start(ref, e, m):
        block = ref.at[row_rows(m, c, y), :]
        begin(copy(block, block, ga_ss.at[e, m, 0], ga_rs.at[e, m, 0], beside))
        begin(copy(block, block, ga_ss.at[e, m, 1], ga_rs.at[e, m, 1], sibling))

    def row_pass(ref, e, m):
        block = ref.at[row_rows(m, c, 1 - y), :]
        copy(block, block, ga_ss.at[e, m, 0], ga_rs.at[e, m, 0], beside).wait_recv()
        begin(copy(block, block, ga_ss.at[e, m, 2], ga_rs.at[e, m, 2], sibling))

    def row_end(ref, e, m):
        for which, yy in ((1, y), (2, 1 - y)):
            block = ref.at[row_rows(m, 1 - c, yy), :]
            copy(block, block, ga_ss.at[e, m, which], ga_rs.at[e, m, which], sibling).wait_recv()

    def slot_rows(m, cc, place):
        return span(m * 1024 + cc * 512 + place * 128, 128)

    def gather_start(ref, e, m):
        block = ref.at[slot_rows(m, c, chip), :]
        for r in (0, 1, 3):
            begin(copy(block, block, ag_ss.at[e, m, r], ag_rs.at[e, m, r], teams[r][0]))

    def gather_hand(ref, e, m, r):
        block = ref.at[slot_rows(m, c, chips[r]), :]
        copy(block, block, ag_ss.at[e, m, r], ag_rs.at[e, m, r], teams[r][0]).wait_recv()
        begin(copy(block, block, ag_ss.at[e, m, 4 + r], ag_rs.at[e, m, 4 + r], sibling))

    def gather_pass(ref, e, m, last):
        first = 1 - last
        gather_hand(ref, e, m, first)
        block = ref.at[slot_rows(m, c, chips[first]), :]
        begin(copy(block, block, ag_ss.at[e, m, 2], ag_rs.at[e, m, 2], teams[last][0]))
        gather_hand(ref, e, m, last)

    def gather_far(ref, e, m):
        gather_hand(ref, e, m, 2)

    def gather_end(ref, e, m):
        for r in range(4):
            place = chip if r == 3 else chips[r]
            which = 3 if r == 3 else 4 + r
            block = ref.at[slot_rows(m, 1 - c, place), :]
            copy(block, block, ag_ss.at[e, m, which], ag_rs.at[e, m, which], sibling).wait_recv()

    for m in range(2):
        unit, _ = unit_of(x_ref[m].astype(F32))
        n1[row_rows(m, c, y), :] = (unit * vector(0) + vector(1)).astype(BF)
        row_start(n1, 0, m)
    for m in range(2):
        db[slot_rows(m, c, chip), :] = (g_ref[m].astype(F32) * vector(5)).astype(BF)
    gather_start(db, 0, 0)

    def make_trig(index, carry):
        m, slot = index // 4, index % 4
        cc, yy = slot // 2, slot % 2
        row = vec_all[z, xi * 4 + yy * 2 + cc, pl.ds(6 + m, 1), :]
        places = jnp.transpose(jnp.broadcast_to(row, (128, 128)))
        rows = span(index * 128, 128)
        pos[rows, :] = places
        hits = lax.broadcasted_iota(jnp.int32, (128, PLACES), 1).astype(F32) == jnp.concatenate(
            [places, places], axis=1
        )
        both = dot(hits.astype(F32).astype(BF), table_ref[...])
        trig[rows, :] = both[:, :128] + both[:, 128:]
        return carry

    lax.fori_loop(0, 8, make_trig, 0)

    def expand(rows, count):
        both = trig[rows, :]
        front = lax.broadcasted_iota(jnp.int32, (count, 128), 1) % 64 < 32
        cosine = jnp.where(front, both, pltpu.roll(both, 32, 1))
        sine = jnp.where(front, -pltpu.roll(both, 96, 1), both)
        return front, cosine, sine

    def swap(values, front):
        return jnp.where(front, pltpu.roll(values, 96, 1), pltpu.roll(values, 32, 1))

    slab_pass(0)
    slab_up(1)
    weights_up(0)
    row_pass(n1, 0, 0)
    row_pass(n1, 0, 1)
    gather_pass(db, 0, 0, 1)
    weights_out(1)
    slab_in(0)

    first_head = lax.broadcasted_iota(jnp.int32, (128, 128), 1) < 64

    def split_heads(values):
        zero = jnp.zeros_like(values)
        return jnp.concatenate(
            [jnp.where(first_head, values, zero), jnp.where(first_head, zero, values)], axis=0
        )

    def join_heads(values):
        return jnp.where(first_head, values[:128], values[128:])

    def project(m):
        def step(i, carry):
            rows = span(m * 512 + i * 256, 256)
            raw = dot(n1[rows, :], w0[:, 0:768])
            front, cosine, sine = expand(rows, 256)
            for b in range(4):
                part = raw[:, 128 * b : 128 * b + 128]
                qkv[rows, 128 * b : 128 * b + 128] = (
                    part * cosine + swap(part, front) * sine
                ).astype(BF)
            qkv[rows, 512:768] = raw[:, 512:768].astype(BF)
            return carry

        lax.fori_loop(0, 2, step, 0)

    def block_rows(m, s):
        return span(m * 512 + (s % 2) * 256 + (s // 2) * 128, 128)

    def pair(b, p):
        return slice(256 * b + 128 * p, 256 * b + 128 * p + 128)

    def attend(m):
        def step(s, carry):
            rows = block_rows(m, s)
            before = block_rows(m, jnp.maximum(s - 1, 0))
            r = lax.broadcasted_iota(jnp.int32, (128, 256), 0)
            k = lax.broadcasted_iota(jnp.int32, (128, 256), 1)
            back = r + 128 - k
            places = pos[rows, :]
            limit = jnp.minimum(jnp.concatenate([places, places], axis=1).astype(jnp.int32), 127)
            limit = jnp.minimum(limit, s * 128 + r)
            allowed = (back >= 0) & (back <= limit)
            allowed = jnp.concatenate([allowed, allowed], axis=0)
            for p in range(2):
                query = split_heads(qkv[rows, pair(0, p)])
                keys = jnp.concatenate([qkv[before, pair(1, p)], qkv[rows, pair(1, p)]], axis=0)
                held = jnp.concatenate([qkv[before, pair(2, p)], qkv[rows, pair(2, p)]], axis=0)
                scores = dot_rows(query, keys) * (HD ** -0.5)
                scores = jnp.where(allowed, scores, NEGATIVE)
                top = jnp.max(scores, axis=-1, keepdims=True)
                exponent = jnp.exp(scores - top)
                total = jnp.sum(exponent, axis=-1, keepdims=True)
                share = (exponent / total).astype(BF)
                probs[(m * 4 + s) * 2 + p] = share
                att[rows, pair(0, p)] = join_heads(dot(share, held)).astype(BF)
            return carry

        lax.fori_loop(0, 4, step, 0)

    def row_send(e, m):
        return copy(
            send_a0.at[m, span((1 - y) * 128, 128), :], recv_d0.at[m], ra_ss.at[e, m, 1],
            ra_rs.at[e, m, 1], beside,
        )

    def row_scatter(e, m, compute):
        hand = copy(send_b.at[m], recv_c0.at[m], ra_ss.at[e, m, 0], ra_rs.at[e, m, 0], sibling)

        def step(j, carry):
            part = compute(pl.multiple_of(m * 512 + ((c + 1 + j) % 2) * 256, 256))

            @pl.when(j == 0)
            def _():
                send_b[m] = part.astype(BF)
                hand.start()

            @pl.when(j == 1)
            def _():
                hand.wait_recv()
                send_a0[m] = (part + recv_c0[m].astype(F32)).astype(BF)
                row_send(e, m).start()

            return carry

        lax.fori_loop(0, 2, step, 0)
        hand.wait_send()

    def row_scatter_end(e, m):
        row_send(e, m).wait()
        return send_a0[m, span(y * 128, 128), :].astype(F32) + recv_d0[m].astype(F32)

    def scatter(e, m, compute):
        def step(j, carry):
            cc = (c + 1 + j // 2) % 2
            xx = (xi + 1 + j % 2) % 2
            part = compute(pl.multiple_of(m * 1024 + cc * 512 + xx * 256, 256))
            there = span(xx * 256, 256)

            @pl.when(j < 2)
            def _():
                send_b[j] = part.astype(BF)
                copy(
                    send_b.at[j], recv_c.at[e, m, there, :], rs_ss.at[e, m, j], rs_rs.at[e, m, j],
                    sibling,
                ).start()

            @pl.when(j >= 2)
            def _():
                copy(
                    send_b.at[j - 2], recv_c.at[e, m, there, :], rs_ss.at[e, m, j - 2],
                    rs_rs.at[e, m, j - 2], sibling,
                ).wait_recv()
                send_a[m, there, :] = (
                    part + recv_c[e, m, there, :].astype(F32)
                ).astype(BF)

            @pl.when(j == 2)
            def _():
                scatter_send(e, m, 2).start()
                if LEG[e] != 1:
                    scatter_send(e, m, 0).start()

            @pl.when(j == 3)
            def _():
                if LEG[e] != 0:
                    scatter_send(e, m, 1).start()

            return carry

        lax.fori_loop(0, 4, step, 0)
        for j in range(2):
            copy(
                send_b.at[j], recv_c.at[e, m, pl.ds(0, 256), :], rs_ss.at[e, m, j],
                rs_rs.at[e, m, j], sibling,
            ).wait_send()

    def scatter_send(e, m, r):
        rows = span(chips[r] * 128, 128)
        return copy(
            send_a.at[m, rows, :], recv_d.at[e, m, r], rs_ss.at[e, m, 2 + r],
            rs_rs.at[e, m, 2 + r], teams[r if r < 2 or LEG[e] is None else LEG[e]][0],
        )

    def scatter_pass(e, m):
        r = 1 - LEG[e]
        rows = span(chips[r] * 128, 128)
        scatter_send(e, m, 2).wait_recv()
        send_a[m, rows, :] = (
            send_a[m, rows, :].astype(F32) + recv_d[e, m, 2].astype(F32)
        ).astype(BF)
        scatter_send(e, m, r).start()

    def scatter_end(e, m):
        direct = LEG[e] is None
        for r in range(3):
            if r < 2 or direct:
                scatter_send(e, m, r).wait()
            else:
                scatter_send(e, m, r).wait_send()
        total = send_a[m, span(chip * 128, 128), :].astype(F32)
        for r in range(3 if direct else 2):
            total = total + recv_d[e, m, r].astype(F32)
        return total

    def outwards(row):
        return dot(att[pl.ds(row, 256), :], outw[...])

    row_end(n1, 0, 0)
    project(0)
    slab_pass(1)
    attend(0)
    slab_in(1)
    for i, k in enumerate(ROW_TEAM):
        device, g = teams[k]
        begin(
            copy(
                w0.at[span((g % 4) * 256, 256), pl.ds(768, 256)],
                outw.at[:, span(sq * 256, 256)], o_ss.at[i], o_rs.at[i], device,
            )
        )
    outw[:, span(sq * 256, 256)] = w0[span(sq * 256, 256), 768:1024]
    row_end(n1, 0, 1)
    project(1)
    for i, k in enumerate(ROW_TEAM):
        device, g = teams[k]
        copy(
            w0.at[span((g % 4) * 256, 256), pl.ds(768, 256)],
            outw.at[:, span((g % 4) * 256, 256)], o_ss.at[i], o_rs.at[i], device,
        ).wait_recv()
    row_scatter(0, 0, outwards)
    gather_start(db, 0, 1)
    weights_up(1)
    attend(1)
    row_scatter(0, 1, outwards)

    def second_norm(m):
        total = row_scatter_end(0, m)
        attn[m] = total
        middle = x_ref[m].astype(F32) + vector(4) * total
        mid[m] = middle
        unit, _ = unit_of(middle)
        n2[slot_rows(m, c, chip), :] = (unit * vector(2) + vector(3)).astype(BF)

    gather_far(db, 0, 0)
    second_norm(0)
    gather_start(n2, 1, 0)
    gather_pass(db, 0, 1, 0)
    weights_pass(0)
    second_norm(1)
    gather_start(n2, 1, 1)
    gather_pass(n2, 1, 0, 0)
    gather_far(db, 0, 1)
    gather_far(n2, 1, 0)
    gather_pass(n2, 1, 1, 1)
    weights_pass(1)

    def mlp(row):
        rows = pl.ds(row, 256)
        both = dot(n2[rows, :], w1[...])
        d_hidden = dot(db[rows, :], w2[...])
        gate, up = both[:, :512], both[:, 512:]
        sig = sigmoid(gate)
        silu = gate * sig
        hid[rows, :] = (silu * up).astype(BF)
        dgu[rows, 0:512] = (d_hidden * up * sig * (1.0 + gate * (1.0 - sig))).astype(BF)
        dgu[rows, 512:1024] = (d_hidden * silu).astype(BF)
        return dot_rows(dgu[rows, :], w1[...])

    weights_in(0)
    weights_in(1)
    gather_end(db, 0, 0)
    gather_end(n2, 1, 0)
    scatter(0, 0, mlp)
    gather_far(n2, 1, 1)
    gather_end(db, 0, 1)
    gather_end(n2, 1, 1)
    scatter(0, 1, mlp)

    turned = (z == 0) | (z == 2)
    at_end = (z == 0) | (z == 3)

    def target(i):
        inner = jnp.where(i == 3, 1, jnp.where(i == 0, 0, i + 1))
        plain = jnp.where(at_end, i, inner)
        return jnp.where(turned, 3 - plain, plain)

    def descend(n, i, stage, arrive, relay):
        zz = target(i)

        @pl.when(at_end & (i == 0))
        def _():
            via = jnp.where(z == 0, 1, 2)
            copy(stage.at[i], relay, z_ss.at[n, i], z_rs.at[n, 3], (via * 2 + xi, sq)).start()

        @pl.when(jnp.logical_not(at_end & (i == 0)) & (at_end | (i < 2)))
        def _():
            slot = (zz + 3 - z) % 4
            copy(
                stage.at[i], arrive.at[slot], z_ss.at[n, i], z_rs.at[n, slot], (zz * 2 + xi, sq)
            ).start()

    def descend_pass(n, stage, arrive, relay):
        @pl.when(passes)
        def _():
            zz = target(2)
            slot = (zz + 3 - z) % 4
            copy(stage.at[2], relay, z_ss.at[n, 2], z_rs.at[n, 3], levels[0][0]).wait_recv()
            stage[2] = (stage[2].astype(F32) + relay[...].astype(F32)).astype(BF)
            copy(
                stage.at[2], arrive.at[slot], z_ss.at[n, 2], z_rs.at[n, slot], (zz * 2 + xi, sq)
            ).start()

    def weight_grad(n, left, right, stage, own, arrive, relay):
        def step(i, carry):
            part = dot_cols(left[:, span(target(i) * 256, 256)], right[...])

            @pl.when(i < 3)
            def _():
                stage[i] = part.astype(BF)
                descend(n, i, stage, arrive, relay)

            @pl.when(i == 3)
            def _():
                own[...] = part.astype(own.dtype)

            return carry

        lax.fori_loop(0, 4, step, 0)

    weight_grad(0, n2, dgu, stage_g, own_g, zg_ref, relay_g)

    def norm_back(grad, values, gain, row):
        unit, inverse = unit_of(values)
        gacc[row : row + 1, :] += jnp.sum(grad * unit, axis=0, keepdims=True)
        gacc[row + 1 : row + 2, :] += jnp.sum(grad, axis=0, keepdims=True)
        scaled = grad * gain
        return inverse * (
            scaled
            - jnp.mean(scaled, axis=-1, keepdims=True)
            - unit * jnp.mean(scaled * unit, axis=-1, keepdims=True)
        )

    def second_norm_back(m):
        grad = scatter_end(0, m)
        d_mid = g_ref[m].astype(F32) + norm_back(grad, mid[m], vector(2), 2)
        gacc[4:5, :] += jnp.sum(d_mid * attn[m], axis=0, keepdims=True)
        attn[m] = d_mid
        da[row_rows(m, c, y), :] = (vector(4) * d_mid).astype(BF)
        row_start(da, 1, m)

    second_norm_back(0)
    weight_grad(1, db, hid, stage_d, own_d, zd_ref, relay_d)

    def downwards(row):
        return dot_rows(hid[pl.ds(row, 256), :], w2[...])

    def attend_back(m):
        def step(s, carry):
            rows = block_rows(m, s)
            before = block_rows(m, jnp.maximum(s - 1, 0))
            d_att = dot_rows(da[rows, :], outw[...]).astype(BF)
            here = span(s * 128, 128)
            prior = span(jnp.maximum(s - 1, 0) * 128, 128)
            for p in range(2):
                d_heads = split_heads(d_att[:, 128 * p : 128 * p + 128])
                query = split_heads(qkv[rows, pair(0, p)])
                keys = jnp.concatenate([qkv[before, pair(1, p)], qkv[rows, pair(1, p)]], axis=0)
                held = jnp.concatenate([qkv[before, pair(2, p)], qkv[rows, pair(2, p)]], axis=0)
                share = probs[(m * 4 + s) * 2 + p]
                weights = share.astype(F32)
                d_probs = dot_rows(d_heads, held)
                inner = jnp.sum(weights * d_probs, axis=-1, keepdims=True)
                d_scores = (weights * (d_probs - inner) * (HD ** -0.5)).astype(BF)
                dqs[here, pair(0, p)] = join_heads(dot(d_scores, keys))
                d_keys = dot_cols(d_scores, query)
                d_held = dot_cols(share, d_heads)
                dkv[prior, pair(0, p)] += d_keys[:128]
                dkv[prior, pair(1, p)] += d_held[:128]
                dkv[here, pair(0, p)] = d_keys[128:]
                dkv[here, pair(1, p)] = d_held[128:]
            return carry

        lax.fori_loop(0, 4, step, 0)

        def finish(s, carry):
            rows = block_rows(m, s)
            here = span(s * 128, 128)
            front, cosine, sine = expand(rows, 128)
            for b in range(4):
                part = dqs[here, 128 * b : 128 * b + 128] if b < 2 else dkv[here, pair(0, b - 2)]
                qkv[rows, 128 * b : 128 * b + 128] = (
                    part * cosine - swap(part, front) * sine
                ).astype(BF)
            qkv[rows, 512:768] = dkv[here, 256:512].astype(BF)
            return carry

        lax.fori_loop(0, 4, finish, 0)

    def inwards(row):
        return dot_rows(qkv[pl.ds(row, 256), :], w0[:, 0:768])

    dkv[...] = jnp.zeros_like(dkv)
    scatter(1, 0, downwards)
    row_pass(da, 1, 0)
    second_norm_back(1)
    row_end(da, 1, 0)
    attend_back(0)
    row_scatter(1, 0, inwards)
    scatter_pass(1, 0)
    scatter(1, 1, downwards)
    row_pass(da, 1, 1)
    row_end(da, 1, 1)
    part = dot_cols(att[...], da[...])
    for u in range(4):
        gsend[u] = part[:, 256 * u : 256 * u + 256].astype(BF)
    gout[span(sq * 256, 256), :] = gsend[sq]
    for i, k in enumerate(ROW_TEAM):
        device, g = teams[k]
        begin(
            copy(gsend.at[g % 4], gout.at[span(sq * 256, 256), :], go_ss.at[i], go_rs.at[i], device)
        )

    attend_back(1)
    row_scatter(1, 1, inwards)
    def mine_of(values):
        return jnp.where(xi == 0, values[:128], values[128:])

    def other_of(values):
        return jnp.where(xi == 0, values[128:], values[:128])

    for i, k in enumerate(ROW_TEAM):
        device, g = teams[k]
        theirs = span((g % 4) * 256, 256)
        copy(gsend.at[g % 4], gout.at[theirs, :], go_ss.at[i], go_rs.at[i], device).wait_recv()
    for j in range(4):
        zz = target(j)
        begin(
            copy(
                gout.at[span((zz * 2 + 1 - xi) * 128, 128), :], side_o.at[j], sx_ss.at[1, j],
                sx_rs.at[1, j], across,
            )
        )

    def qkv_grad(j, carry):
        part = dot_cols(n1[:, span(target(j) * 256, 256)], qkv[...])
        send_q[j] = other_of(part).astype(BF)
        copy(send_q.at[j], side_q.at[j], sx_ss.at[0, j], sx_rs.at[0, j], across).start()
        keep_q[j] = mine_of(part).astype(BF)
        return carry

    lax.fori_loop(0, 4, qkv_grad, 0)


    def summed(n, i, mine, side, stage, own, arrive, relay):
        copy(side.at[i], side.at[i], sx_ss.at[n, i], sx_rs.at[n, i], across).wait_recv()
        total = mine + side[i].astype(F32)
        if i < 3:
            stage[i] = total.astype(BF)
            descend(2 + n, i, stage, arrive, relay)
        else:
            own[...] = total

    def sum_q(i):
        summed(0, i, keep_q[i].astype(F32), side_q, stage_q, own_q, zq_ref, relay_q)

    def sum_o(i):
        part = gout[span((target(i) * 2 + xi) * 128, 128), :].astype(F32)
        summed(1, i, part, side_o, stage_o, own_o, zo_ref, relay_o)

    def summed_levels(n, stage, own, arrive):
        for i in range(3):
            copy(stage.at[i], arrive.at[i], z_ss.at[n, i], z_rs.at[n, i], levels[0][0]).wait_send()
        loads = [pltpu.make_async_copy(arrive.at[j], stage.at[j], loc_sem.at[j]) for j in range(3)]
        absent = [z == 0, None, z == 3]
        for j in range(3):
            def load(j=j):
                copy(
                    stage.at[j], arrive.at[j], z_ss.at[n, j], z_rs.at[n, j], levels[0][0]
                ).wait_recv()
                loads[j].start()

            def clear(j=j):
                stage[j] = jnp.zeros(stage.shape[1:], BF)

            if absent[j] is None:
                load()
            else:
                pl.when(jnp.logical_not(absent[j]))(load)
                pl.when(absent[j])(clear)
        for j in range(3):
            if absent[j] is None:
                loads[j].wait()
            else:
                pl.when(jnp.logical_not(absent[j]))(loads[j].wait)
        total = own[...].astype(F32)
        for j in range(3):
            total = total + stage[j].astype(F32)
        return total.astype(BF)

    def last_copies(n, pack, first, width, fin, people, who):
        found = []
        for i, k in enumerate(people):
            device, g = teams[k]
            found.append(
                copy(
                    pack.at[span((g % who) * 32, 32), pl.ds(first, width)],
                    fin.at[me % who, :, pl.ds(first, width)], f_ss.at[n, i], f_rs.at[n, i], device,
                )
            )
        return found

    def finals(n, first, width, stage, own, arrive, pack, fin, people, who):
        pack[:, first : first + width] = summed_levels(n, stage, own, arrive)
        stay = pltpu.make_async_copy(
            pack.at[span((me % who) * 32, 32), pl.ds(first, width)],
            fin.at[me % who, :, pl.ds(first, width)], loc_sem.at[3],
        )
        stay.start()
        for item in last_copies(n, pack, first, width, fin, people, who):
            item.start()
        stay.wait()

    plans = [
        (0, 0, 1024, stage_g, own_g, zg_ref, pack_m, fin_m, range(7), 8),
        (1, 1024, 512, stage_d, own_d, zd_ref, pack_m, fin_m, range(7), 8),
        (3, 768, 256, stage_o, own_o, zo_ref, pack_a, fin_a, ROW_TEAM, 4),
        (2, 0, 768, stage_q, own_q, zq_ref, pack_a, fin_a, ROW_TEAM, 4),
    ]
    def first_norm_back(m):
        grad = row_scatter_end(1, m)
        back = norm_back(grad, x_ref[m].astype(F32), vector(0), 0)
        dx_ref[m] = (attn[m] + back).astype(BF)

    def result(m):
        branch = scatter_end(1, m)
        gacc[5:6, :] += jnp.sum(g_ref[m].astype(F32) * branch, axis=0, keepdims=True)
        y_ref[m] = (mid[m] + vector(5) * branch).astype(BF)

    descend_pass(0, stage_g, zg_ref, relay_g)
    for i in range(4):
        sum_o(i)
    sum_q(0)
    scatter_pass(1, 1)
    sum_q(1)
    descend_pass(1, stage_d, zd_ref, relay_d)
    first_norm_back(0)
    sum_q(2)
    descend_pass(3, stage_o, zo_ref, relay_o)
    first_norm_back(1)
    sum_q(3)
    result(0)
    result(1)
    for k in range(8):
        gv_send[k] = gacc[:, 128 * k : 128 * k + 128]
    for k, (device, g) in enumerate(teams):
        begin(copy(gv_send.at[g], gv_in.at[k], gv_ss.at[k], gv_rs.at[k], device))

    descend_pass(2, stage_q, zq_ref, relay_q)
    for item in pack_sends:
        item.wait_send()
    finals(*plans[0])
    for item in pending:
        if isinstance(item, tuple):
            pl.when(jnp.logical_not(item[0]))(item[1].wait_send)
        else:
            item.wait_send()
    for j in range(4):
        copy(send_q.at[j], side_q.at[j], sx_ss.at[0, j], sx_rs.at[0, j], across).wait_send()
    for k, (device, g) in enumerate(teams):
        copy(gv_send.at[g], gv_in.at[k], gv_ss.at[k], gv_rs.at[k], device).wait_recv()
    total = gv_send[me]
    for k in range(7):
        total = total + gv_in[k]
    gv_z[0] = total
    level_sends = []
    for j, (device, _) in enumerate(levels):
        item = copy(gv_z.at[0], gv_z.at[1 + j], gv_ss.at[7 + j], gv_rs.at[7 + j], device)
        item.start()
        level_sends.append(item)
    finals(*plans[1])
    for item in level_sends:
        item.wait()
    gv_all[me] = gv_z[0] + gv_z[1] + gv_z[2] + gv_z[3]
    for k, (device, g) in enumerate(teams):
        copy(gv_all.at[me], gv_all.at[me], gv_ss.at[10 + k], gv_rs.at[10 + k], device).start()
    finals(*plans[2])
    finals(*plans[3])
    for k, (device, g) in enumerate(teams):
        copy(gv_all.at[g], gv_all.at[g], gv_ss.at[10 + k], gv_rs.at[10 + k], device).wait()
    vg_ref[...] = gv_all[z * 2 + me // 4]
    for n, first, width, _, _, _, pack, fin, people, who in plans:
        for item in last_copies(n, pack, first, width, fin, people, who):
            item.wait()


def layer_fast(
    block_input,
    positions,
    out_grad,
    qkv_weight,
    out_weight,
    gate_weight,
    up_weight,
    down_weight,
    norm1_gain,
    norm1_shift,
    norm2_gain,
    norm2_shift,
    attn_scale,
    mlp_scale,
):
    vectors = jnp.stack(
        [norm1_gain, norm1_shift, norm2_gain, norm2_shift, attn_scale, mlp_scale]
    ).astype(F32)
    packed = jnp.concatenate([jnp.tile(vectors, (1, 4)), positions.astype(F32)], axis=0)
    vmem, anywhere = pl.BlockSpec(memory_space=pltpu.VMEM), pl.BlockSpec(memory_space=pl.ANY)
    dma = pltpu.SemaphoreType.DMA
    scratch = [
        pltpu.VMEM((4, 8, 8, 128), F32), pltpu.VMEM((8, 1024), F32), pltpu.VMEM((8, 1024), F32),
        pltpu.VMEM((7, 8, 128), F32), pltpu.VMEM((4, 8, 128), F32), pltpu.VMEM((8, 8, 128), F32),
        pltpu.VMEM((8, 8, 128), F32),
        pltpu.VMEM((128, 1024), BF), pltpu.VMEM((256, 1536), BF), pltpu.VMEM((1024, 1024), BF),
        pltpu.VMEM((1024, 1024), BF), pltpu.VMEM((1024, 512), BF), pltpu.VMEM((256, 1024), BF),
        pltpu.VMEM((1024, 1024), BF), pltpu.VMEM((2048, 1024), BF), pltpu.VMEM((2048, 1024), BF),
        pltpu.VMEM((1024, 1024), BF),
        pltpu.VMEM((1024, 768), BF), pltpu.VMEM((1024, 256), BF), pltpu.VMEM((16, 256, 256), BF),
        pltpu.VMEM((512, 256), F32), pltpu.VMEM((512, 512), F32),
        pltpu.VMEM((2048, 512), BF), pltpu.VMEM((2048, 1024), BF),
        pltpu.VMEM((2, 512, 1024), BF), pltpu.VMEM((2, 2, 512, 1024), BF),
        pltpu.VMEM((2, 2, 3, 128, 1024), BF), pltpu.VMEM((2, 256, 1024), BF),
        pltpu.VMEM((2, 256, 1024), BF), pltpu.VMEM((2, 256, 1024), BF),
        pltpu.VMEM((2, 128, 1024), BF),
        pltpu.VMEM((3, 128, 768), BF), pltpu.VMEM((3, 128, 256), BF),
        pltpu.VMEM((3, 256, 1024), BF), pltpu.VMEM((3, 256, 512), BF),
        pltpu.VMEM((128, 768), F32), pltpu.VMEM((128, 256), F32),
        pltpu.VMEM((256, 1024), BF), pltpu.VMEM((256, 512), BF),
        pltpu.VMEM((1024, 256), BF), pltpu.VMEM((4, 256, 256), BF),
        pltpu.VMEM((4, 128, 768), BF), pltpu.VMEM((4, 128, 256), BF),
        pltpu.VMEM((4, 128, 768), BF), pltpu.VMEM((4, 128, 768), BF),
        pltpu.VMEM((256, 1024), BF), pltpu.VMEM((256, 512), BF), pltpu.VMEM((128, 768), BF),
        pltpu.VMEM((128, 256), BF),
        pltpu.VMEM((2, 128, 1024), F32), pltpu.VMEM((2, 128, 1024), F32),
        pltpu.VMEM((1024, 128), F32), pltpu.VMEM((1024, 128), F32),
        dma((10,)), dma((10,)), dma((3,)), dma((3,)), dma((2, 8)), dma((2, 8)), dma((2, 11)), dma((2, 11)),
        dma((3,)), dma((3,)), dma((2, 2, 3)), dma((2, 2, 3)), dma((2, 2, 7)), dma((2, 2, 7)),
        dma((2, 2, 2)), dma((2, 2, 2)), dma((2, 2, 5)), dma((2, 2, 5)), dma((3,)), dma((3,)),
        dma((2, 4)), dma((2, 4)), dma((4, 4)), dma((4, 4)), dma((4, 7)), dma((4, 7)),
        dma((17,)), dma((17,)), dma((4,)),
    ]
    y, dx, vg, fin_a, fin_m = pl.pallas_call(
        layer_kernel,
        out_shape=(
            jax.ShapeDtypeStruct((2, 128, 1024), BF),
            jax.ShapeDtypeStruct((2, 128, 1024), BF),
            jax.ShapeDtypeStruct((8, 128), F32),
            jax.ShapeDtypeStruct((4, 32, 1024), BF),
            jax.ShapeDtypeStruct((8, 32, 1536), BF),
            jax.ShapeDtypeStruct((3, 128, 768), BF),
            jax.ShapeDtypeStruct((3, 128, 256), BF),
            jax.ShapeDtypeStruct((3, 256, 1024), BF),
            jax.ShapeDtypeStruct((3, 256, 512), BF),
        ),
        in_specs=[vmem] * 9,
        out_specs=(vmem, vmem, vmem) + (anywhere,) * 6,
        scratch_shapes=scratch,
        compiler_params=pltpu.CompilerParams(
            collective_id=0, has_side_effects=True, vmem_limit_bytes=VMEM_BYTES
        ),
        cost_estimate=pl.CostEstimate(
            flops=26_000_000_000, bytes_accessed=8_000_000, transcendentals=4_000_000
        ),
        name="layer",
    )(
        block_input, out_grad, packed, jnp.asarray(trig_table()), qkv_weight, out_weight,
        gate_weight, up_weight, down_weight.T,
    )[:5]
    fin_a, fin_m = fin_a.astype(F32), fin_m.astype(F32)
    grad_qkv = (
        fin_a[:, :, 0:768].reshape(4, 32, 3, 256).transpose(1, 2, 0, 3).reshape(32, 3072)
    )
    grad_out = fin_a[:, :, 768:1024].transpose(1, 0, 2).reshape(32, 1024)
    grad_gate = fin_m[:, :, 0:512].transpose(1, 0, 2).reshape(32, 4096)
    grad_up = fin_m[:, :, 512:1024].transpose(1, 0, 2).reshape(32, 4096)
    grad_down = fin_m[:, :, 1024:1536].transpose(0, 2, 1).reshape(4096, 32)
    part = lax.axis_index(("dp", "seq")) % 4
    vg = lax.dynamic_index_in_dim(vg.reshape(8, 4, 32), part, 1, keepdims=False)
    return (y, dx, grad_qkv, grad_out, grad_gate, grad_up, grad_down) + tuple(
        vg[i] for i in range(6)
    )


def fits(mesh):
    return mesh.shape["dp"] == 8 and mesh.shape["seq"] == 4


def solution(mesh):
    return jax.shard_map(
        layer_fast if fits(mesh) else body,
        mesh=mesh,
        in_specs=(
            P(None, ("dp", "seq"), None),
            P(None, ("dp", "seq")),
            P(None, ("dp", "seq"), None),
            P(("dp", "seq"), None),
            P(("dp", "seq"), None),
            P(("dp", "seq"), None),
            P(("dp", "seq"), None),
            P(None, ("dp", "seq")),
            P(("dp", "seq")),
            P(("dp", "seq")),
            P(("dp", "seq")),
            P(("dp", "seq")),
            P(("dp", "seq")),
            P(("dp", "seq")),
        ),
        out_specs=(
            P(None, ("dp", "seq"), None),
            P(None, ("dp", "seq"), None),
            P(("dp", "seq"), None),
            P(("dp", "seq"), None),
            P(("dp", "seq"), None),
            P(("dp", "seq"), None),
            P(None, ("dp", "seq")),
            P(("dp", "seq")),
            P(("dp", "seq")),
            P(("dp", "seq")),
            P(("dp", "seq")),
            P(("dp", "seq")),
            P(("dp", "seq")),
        ),
        check_vma=False,
    )
```

```python
import jax
import jax.numpy as jnp
import ml_dtypes
import numpy as np
from jax import lax
from jax.experimental import pallas as pl
from jax.experimental.pallas import tpu as pltpu
from jax.sharding import PartitionSpec as P

H = 16
HD = 64
WINDOW = 128


EPSILON = 1e-05
NEGATIVE = -1e30


def normalize(values, gain, shift):
    center = values - jnp.mean(values, axis=-1, keepdims=True)
    inverse = lax.rsqrt(jnp.mean(center * center, axis=-1, keepdims=True) + EPSILON)
    unit = center * inverse
    return (unit * gain + shift, unit, inverse)


def normalize_back(incoming, unit, inverse, gain):
    scaled = incoming * gain
    middle = (
        scaled
        - jnp.mean(scaled, axis=-1, keepdims=True)
        - unit * jnp.mean(scaled * unit, axis=-1, keepdims=True)
    )
    return (inverse * middle, jnp.sum(incoming * unit, axis=0), jnp.sum(incoming, axis=0))


def angles_of(places, size):
    inverse = 10000.0 ** (-(jnp.arange(size // 2, dtype=jnp.float32) * (2.0 / size)))
    return places.astype(jnp.float32)[:, None] * inverse[None, :]


def rotate(values, angles):
    half = values.shape[-1] // 2
    cosine = jnp.cos(angles)[:, None, :]
    sine = jnp.sin(angles)[:, None, :]
    first_half = values[..., :half]
    second_half = values[..., half:]
    return jnp.concatenate(
        [first_half * cosine - second_half * sine, second_half * cosine + first_half * sine],
        axis=-1,
    )


def unrotate(values, angles):
    half = values.shape[-1] // 2
    cosine = jnp.cos(angles)[:, None, :]
    sine = jnp.sin(angles)[:, None, :]
    first_half = values[..., :half]
    second_half = values[..., half:]
    return jnp.concatenate(
        [first_half * cosine + second_half * sine, second_half * cosine - first_half * sine],
        axis=-1,
    )


def pack_shards(shards):
    return jnp.concatenate([item.reshape(1, -1) for item in shards], axis=1)


def unpack_gathered(whole, shards):
    devices = whole.shape[0]
    result = []
    offset = 0
    for number, item in enumerate(shards):
        count = item.size
        piece = whole[:, offset : offset + count]
        offset = offset + count
        if number == 4:
            rows, cols = item.shape
            result.append(
                piece.reshape(devices, rows, cols).transpose(1, 0, 2).reshape(rows, devices * cols)
            )
        elif item.ndim == 2:
            result.append(piece.reshape(devices * item.shape[0], item.shape[1]))
        else:
            result.append(piece.reshape(-1))
    return tuple(result)


def pack_grads(totals, devices):
    pieces = []
    for number, item in enumerate(totals):
        if number == 4:
            rows, cols = item.shape
            pieces.append(
                item.reshape(rows, devices, cols // devices).transpose(1, 0, 2).reshape(devices, -1)
            )
        else:
            pieces.append(item.reshape(devices, -1))
    return jnp.concatenate(pieces, axis=1)


def unpack_summed(summed, shards):
    flat = summed.reshape(-1)
    result = []
    offset = 0
    for item in shards:
        count = item.size
        result.append(flat[offset : offset + count].reshape(item.shape))
        offset = offset + count
    return tuple(result)


def block_scores(query, keys_padded, values_padded, starts, first, size):
    block_query = lax.dynamic_slice_in_dim(query, first, size, 0)
    block_keys = lax.dynamic_slice_in_dim(keys_padded, first, size + WINDOW, 0)
    block_values = lax.dynamic_slice_in_dim(values_padded, first, size + WINDOW, 0)
    begin = lax.dynamic_slice_in_dim(starts, first, size, 0)
    here = first + jnp.arange(size, dtype=jnp.int32)
    there = first - WINDOW + jnp.arange(size + WINDOW, dtype=jnp.int32)
    allowed = (
        (there[None, :] >= begin[:, None])
        & (there[None, :] <= here[:, None])
        & (here[:, None] - there[None, :] < WINDOW)
    )
    raw = jnp.einsum("qhd,khd->hqk", block_query, block_keys, preferred_element_type=jnp.float32)
    scores = jnp.where(allowed[None], raw * HD ** (-0.5), NEGATIVE)
    return (scores, block_query, block_keys, block_values)


def attend_forward(query, keys_padded, values_padded, starts):
    length = query.shape[0]
    size = min(512, length)
    count = length // size

    def step(carry, index):
        scores, block_query, block_keys, block_values = block_scores(
            query, keys_padded, values_padded, starts, index * size, size
        )
        top = jnp.max(scores, axis=-1, keepdims=True)
        exponent = jnp.exp(scores - top)
        total = jnp.sum(exponent, axis=-1, keepdims=True)
        probs = (exponent / total).astype(jnp.bfloat16)
        outcome = jnp.einsum(
            "hqk,khd->qhd", probs, block_values, preferred_element_type=jnp.float32
        )
        return (carry, (outcome, (top + jnp.log(total))[..., 0]))

    unused, (outcomes, logs) = lax.scan(step, 0, jnp.arange(count, dtype=jnp.int32))
    return (outcomes.reshape(query.shape), logs)


def attend_backward(query, keys_padded, values_padded, starts, logs, grad_out):
    length = query.shape[0]
    size = min(512, length)
    count = length // size

    def step(carry, index):
        grad_query, grad_keys, grad_values = carry
        first = index * size
        scores, block_query, block_keys, block_values = block_scores(
            query, keys_padded, values_padded, starts, first, size
        )
        probs = jnp.exp(scores - logs[index][..., None])
        grad_block = lax.dynamic_slice_in_dim(grad_out, first, size, 0)
        grad_probs = jnp.einsum(
            "qhd,khd->hqk", grad_block, block_values, preferred_element_type=jnp.float32
        )
        inner = jnp.sum(probs * grad_probs, axis=-1, keepdims=True)
        grad_scores = (probs * (grad_probs - inner) * HD ** (-0.5)).astype(jnp.bfloat16)
        query_part = jnp.einsum(
            "hqk,khd->qhd", grad_scores, block_keys, preferred_element_type=jnp.float32
        )
        keys_part = jnp.einsum(
            "hqk,qhd->khd", grad_scores, block_query, preferred_element_type=jnp.float32
        )
        values_part = jnp.einsum(
            "hqk,qhd->khd",
            probs.astype(jnp.bfloat16),
            grad_block,
            preferred_element_type=jnp.float32,
        )
        grad_query = lax.dynamic_update_slice_in_dim(grad_query, query_part, first, 0)
        grad_keys = lax.dynamic_update_slice_in_dim(
            grad_keys,
            lax.dynamic_slice_in_dim(grad_keys, first, size + WINDOW, 0) + keys_part,
            first,
            0,
        )
        grad_values = lax.dynamic_update_slice_in_dim(
            grad_values,
            lax.dynamic_slice_in_dim(grad_values, first, size + WINDOW, 0) + values_part,
            first,
            0,
        )
        return ((grad_query, grad_keys, grad_values), None)

    start_state = (
        jnp.zeros(query.shape, jnp.float32),
        jnp.zeros(keys_padded.shape, jnp.float32),
        jnp.zeros(values_padded.shape, jnp.float32),
    )
    (grad_query, grad_keys, grad_values), unused = lax.scan(
        step, start_state, jnp.arange(count, dtype=jnp.int32)
    )
    return (grad_query, grad_keys, grad_values)


def attention_forward(query, keyset, valueset, places):
    rows, heads, depth = query.shape
    width = heads * depth
    parts = lax.axis_size("seq")
    slab = width // parts
    local = slab // depth
    packed = jnp.stack(
        [query.reshape(rows, width), keyset.reshape(rows, width), valueset], axis=1
    ).reshape(rows, 3, parts, slab)
    moved = lax.all_to_all(packed, "seq", split_axis=2, concat_axis=0, tiled=True)
    group = moved.shape[0]
    every = lax.all_gather(places, "seq", axis=0, tiled=True)
    starts = jnp.maximum(jnp.arange(group, dtype=jnp.int32) - every, 0)
    padding = jnp.zeros((WINDOW, local, depth), jnp.bfloat16)
    head_query = moved[:, 0, 0].reshape(group, local, depth)
    keys_padded = jnp.concatenate([padding, moved[:, 1, 0].reshape(group, local, depth)], axis=0)
    values_padded = jnp.concatenate([padding, moved[:, 2, 0].reshape(group, local, depth)], axis=0)
    outcome, logs = attend_forward(head_query, keys_padded, values_padded, starts)
    sent = outcome.astype(jnp.bfloat16).reshape(group, 1, slab)
    attended = lax.all_to_all(sent, "seq", split_axis=0, concat_axis=1, tiled=True).reshape(
        rows, width
    )
    return (attended, (head_query, keys_padded, values_padded, starts, logs))


def attention_backward(kept, grad_attended, rows, width):
    head_query, keys_padded, values_padded, starts, logs = kept
    depth = head_query.shape[-1]
    parts = lax.axis_size("seq")
    slab = width // parts
    local = slab // depth
    came = lax.all_to_all(
        grad_attended.reshape(rows, parts, slab), "seq", split_axis=1, concat_axis=0, tiled=True
    )
    group = came.shape[0]
    grad_out = came.reshape(group, local, depth)
    grad_query, grad_keys, grad_values = attend_backward(
        head_query, keys_padded, values_padded, starts, logs, grad_out
    )
    packed = (
        jnp.stack([grad_query, grad_keys[WINDOW:], grad_values[WINDOW:]], axis=1)
        .astype(jnp.bfloat16)
        .reshape(group, 3, 1, slab)
    )
    back = lax.all_to_all(packed, "seq", split_axis=0, concat_axis=2, tiled=True).reshape(
        rows, 3, width
    )
    return (back[:, 0], back[:, 1], back[:, 2])


def forward_micro(weights, block, places):
    (
        qkv_weight,
        out_weight,
        gate_weight,
        up_weight,
        down_weight,
        gain1,
        shift1,
        gain2,
        shift2,
        scale1,
        scale2,
    ) = weights
    rows, width = block.shape
    start_in = block.astype(jnp.float32)
    normed1, unit1, inverse1 = normalize(start_in, gain1, shift1)
    acted1 = normed1.astype(jnp.bfloat16)
    projected = jnp.dot(acted1, qkv_weight, preferred_element_type=jnp.float32)
    angles = angles_of(places, HD)
    query = rotate(projected[:, :width].reshape(rows, H, HD), angles).astype(jnp.bfloat16)
    keyset = rotate(projected[:, width : 2 * width].reshape(rows, H, HD), angles).astype(
        jnp.bfloat16
    )
    valueset = projected[:, 2 * width :].astype(jnp.bfloat16)
    attended, kept = attention_forward(query, keyset, valueset, places)
    attn = jnp.dot(attended, out_weight, preferred_element_type=jnp.float32)
    mid = start_in + scale1 * attn
    normed2, unit2, inverse2 = normalize(mid, gain2, shift2)
    acted2 = normed2.astype(jnp.bfloat16)
    gate = jnp.dot(acted2, gate_weight, preferred_element_type=jnp.float32)
    up_value = jnp.dot(acted2, up_weight, preferred_element_type=jnp.float32)
    hidden = (jax.nn.silu(gate) * up_value).astype(jnp.bfloat16)
    branch = jnp.dot(hidden, down_weight, preferred_element_type=jnp.float32)
    result = (mid + scale2 * branch).astype(jnp.bfloat16)
    saved = (
        acted1,
        unit1,
        inverse1,
        angles,
        kept,
        attended,
        attn,
        unit2,
        inverse2,
        acted2,
        gate,
        up_value,
        hidden,
        branch,
    )
    return (result, saved)


def backward_micro(weights, saved, cotangent):
    (
        qkv_weight,
        out_weight,
        gate_weight,
        up_weight,
        down_weight,
        gain1,
        shift1,
        gain2,
        shift2,
        scale1,
        scale2,
    ) = weights
    (
        acted1,
        unit1,
        inverse1,
        angles,
        kept,
        attended,
        attn,
        unit2,
        inverse2,
        acted2,
        gate,
        up_value,
        hidden,
        branch,
    ) = saved
    rows, width = attended.shape
    flow = cotangent.astype(jnp.float32)
    grad_branch = (scale2 * flow).astype(jnp.bfloat16)
    grad_scale2 = jnp.sum(flow * branch, axis=0)
    grad_down = jnp.einsum("rf,rd->fd", hidden, grad_branch, preferred_element_type=jnp.float32)
    grad_hidden = jnp.einsum(
        "rd,fd->rf", grad_branch, down_weight, preferred_element_type=jnp.float32
    )
    sigmoid_gate = jax.nn.sigmoid(gate)
    grad_gate = (
        grad_hidden * up_value * sigmoid_gate * (1.0 + gate * (1.0 - sigmoid_gate))
    ).astype(jnp.bfloat16)
    grad_up = (grad_hidden * gate * sigmoid_gate).astype(jnp.bfloat16)
    grad_gate_w = jnp.einsum("rd,rf->df", acted2, grad_gate, preferred_element_type=jnp.float32)
    grad_up_w = jnp.einsum("rd,rf->df", acted2, grad_up, preferred_element_type=jnp.float32)
    grad_acted2 = jnp.einsum(
        "rf,df->rd", grad_gate, gate_weight, preferred_element_type=jnp.float32
    ) + jnp.einsum("rf,df->rd", grad_up, up_weight, preferred_element_type=jnp.float32)
    grad_mid, grad_gain2, grad_shift2 = normalize_back(grad_acted2, unit2, inverse2, gain2)
    grad_mid = flow + grad_mid
    grad_scale1 = jnp.sum(grad_mid * attn, axis=0)
    grad_attn = (scale1 * grad_mid).astype(jnp.bfloat16)
    grad_out_w = jnp.einsum("rd,re->de", attended, grad_attn, preferred_element_type=jnp.float32)
    grad_attended = jnp.einsum(
        "re,de->rd", grad_attn, out_weight, preferred_element_type=jnp.float32
    ).astype(jnp.bfloat16)
    grad_query, grad_keys, grad_values = attention_backward(kept, grad_attended, rows, width)
    query_plain = unrotate(grad_query.astype(jnp.float32).reshape(rows, H, HD), angles).reshape(
        rows, width
    )
    keys_plain = unrotate(grad_keys.astype(jnp.float32).reshape(rows, H, HD), angles).reshape(
        rows, width
    )
    grad_projected = jnp.concatenate(
        [query_plain, keys_plain, grad_values.astype(jnp.float32)], axis=1
    ).astype(jnp.bfloat16)
    grad_qkv_w = jnp.einsum("rd,re->de", acted1, grad_projected, preferred_element_type=jnp.float32)
    grad_acted1 = jnp.einsum(
        "re,de->rd", grad_projected, qkv_weight, preferred_element_type=jnp.float32
    )
    grad_first, grad_gain1, grad_shift1 = normalize_back(grad_acted1, unit1, inverse1, gain1)
    grad_input = (grad_mid + grad_first).astype(jnp.bfloat16)
    terms = (
        grad_qkv_w,
        grad_out_w,
        grad_gate_w,
        grad_up_w,
        grad_down,
        grad_gain1,
        grad_shift1,
        grad_gain2,
        grad_shift2,
        grad_scale1,
        grad_scale2,
    )
    return (grad_input, terms)


def body(
    block_input,
    positions,
    out_grad,
    qkv_weight,
    out_weight,
    gate_weight,
    up_weight,
    down_weight,
    norm1_gain,
    norm1_shift,
    norm2_gain,
    norm2_shift,
    attn_scale,
    mlp_scale,
):
    shards = (
        qkv_weight,
        out_weight,
        gate_weight,
        up_weight,
        down_weight,
        norm1_gain,
        norm1_shift,
        norm2_gain,
        norm2_shift,
        attn_scale,
        mlp_scale,
    )
    devices = lax.axis_size(("dp", "seq"))
    outer = lax.axis_size("dp")
    inner = lax.axis_size("seq")
    packed = pack_shards(shards)
    totals = None
    results = []
    grads_in = []
    for index in range(block_input.shape[0]):
        weights = unpack_gathered(lax.all_gather(packed, ("dp", "seq"), axis=0, tiled=True), shards)
        result, saved = forward_micro(weights, block_input[index], positions[index])
        backward_weights = unpack_gathered(
            lax.all_gather(packed, ("dp", "seq"), axis=0, tiled=True), shards
        )
        grad_input, terms = backward_micro(backward_weights, saved, out_grad[index])
        if totals is None:
            totals = terms
        else:
            totals = tuple(
                (first_term + second_term for first_term, second_term in zip(totals, terms))
            )
        results.append(result)
        grads_in.append(grad_input)
    laid = pack_grads(totals, devices)
    laid = laid.reshape(outer, inner, laid.shape[1])
    partial_sum = lax.psum_scatter(laid.astype(jnp.bfloat16), "dp", scatter_dimension=0, tiled=True)
    summed = lax.psum_scatter(partial_sum, "seq", scatter_dimension=1, tiled=True).astype(
        jnp.float32
    )
    return (jnp.stack(results), jnp.stack(grads_in)) + unpack_summed(summed, shards)


VMEM_BYTES = 64 * 1024 * 1024
BF = jnp.bfloat16
F32 = jnp.float32
MESH = pl.DeviceIdType.MESH
TEAM = 8
PLACES = 256
RELATIONS = [(1, 0, 0), (0, 1, 0), (1, 1, 0), (0, 0, 1), (1, 0, 1), (0, 1, 1), (1, 1, 1)]
ROW_TEAM = (1, 3, 5)
LEG = (None, 0)


def trig_table():
    inverse = 10000.0 ** (-(np.arange(HD // 2, dtype=np.float64) * (2.0 / HD)))
    angles = np.arange(PLACES, dtype=np.float64)[:, None] * inverse[None, :]
    values = np.concatenate([np.cos(angles), np.sin(angles)] * 2, axis=1).astype(np.float32)
    high = values.astype(ml_dtypes.bfloat16)
    rest = (values - high.astype(np.float32)).astype(ml_dtypes.bfloat16)
    return np.concatenate([high, rest], axis=1)


def dot(a, b):
    return lax.dot_general(a, b, (((1,), (0,)), ((), ())), preferred_element_type=F32)


def dot_rows(a, b):
    return lax.dot_general(a, b, (((1,), (1,)), ((), ())), preferred_element_type=F32)


def dot_cols(a, b):
    return lax.dot_general(a, b, (((0,), (0,)), ((), ())), preferred_element_type=F32)


def sigmoid(v):
    return 0.5 * jnp.tanh(0.5 * v) + 0.5


def unit_of(values):
    center = values - jnp.mean(values, axis=-1, keepdims=True)
    inverse = lax.rsqrt(jnp.mean(center * center, axis=-1, keepdims=True) + EPSILON)
    return center * inverse, inverse


def layer_kernel(
    x_ref, g_ref, vec_ref, table_ref, qkv_ref, out_ref, gate_ref, up_ref, down_ref,
    y_ref, dx_ref, vg_ref, fin_a, fin_m, zq_ref, zo_ref, zg_ref, zd_ref,
    vec_all, vecs, gacc, gv_in, gv_z, gv_send, gv_all,
    pack_a, pack_m, w0, w1, w2, outw,
    n1, n2, db, da, qkv, att, probs, dqs, dkv, hid, dgu,
    send_a, recv_c, recv_d, send_b, send_a0, recv_c0, recv_d0,
    stage_q, stage_o, stage_g, stage_d, own_q, own_o, own_g, own_d, gout, gsend,
    side_q, side_o, keep_q, send_q, relay_g, relay_d, relay_q, relay_o,
    mid, attn, trig, pos,
    vec_ss, vec_rs, wr_ss, wr_rs, wa_ss, wa_rs, w_ss, w_rs, o_ss, o_rs, ga_ss, ga_rs, ag_ss, ag_rs,
    ra_ss, ra_rs, rs_ss, rs_rs, go_ss, go_rs, sx_ss, sx_rs, z_ss, z_rs, f_ss, f_rs,
    gv_ss, gv_rs, loc_sem,
):
    dp = lax.axis_index("dp")
    sq = lax.axis_index("seq")
    z, xi, y, c = dp // 2, dp % 2, sq // 2, sq % 2
    me = xi * 4 + sq
    chip = xi * 2 + y

    def copy(src, dst, ss, rs, device):
        return pltpu.make_async_remote_copy(
            src_ref=src, dst_ref=dst, send_sem=ss, recv_sem=rs,
            device_id=device, device_id_type=MESH,
        )

    def span(start, size):
        return pl.ds(pl.multiple_of(start, size), size)

    def team(k):
        kx, ky, kc = RELATIONS[k]
        xx, yy, cc = (xi + kx) % 2, (y + ky) % 2, (c + kc) % 2
        return (z * 2 + xx, yy * 2 + cc), xx * 4 + yy * 2 + cc

    def level(j):
        zz = (z + j) % 4
        return (zz * 2 + xi, sq), zz

    teams = [team(k) for k in range(7)]
    levels = [level(j) for j in range(1, 4)]
    sources = [(z + 4 - j) % 4 for j in range(1, 4)]
    across, beside, sibling = teams[0][0], teams[1][0], teams[3][0]
    chips = [(1 - xi) * 2 + y, xi * 2 + (1 - y), (1 - xi) * 2 + (1 - y)]

    pending = []
    pack_sends = []
    barrier = pltpu.get_barrier_semaphore()
    for device, _ in teams + levels:
        pl.semaphore_signal(barrier, inc=1, device_id=device, device_id_type=MESH)

    for t in range(4):
        for b in range(3):
            pack_a[32 * t : 32 * t + 32, 256 * b : 256 * b + 256] = qkv_ref[
                :, 1024 * b + 256 * t : 1024 * b + 256 * t + 256
            ]
        pack_a[32 * t : 32 * t + 32, 768:1024] = out_ref[:, 256 * t : 256 * t + 256]
    lane = lax.broadcasted_iota(jnp.int32, (8, 128), 1)
    sub = lax.broadcasted_iota(jnp.int32, (8, 128), 0)
    vec_all[z, me] = jnp.where((sub >= 6) | (lane // 32 == me % 4), vec_ref[...], 0.0)
    gacc[...] = jnp.zeros_like(gacc)
    pl.semaphore_wait(barrier, 10)

    def begin(item):
        item.start()
        pending.append(item)

    for k, (device, _) in enumerate(teams):
        begin(copy(vec_all.at[z, me], vec_all.at[z, me], vec_ss.at[k], vec_rs.at[k], device))

    my_rows = span((z * 8 + me) * 32, 32)
    w0[my_rows, :] = pack_a[span(sq * 32, 32), :]
    for i, k in enumerate(ROW_TEAM):
        device, g = teams[k]
        begin(
            copy(pack_a.at[span((g % 4) * 32, 32), :], w0.at[my_rows, :], wr_ss.at[i], wr_rs.at[i],
                 device)
        )
    for t in range(TEAM):
        pack_m[32 * t : 32 * t + 32, 0:512] = gate_ref[:, 512 * t : 512 * t + 512]
        pack_m[32 * t : 32 * t + 32, 512:1024] = up_ref[:, 512 * t : 512 * t + 512]
        pack_m[32 * t : 32 * t + 32, 1024:1536] = down_ref[:, 512 * t : 512 * t + 512]

    jumps = [z == 3, None, z == 0]
    passes = (z == 1) | (z == 2)

    def rise(ref, piece, ss, rs, base):
        for j in (1, 0, 2):
            item = copy(
                ref.at[piece(z)], ref.at[piece(z)], ss.at[base + j], rs.at[base + j], levels[j][0]
            )
            if jumps[j] is None:
                begin(item)
            else:
                pl.when(jnp.logical_not(jumps[j]))(item.start)
                pending.append((jumps[j], item))

    def rise_pass(ref, piece, ss, rs, base):
        arrived = ref.at[piece(sources[1])]
        copy(arrived, arrived, ss.at[base + 1], rs.at[base + 1], levels[1][0]).wait_recv()
        slot = jnp.where(z == 1, 0, 2)
        end = jnp.where(z == 1, 0, 3)
        item = copy(arrived, arrived, ss.at[base + 3], rs.at[base + slot], (end * 2 + xi, sq))
        pl.when(passes)(item.start)
        pending.append((jnp.logical_not(passes), item))

    def rise_wait(ref, piece, ss, rs, base, j):
        arrived = ref.at[piece(sources[j])]
        copy(arrived, arrived, ss.at[base + j], rs.at[base + j], levels[j][0]).wait_recv()

    groups = [(w1, 0, 1024), (w2, 1024, 512)]

    def level_rows(zz):
        return span(zz * 256, 256)

    def weights_out(n):
        ref, first, width = groups[n]
        ref[my_rows, :] = pack_m[span(me * 32, 32), first : first + width]
        for k, (device, g) in enumerate(teams):
            item = copy(
                pack_m.at[span(g * 32, 32), pl.ds(first, width)],
                ref.at[my_rows, :], w_ss.at[n, k], w_rs.at[n, k], device,
            )
            item.start()
            pack_sends.append(item)

    def weights_up(n):
        ref = groups[n][0]
        for k, (device, g) in enumerate(teams):
            rows = span((z * 8 + g) * 32, 32)
            copy(ref.at[rows, :], ref.at[rows, :], w_ss.at[n, k], w_rs.at[n, k], device).wait_recv()
        rise(ref, level_rows, w_ss.at[n], w_rs.at[n], 7)

    def weights_pass(n):
        rise_pass(groups[n][0], level_rows, w_ss.at[n], w_rs.at[n], 7)

    def weights_in(n):
        for j in (0, 2):
            rise_wait(groups[n][0], level_rows, w_ss.at[n], w_rs.at[n], 7, j)

    halves = [pl.ds(0, 768), pl.ds(768, 256)]

    def slab(n, zz, xx):
        return span((zz * 2 + xx) * 128, 128), halves[n]

    def slab_up(n):
        rise(w0, lambda zz: slab(n, zz, xi), wa_ss.at[n], wa_rs.at[n], 0)
        mine = w0.at[slab(n, z, xi)]
        begin(copy(mine, mine, wa_ss.at[n, 4], wa_rs.at[n, 4], across))

    def slab_pass(n):
        rise_pass(w0, lambda zz: slab(n, zz, xi), wa_ss.at[n], wa_rs.at[n], 0)
        for j in (1, 0, 2):
            if j != 1:
                rise_wait(w0, lambda zz: slab(n, zz, xi), wa_ss.at[n], wa_rs.at[n], 0, j)
            block = w0.at[slab(n, sources[j], xi)]
            begin(copy(block, block, wa_ss.at[n, 5 + j], wa_rs.at[n, 5 + j], across))

    def slab_in(n):
        for j in range(4):
            block = w0.at[slab(n, z if j == 0 else sources[j - 1], 1 - xi)]
            copy(block, block, wa_ss.at[n, 4 + j], wa_rs.at[n, 4 + j], across).wait_recv()

    for k, (device, g) in enumerate(teams):
        copy(vec_all.at[z, g], vec_all.at[z, g], vec_ss.at[k], vec_rs.at[k], device).wait_recv()
    for j, (device, _) in enumerate(levels):
        begin(copy(vec_all.at[z], vec_all.at[z], vec_ss.at[7 + j], vec_rs.at[7 + j], device))
    for i, k in enumerate(ROW_TEAM):
        device, g = teams[k]
        rows = w0.at[span((z * 8 + g) * 32, 32), :]
        copy(rows, rows, wr_ss.at[i], wr_rs.at[i], device).wait_recv()
    slab_up(0)
    weights_out(0)
    for j in range(3):
        block = vec_all.at[sources[j]]
        copy(block, block, vec_ss.at[7 + j], vec_rs.at[7 + j], levels[j][0]).wait_recv()
    for k in range(8):
        total = vec_all[k // 2, 4 * (k % 2)]
        for j in range(1, 4):
            total = total + vec_all[k // 2, 4 * (k % 2) + j]
        vecs[:, 128 * k : 128 * k + 128] = total

    def vector(n):
        return vecs[n : n + 1, :]

    def row_rows(m, cc, yy):
        return span(m * 512 + cc * 256 + yy * 128, 128)

    def row_start(ref, e, m):
        block = ref.at[row_rows(m, c, y), :]
        begin(copy(block, block, ga_ss.at[e, m, 0], ga_rs.at[e, m, 0], beside))
        begin(copy(block, block, ga_ss.at[e, m, 1], ga_rs.at[e, m, 1], sibling))

    def row_pass(ref, e, m):
        block = ref.at[row_rows(m, c, 1 - y), :]
        copy(block, block, ga_ss.at[e, m, 0], ga_rs.at[e, m, 0], beside).wait_recv()
        begin(copy(block, block, ga_ss.at[e, m, 2], ga_rs.at[e, m, 2], sibling))

    def row_end(ref, e, m):
        for which, yy in ((1, y), (2, 1 - y)):
            block = ref.at[row_rows(m, 1 - c, yy), :]
            copy(block, block, ga_ss.at[e, m, which], ga_rs.at[e, m, which], sibling).wait_recv()

    def slot_rows(m, cc, place):
        return span(m * 1024 + cc * 512 + place * 128, 128)

    def gather_start(ref, e, m):
        block = ref.at[slot_rows(m, c, chip), :]
        for r in (0, 1, 3):
            begin(copy(block, block, ag_ss.at[e, m, r], ag_rs.at[e, m, r], teams[r][0]))

    def gather_hand(ref, e, m, r):
        block = ref.at[slot_rows(m, c, chips[r]), :]
        copy(block, block, ag_ss.at[e, m, r], ag_rs.at[e, m, r], teams[r][0]).wait_recv()
        begin(copy(block, block, ag_ss.at[e, m, 4 + r], ag_rs.at[e, m, 4 + r], sibling))

    def gather_pass(ref, e, m, last):
        first = 1 - last
        gather_hand(ref, e, m, first)
        block = ref.at[slot_rows(m, c, chips[first]), :]
        begin(copy(block, block, ag_ss.at[e, m, 2], ag_rs.at[e, m, 2], teams[last][0]))
        gather_hand(ref, e, m, last)

    def gather_far(ref, e, m):
        gather_hand(ref, e, m, 2)

    def gather_end(ref, e, m):
        for r in range(4):
            place = chip if r == 3 else chips[r]
            which = 3 if r == 3 else 4 + r
            block = ref.at[slot_rows(m, 1 - c, place), :]
            copy(block, block, ag_ss.at[e, m, which], ag_rs.at[e, m, which], sibling).wait_recv()

    for m in range(2):
        unit, _ = unit_of(x_ref[m].astype(F32))
        n1[row_rows(m, c, y), :] = (unit * vector(0) + vector(1)).astype(BF)
        row_start(n1, 0, m)
    for m in range(2):
        db[slot_rows(m, c, chip), :] = (g_ref[m].astype(F32) * vector(5)).astype(BF)
    gather_start(db, 0, 0)

    def make_trig(index, carry):
        m, slot = index // 4, index % 4
        cc, yy = slot // 2, slot % 2
        row = vec_all[z, xi * 4 + yy * 2 + cc, pl.ds(6 + m, 1), :]
        places = jnp.transpose(jnp.broadcast_to(row, (128, 128)))
        rows = span(index * 128, 128)
        pos[rows, :] = places
        hits = lax.broadcasted_iota(jnp.int32, (128, PLACES), 1).astype(F32) == jnp.concatenate(
            [places, places], axis=1
        )
        both = dot(hits.astype(F32).astype(BF), table_ref[...])
        trig[rows, :] = both[:, :128] + both[:, 128:]
        return carry

    lax.fori_loop(0, 8, make_trig, 0)

    def expand(rows, count):
        both = trig[rows, :]
        front = lax.broadcasted_iota(jnp.int32, (count, 128), 1) % 64 < 32
        cosine = jnp.where(front, both, pltpu.roll(both, 32, 1))
        sine = jnp.where(front, -pltpu.roll(both, 96, 1), both)
        return front, cosine, sine

    def swap(values, front):
        return jnp.where(front, pltpu.roll(values, 96, 1), pltpu.roll(values, 32, 1))

    slab_pass(0)
    slab_up(1)
    weights_up(0)
    row_pass(n1, 0, 0)
    row_pass(n1, 0, 1)
    gather_pass(db, 0, 0, 1)
    weights_out(1)
    slab_in(0)

    first_head = lax.broadcasted_iota(jnp.int32, (128, 128), 1) < 64

    def split_heads(values):
        zero = jnp.zeros_like(values)
        return jnp.concatenate(
            [jnp.where(first_head, values, zero), jnp.where(first_head, zero, values)], axis=0
        )

    def join_heads(values):
        return jnp.where(first_head, values[:128], values[128:])

    def project(m):
        def step(i, carry):
            rows = span(m * 512 + i * 256, 256)
            raw = dot(n1[rows, :], w0[:, 0:768])
            front, cosine, sine = expand(rows, 256)
            for b in range(4):
                part = raw[:, 128 * b : 128 * b + 128]
                qkv[rows, 128 * b : 128 * b + 128] = (
                    part * cosine + swap(part, front) * sine
                ).astype(BF)
            qkv[rows, 512:768] = raw[:, 512:768].astype(BF)
            return carry

        lax.fori_loop(0, 2, step, 0)

    def block_rows(m, s):
        return span(m * 512 + (s % 2) * 256 + (s // 2) * 128, 128)

    def pair(b, p):
        return slice(256 * b + 128 * p, 256 * b + 128 * p + 128)

    def attend(m):
        def step(s, carry):
            rows = block_rows(m, s)
            before = block_rows(m, jnp.maximum(s - 1, 0))
            r = lax.broadcasted_iota(jnp.int32, (128, 256), 0)
            k = lax.broadcasted_iota(jnp.int32, (128, 256), 1)
            back = r + 128 - k
            places = pos[rows, :]
            limit = jnp.minimum(jnp.concatenate([places, places], axis=1).astype(jnp.int32), 127)
            limit = jnp.minimum(limit, s * 128 + r)
            allowed = (back >= 0) & (back <= limit)
            allowed = jnp.concatenate([allowed, allowed], axis=0)
            for p in range(2):
                query = split_heads(qkv[rows, pair(0, p)])
                keys = jnp.concatenate([qkv[before, pair(1, p)], qkv[rows, pair(1, p)]], axis=0)
                held = jnp.concatenate([qkv[before, pair(2, p)], qkv[rows, pair(2, p)]], axis=0)
                scores = dot_rows(query, keys) * (HD ** -0.5)
                scores = jnp.where(allowed, scores, NEGATIVE)
                top = jnp.max(scores, axis=-1, keepdims=True)
                exponent = jnp.exp(scores - top)
                total = jnp.sum(exponent, axis=-1, keepdims=True)
                share = (exponent / total).astype(BF)
                probs[(m * 4 + s) * 2 + p] = share
                att[rows, pair(0, p)] = join_heads(dot(share, held)).astype(BF)
            return carry

        lax.fori_loop(0, 4, step, 0)

    def row_send(e, m):
        return copy(
            send_a0.at[m, span((1 - y) * 128, 128), :], recv_d0.at[m], ra_ss.at[e, m, 1],
            ra_rs.at[e, m, 1], beside,
        )

    def row_scatter(e, m, compute):
        hand = copy(send_b.at[m], recv_c0.at[m], ra_ss.at[e, m, 0], ra_rs.at[e, m, 0], sibling)

        def step(j, carry):
            part = compute(pl.multiple_of(m * 512 + ((c + 1 + j) % 2) * 256, 256))

            @pl.when(j == 0)
            def _():
                send_b[m] = part.astype(BF)
                hand.start()

            @pl.when(j == 1)
            def _():
                hand.wait_recv()
                send_a0[m] = (part + recv_c0[m].astype(F32)).astype(BF)
                row_send(e, m).start()

            return carry

        lax.fori_loop(0, 2, step, 0)
        hand.wait_send()

    def row_scatter_end(e, m):
        row_send(e, m).wait()
        return send_a0[m, span(y * 128, 128), :].astype(F32) + recv_d0[m].astype(F32)

    def scatter(e, m, compute):
        def step(j, carry):
            cc = (c + 1 + j // 2) % 2
            xx = (xi + 1 + j % 2) % 2
            part = compute(pl.multiple_of(m * 1024 + cc * 512 + xx * 256, 256))
            there = span(xx * 256, 256)

            @pl.when(j < 2)
            def _():
                send_b[j] = part.astype(BF)
                copy(
                    send_b.at[j], recv_c.at[e, m, there, :], rs_ss.at[e, m, j], rs_rs.at[e, m, j],
                    sibling,
                ).start()

            @pl.when(j >= 2)
            def _():
                copy(
                    send_b.at[j - 2], recv_c.at[e, m, there, :], rs_ss.at[e, m, j - 2],
                    rs_rs.at[e, m, j - 2], sibling,
                ).wait_recv()
                send_a[m, there, :] = (
                    part + recv_c[e, m, there, :].astype(F32)
                ).astype(BF)

            @pl.when(j == 2)
            def _():
                scatter_send(e, m, 2).start()
                if LEG[e] != 1:
                    scatter_send(e, m, 0).start()

            @pl.when(j == 3)
            def _():
                if LEG[e] != 0:
                    scatter_send(e, m, 1).start()

            return carry

        lax.fori_loop(0, 4, step, 0)
        for j in range(2):
            copy(
                send_b.at[j], recv_c.at[e, m, pl.ds(0, 256), :], rs_ss.at[e, m, j],
                rs_rs.at[e, m, j], sibling,
            ).wait_send()

    def scatter_send(e, m, r):
        rows = span(chips[r] * 128, 128)
        return copy(
            send_a.at[m, rows, :], recv_d.at[e, m, r], rs_ss.at[e, m, 2 + r],
            rs_rs.at[e, m, 2 + r], teams[r if r < 2 or LEG[e] is None else LEG[e]][0],
        )

    def scatter_pass(e, m):
        r = 1 - LEG[e]
        rows = span(chips[r] * 128, 128)
        scatter_send(e, m, 2).wait_recv()
        send_a[m, rows, :] = (
            send_a[m, rows, :].astype(F32) + recv_d[e, m, 2].astype(F32)
        ).astype(BF)
        scatter_send(e, m, r).start()

    def scatter_end(e, m):
        direct = LEG[e] is None
        for r in range(3):
            if r < 2 or direct:
                scatter_send(e, m, r).wait()
            else:
                scatter_send(e, m, r).wait_send()
        total = send_a[m, span(chip * 128, 128), :].astype(F32)
        for r in range(3 if direct else 2):
            total = total + recv_d[e, m, r].astype(F32)
        return total

    def outwards(row):
        return dot(att[pl.ds(row, 256), :], outw[...])

    row_end(n1, 0, 0)
    project(0)
    slab_pass(1)
    attend(0)
    slab_in(1)
    for i, k in enumerate(ROW_TEAM):
        device, g = teams[k]
        begin(
            copy(
                w0.at[span((g % 4) * 256, 256), pl.ds(768, 256)],
                outw.at[:, span(sq * 256, 256)], o_ss.at[i], o_rs.at[i], device,
            )
        )
    outw[:, span(sq * 256, 256)] = w0[span(sq * 256, 256), 768:1024]
    row_end(n1, 0, 1)
    project(1)
    for i, k in enumerate(ROW_TEAM):
        device, g = teams[k]
        copy(
            w0.at[span((g % 4) * 256, 256), pl.ds(768, 256)],
            outw.at[:, span((g % 4) * 256, 256)], o_ss.at[i], o_rs.at[i], device,
        ).wait_recv()
    row_scatter(0, 0, outwards)
    gather_start(db, 0, 1)
    weights_up(1)
    attend(1)
    row_scatter(0, 1, outwards)

    def second_norm(m):
        total = row_scatter_end(0, m)
        attn[m] = total
        middle = x_ref[m].astype(F32) + vector(4) * total
        mid[m] = middle
        unit, _ = unit_of(middle)
        n2[slot_rows(m, c, chip), :] = (unit * vector(2) + vector(3)).astype(BF)

    gather_far(db, 0, 0)
    second_norm(0)
    gather_start(n2, 1, 0)
    gather_pass(db, 0, 1, 0)
    weights_pass(0)
    second_norm(1)
    gather_start(n2, 1, 1)
    gather_pass(n2, 1, 0, 0)
    gather_far(db, 0, 1)
    gather_far(n2, 1, 0)
    gather_pass(n2, 1, 1, 1)
    weights_pass(1)

    def mlp(row):
        rows = pl.ds(row, 256)
        both = dot(n2[rows, :], w1[...])
        d_hidden = dot(db[rows, :], w2[...])
        gate, up = both[:, :512], both[:, 512:]
        sig = sigmoid(gate)
        silu = gate * sig
        hid[rows, :] = (silu * up).astype(BF)
        dgu[rows, 0:512] = (d_hidden * up * sig * (1.0 + gate * (1.0 - sig))).astype(BF)
        dgu[rows, 512:1024] = (d_hidden * silu).astype(BF)
        return dot_rows(dgu[rows, :], w1[...])

    weights_in(0)
    weights_in(1)
    gather_end(db, 0, 0)
    gather_end(n2, 1, 0)
    scatter(0, 0, mlp)
    gather_far(n2, 1, 1)
    gather_end(db, 0, 1)
    gather_end(n2, 1, 1)
    scatter(0, 1, mlp)

    turned = (z == 0) | (z == 2)
    at_end = (z == 0) | (z == 3)

    def target(i):
        inner = jnp.where(i == 3, 1, jnp.where(i == 0, 0, i + 1))
        plain = jnp.where(at_end, i, inner)
        return jnp.where(turned, 3 - plain, plain)

    def descend(n, i, stage, arrive, relay):
        zz = target(i)

        @pl.when(at_end & (i == 0))
        def _():
            via = jnp.where(z == 0, 1, 2)
            copy(stage.at[i], relay, z_ss.at[n, i], z_rs.at[n, 3], (via * 2 + xi, sq)).start()

        @pl.when(jnp.logical_not(at_end & (i == 0)) & (at_end | (i < 2)))
        def _():
            slot = (zz + 3 - z) % 4
            copy(
                stage.at[i], arrive.at[slot], z_ss.at[n, i], z_rs.at[n, slot], (zz * 2 + xi, sq)
            ).start()

    def descend_pass(n, stage, arrive, relay):
        @pl.when(passes)
        def _():
            zz = target(2)
            slot = (zz + 3 - z) % 4
            copy(stage.at[2], relay, z_ss.at[n, 2], z_rs.at[n, 3], levels[0][0]).wait_recv()
            stage[2] = (stage[2].astype(F32) + relay[...].astype(F32)).astype(BF)
            copy(
                stage.at[2], arrive.at[slot], z_ss.at[n, 2], z_rs.at[n, slot], (zz * 2 + xi, sq)
            ).start()

    def weight_grad(n, left, right, stage, own, arrive, relay):
        def step(i, carry):
            part = dot_cols(left[:, span(target(i) * 256, 256)], right[...])

            @pl.when(i < 3)
            def _():
                stage[i] = part.astype(BF)
                descend(n, i, stage, arrive, relay)

            @pl.when(i == 3)
            def _():
                own[...] = part.astype(own.dtype)

            return carry

        lax.fori_loop(0, 4, step, 0)

    weight_grad(0, n2, dgu, stage_g, own_g, zg_ref, relay_g)

    def norm_back(grad, values, gain, row):
        unit, inverse = unit_of(values)
        gacc[row : row + 1, :] += jnp.sum(grad * unit, axis=0, keepdims=True)
        gacc[row + 1 : row + 2, :] += jnp.sum(grad, axis=0, keepdims=True)
        scaled = grad * gain
        return inverse * (
            scaled
            - jnp.mean(scaled, axis=-1, keepdims=True)
            - unit * jnp.mean(scaled * unit, axis=-1, keepdims=True)
        )

    def second_norm_back(m):
        grad = scatter_end(0, m)
        d_mid = g_ref[m].astype(F32) + norm_back(grad, mid[m], vector(2), 2)
        gacc[4:5, :] += jnp.sum(d_mid * attn[m], axis=0, keepdims=True)
        attn[m] = d_mid
        da[row_rows(m, c, y), :] = (vector(4) * d_mid).astype(BF)
        row_start(da, 1, m)

    second_norm_back(0)
    weight_grad(1, db, hid, stage_d, own_d, zd_ref, relay_d)

    def downwards(row):
        return dot_rows(hid[pl.ds(row, 256), :], w2[...])

    def attend_back(m):
        def step(s, carry):
            rows = block_rows(m, s)
            before = block_rows(m, jnp.maximum(s - 1, 0))
            d_att = dot_rows(da[rows, :], outw[...]).astype(BF)
            here = span(s * 128, 128)
            prior = span(jnp.maximum(s - 1, 0) * 128, 128)
            for p in range(2):
                d_heads = split_heads(d_att[:, 128 * p : 128 * p + 128])
                query = split_heads(qkv[rows, pair(0, p)])
                keys = jnp.concatenate([qkv[before, pair(1, p)], qkv[rows, pair(1, p)]], axis=0)
                held = jnp.concatenate([qkv[before, pair(2, p)], qkv[rows, pair(2, p)]], axis=0)
                share = probs[(m * 4 + s) * 2 + p]
                weights = share.astype(F32)
                d_probs = dot_rows(d_heads, held)
                inner = jnp.sum(weights * d_probs, axis=-1, keepdims=True)
                d_scores = (weights * (d_probs - inner) * (HD ** -0.5)).astype(BF)
                dqs[here, pair(0, p)] = join_heads(dot(d_scores, keys))
                d_keys = dot_cols(d_scores, query)
                d_held = dot_cols(share, d_heads)
                dkv[prior, pair(0, p)] += d_keys[:128]
                dkv[prior, pair(1, p)] += d_held[:128]
                dkv[here, pair(0, p)] = d_keys[128:]
                dkv[here, pair(1, p)] = d_held[128:]
            return carry

        lax.fori_loop(0, 4, step, 0)

        def finish(s, carry):
            rows = block_rows(m, s)
            here = span(s * 128, 128)
            front, cosine, sine = expand(rows, 128)
            for b in range(4):
                part = dqs[here, 128 * b : 128 * b + 128] if b < 2 else dkv[here, pair(0, b - 2)]
                qkv[rows, 128 * b : 128 * b + 128] = (
                    part * cosine - swap(part, front) * sine
                ).astype(BF)
            qkv[rows, 512:768] = dkv[here, 256:512].astype(BF)
            return carry

        lax.fori_loop(0, 4, finish, 0)

    def inwards(row):
        return dot_rows(qkv[pl.ds(row, 256), :], w0[:, 0:768])

    dkv[...] = jnp.zeros_like(dkv)
    scatter(1, 0, downwards)
    row_pass(da, 1, 0)
    second_norm_back(1)
    row_end(da, 1, 0)
    attend_back(0)
    row_scatter(1, 0, inwards)
    scatter_pass(1, 0)
    descend_pass(0, stage_g, zg_ref, relay_g)
    scatter(1, 1, downwards)
    row_pass(da, 1, 1)
    row_end(da, 1, 1)
    part = dot_cols(att[...], da[...])
    for u in range(4):
        gsend[u] = part[:, 256 * u : 256 * u + 256].astype(BF)
    gout[span(sq * 256, 256), :] = gsend[sq]
    for i, k in enumerate(ROW_TEAM):
        device, g = teams[k]
        begin(
            copy(gsend.at[g % 4], gout.at[span(sq * 256, 256), :], go_ss.at[i], go_rs.at[i], device)
        )

    attend_back(1)
    row_scatter(1, 1, inwards)
    def mine_of(values):
        return jnp.where(xi == 0, values[:128], values[128:])

    def other_of(values):
        return jnp.where(xi == 0, values[128:], values[:128])

    for i, k in enumerate(ROW_TEAM):
        device, g = teams[k]
        theirs = span((g % 4) * 256, 256)
        copy(gsend.at[g % 4], gout.at[theirs, :], go_ss.at[i], go_rs.at[i], device).wait_recv()
    for j in range(4):
        zz = target(j)
        begin(
            copy(
                gout.at[span((zz * 2 + 1 - xi) * 128, 128), :], side_o.at[j], sx_ss.at[1, j],
                sx_rs.at[1, j], across,
            )
        )

    def qkv_grad(j, carry):
        part = dot_cols(n1[:, span(target(j) * 256, 256)], qkv[...])
        send_q[j] = other_of(part).astype(BF)
        copy(send_q.at[j], side_q.at[j], sx_ss.at[0, j], sx_rs.at[0, j], across).start()
        keep_q[j] = mine_of(part).astype(BF)
        return carry

    lax.fori_loop(0, 4, qkv_grad, 0)


    def summed(n, i, mine, side, stage, own, arrive, relay):
        copy(side.at[i], side.at[i], sx_ss.at[n, i], sx_rs.at[n, i], across).wait_recv()
        total = mine + side[i].astype(F32)
        if i < 3:
            stage[i] = total.astype(BF)
            descend(2 + n, i, stage, arrive, relay)
        else:
            own[...] = total

    def sum_q(i):
        summed(0, i, keep_q[i].astype(F32), side_q, stage_q, own_q, zq_ref, relay_q)

    def sum_o(i):
        part = gout[span((target(i) * 2 + xi) * 128, 128), :].astype(F32)
        summed(1, i, part, side_o, stage_o, own_o, zo_ref, relay_o)

    def summed_levels(n, stage, own, arrive):
        for i in range(3):
            copy(stage.at[i], arrive.at[i], z_ss.at[n, i], z_rs.at[n, i], levels[0][0]).wait_send()
        loads = [pltpu.make_async_copy(arrive.at[j], stage.at[j], loc_sem.at[j]) for j in range(3)]
        absent = [z == 0, None, z == 3]
        for j in range(3):
            def load(j=j):
                copy(
                    stage.at[j], arrive.at[j], z_ss.at[n, j], z_rs.at[n, j], levels[0][0]
                ).wait_recv()
                loads[j].start()

            def clear(j=j):
                stage[j] = jnp.zeros(stage.shape[1:], BF)

            if absent[j] is None:
                load()
            else:
                pl.when(jnp.logical_not(absent[j]))(load)
                pl.when(absent[j])(clear)
        for j in range(3):
            if absent[j] is None:
                loads[j].wait()
            else:
                pl.when(jnp.logical_not(absent[j]))(loads[j].wait)
        total = own[...].astype(F32)
        for j in range(3):
            total = total + stage[j].astype(F32)
        return total.astype(BF)

    def last_copies(n, pack, first, width, fin, people, who):
        found = []
        for i, k in enumerate(people):
            device, g = teams[k]
            found.append(
                copy(
                    pack.at[span((g % who) * 32, 32), pl.ds(first, width)],
                    fin.at[me % who, :, pl.ds(first, width)], f_ss.at[n, i], f_rs.at[n, i], device,
                )
            )
        return found

    def finals(n, first, width, stage, own, arrive, pack, fin, people, who):
        pack[:, first : first + width] = summed_levels(n, stage, own, arrive)
        stay = pltpu.make_async_copy(
            pack.at[span((me % who) * 32, 32), pl.ds(first, width)],
            fin.at[me % who, :, pl.ds(first, width)], loc_sem.at[3],
        )
        stay.start()
        for item in last_copies(n, pack, first, width, fin, people, who):
            item.start()
        stay.wait()

    plans = [
        (0, 0, 1024, stage_g, own_g, zg_ref, pack_m, fin_m, range(7), 8),
        (1, 1024, 512, stage_d, own_d, zd_ref, pack_m, fin_m, range(7), 8),
        (3, 768, 256, stage_o, own_o, zo_ref, pack_a, fin_a, ROW_TEAM, 4),
        (2, 0, 768, stage_q, own_q, zq_ref, pack_a, fin_a, ROW_TEAM, 4),
    ]
    def first_norm_back(m):
        grad = row_scatter_end(1, m)
        back = norm_back(grad, x_ref[m].astype(F32), vector(0), 0)
        dx_ref[m] = (attn[m] + back).astype(BF)

    def result(m):
        branch = scatter_end(1, m)
        gacc[5:6, :] += jnp.sum(g_ref[m].astype(F32) * branch, axis=0, keepdims=True)
        y_ref[m] = (mid[m] + vector(5) * branch).astype(BF)

    for i in range(4):
        sum_o(i)
    descend_pass(1, stage_d, zd_ref, relay_d)
    sum_q(0)
    scatter_pass(1, 1)
    sum_q(1)
    first_norm_back(0)
    sum_q(2)
    descend_pass(3, stage_o, zo_ref, relay_o)
    first_norm_back(1)
    sum_q(3)
    result(0)
    result(1)
    for k in range(8):
        gv_send[k] = gacc[:, 128 * k : 128 * k + 128]
    for k, (device, g) in enumerate(teams):
        begin(copy(gv_send.at[g], gv_in.at[k], gv_ss.at[k], gv_rs.at[k], device))

    descend_pass(2, stage_q, zq_ref, relay_q)
    for item in pack_sends:
        item.wait_send()
    finals(*plans[0])
    for item in pending:
        if isinstance(item, tuple):
            pl.when(jnp.logical_not(item[0]))(item[1].wait_send)
        else:
            item.wait_send()
    for j in range(4):
        copy(send_q.at[j], side_q.at[j], sx_ss.at[0, j], sx_rs.at[0, j], across).wait_send()
    for k, (device, g) in enumerate(teams):
        copy(gv_send.at[g], gv_in.at[k], gv_ss.at[k], gv_rs.at[k], device).wait_recv()
    total = gv_send[me]
    for k in range(7):
        total = total + gv_in[k]
    gv_z[0] = total
    level_sends = []
    for j, (device, _) in enumerate(levels):
        item = copy(gv_z.at[0], gv_z.at[1 + j], gv_ss.at[7 + j], gv_rs.at[7 + j], device)
        item.start()
        level_sends.append(item)
    finals(*plans[1])
    for item in level_sends:
        item.wait()
    gv_all[me] = gv_z[0] + gv_z[1] + gv_z[2] + gv_z[3]
    for k, (device, g) in enumerate(teams):
        copy(gv_all.at[me], gv_all.at[me], gv_ss.at[10 + k], gv_rs.at[10 + k], device).start()
    finals(*plans[2])
    finals(*plans[3])
    for k, (device, g) in enumerate(teams):
        copy(gv_all.at[g], gv_all.at[g], gv_ss.at[10 + k], gv_rs.at[10 + k], device).wait()
    vg_ref[...] = gv_all[z * 2 + me // 4]
    for n, first, width, _, _, _, pack, fin, people, who in plans:
        for item in last_copies(n, pack, first, width, fin, people, who):
            item.wait()


def layer_fast(
    block_input,
    positions,
    out_grad,
    qkv_weight,
    out_weight,
    gate_weight,
    up_weight,
    down_weight,
    norm1_gain,
    norm1_shift,
    norm2_gain,
    norm2_shift,
    attn_scale,
    mlp_scale,
):
    vectors = jnp.stack(
        [norm1_gain, norm1_shift, norm2_gain, norm2_shift, attn_scale, mlp_scale]
    ).astype(F32)
    packed = jnp.concatenate([jnp.tile(vectors, (1, 4)), positions.astype(F32)], axis=0)
    vmem, anywhere = pl.BlockSpec(memory_space=pltpu.VMEM), pl.BlockSpec(memory_space=pl.ANY)
    dma = pltpu.SemaphoreType.DMA
    scratch = [
        pltpu.VMEM((4, 8, 8, 128), F32), pltpu.VMEM((8, 1024), F32), pltpu.VMEM((8, 1024), F32),
        pltpu.VMEM((7, 8, 128), F32), pltpu.VMEM((4, 8, 128), F32), pltpu.VMEM((8, 8, 128), F32),
        pltpu.VMEM((8, 8, 128), F32),
        pltpu.VMEM((128, 1024), BF), pltpu.VMEM((256, 1536), BF), pltpu.VMEM((1024, 1024), BF),
        pltpu.VMEM((1024, 1024), BF), pltpu.VMEM((1024, 512), BF), pltpu.VMEM((256, 1024), BF),
        pltpu.VMEM((1024, 1024), BF), pltpu.VMEM((2048, 1024), BF), pltpu.VMEM((2048, 1024), BF),
        pltpu.VMEM((1024, 1024), BF),
        pltpu.VMEM((1024, 768), BF), pltpu.VMEM((1024, 256), BF), pltpu.VMEM((16, 256, 256), BF),
        pltpu.VMEM((512, 256), F32), pltpu.VMEM((512, 512), F32),
        pltpu.VMEM((2048, 512), BF), pltpu.VMEM((2048, 1024), BF),
        pltpu.VMEM((2, 512, 1024), BF), pltpu.VMEM((2, 2, 512, 1024), BF),
        pltpu.VMEM((2, 2, 3, 128, 1024), BF), pltpu.VMEM((2, 256, 1024), BF),
        pltpu.VMEM((2, 256, 1024), BF), pltpu.VMEM((2, 256, 1024), BF),
        pltpu.VMEM((2, 128, 1024), BF),
        pltpu.VMEM((3, 128, 768), BF), pltpu.VMEM((3, 128, 256), BF),
        pltpu.VMEM((3, 256, 1024), BF), pltpu.VMEM((3, 256, 512), BF),
        pltpu.VMEM((128, 768), F32), pltpu.VMEM((128, 256), F32),
        pltpu.VMEM((256, 1024), BF), pltpu.VMEM((256, 512), BF),
        pltpu.VMEM((1024, 256), BF), pltpu.VMEM((4, 256, 256), BF),
        pltpu.VMEM((4, 128, 768), BF), pltpu.VMEM((4, 128, 256), BF),
        pltpu.VMEM((4, 128, 768), BF), pltpu.VMEM((4, 128, 768), BF),
        pltpu.VMEM((256, 1024), BF), pltpu.VMEM((256, 512), BF), pltpu.VMEM((128, 768), BF),
        pltpu.VMEM((128, 256), BF),
        pltpu.VMEM((2, 128, 1024), F32), pltpu.VMEM((2, 128, 1024), F32),
        pltpu.VMEM((1024, 128), F32), pltpu.VMEM((1024, 128), F32),
        dma((10,)), dma((10,)), dma((3,)), dma((3,)), dma((2, 8)), dma((2, 8)), dma((2, 11)), dma((2, 11)),
        dma((3,)), dma((3,)), dma((2, 2, 3)), dma((2, 2, 3)), dma((2, 2, 7)), dma((2, 2, 7)),
        dma((2, 2, 2)), dma((2, 2, 2)), dma((2, 2, 5)), dma((2, 2, 5)), dma((3,)), dma((3,)),
        dma((2, 4)), dma((2, 4)), dma((4, 4)), dma((4, 4)), dma((4, 7)), dma((4, 7)),
        dma((17,)), dma((17,)), dma((4,)),
    ]
    y, dx, vg, fin_a, fin_m = pl.pallas_call(
        layer_kernel,
        out_shape=(
            jax.ShapeDtypeStruct((2, 128, 1024), BF),
            jax.ShapeDtypeStruct((2, 128, 1024), BF),
            jax.ShapeDtypeStruct((8, 128), F32),
            jax.ShapeDtypeStruct((4, 32, 1024), BF),
            jax.ShapeDtypeStruct((8, 32, 1536), BF),
            jax.ShapeDtypeStruct((3, 128, 768), BF),
            jax.ShapeDtypeStruct((3, 128, 256), BF),
            jax.ShapeDtypeStruct((3, 256, 1024), BF),
            jax.ShapeDtypeStruct((3, 256, 512), BF),
        ),
        in_specs=[vmem] * 9,
        out_specs=(vmem, vmem, vmem) + (anywhere,) * 6,
        scratch_shapes=scratch,
        compiler_params=pltpu.CompilerParams(
            collective_id=0, has_side_effects=True, vmem_limit_bytes=VMEM_BYTES
        ),
        cost_estimate=pl.CostEstimate(
            flops=26_000_000_000, bytes_accessed=8_000_000, transcendentals=4_000_000
        ),
        name="layer",
    )(
        block_input, out_grad, packed, jnp.asarray(trig_table()), qkv_weight, out_weight,
        gate_weight, up_weight, down_weight.T,
    )[:5]
    fin_a, fin_m = fin_a.astype(F32), fin_m.astype(F32)
    grad_qkv = (
        fin_a[:, :, 0:768].reshape(4, 32, 3, 256).transpose(1, 2, 0, 3).reshape(32, 3072)
    )
    grad_out = fin_a[:, :, 768:1024].transpose(1, 0, 2).reshape(32, 1024)
    grad_gate = fin_m[:, :, 0:512].transpose(1, 0, 2).reshape(32, 4096)
    grad_up = fin_m[:, :, 512:1024].transpose(1, 0, 2).reshape(32, 4096)
    grad_down = fin_m[:, :, 1024:1536].transpose(0, 2, 1).reshape(4096, 32)
    part = lax.axis_index(("dp", "seq")) % 4
    vg = lax.dynamic_index_in_dim(vg.reshape(8, 4, 32), part, 1, keepdims=False)
    return (y, dx, grad_qkv, grad_out, grad_gate, grad_up, grad_down) + tuple(
        vg[i] for i in range(6)
    )


def fits(mesh):
    return mesh.shape["dp"] == 8 and mesh.shape["seq"] == 4


def solution(mesh):
    return jax.shard_map(
        layer_fast if fits(mesh) else body,
        mesh=mesh,
        in_specs=(
            P(None, ("dp", "seq"), None),
            P(None, ("dp", "seq")),
            P(None, ("dp", "seq"), None),
            P(("dp", "seq"), None),
            P(("dp", "seq"), None),
            P(("dp", "seq"), None),
            P(("dp", "seq"), None),
            P(None, ("dp", "seq")),
            P(("dp", "seq")),
            P(("dp", "seq")),
            P(("dp", "seq")),
            P(("dp", "seq")),
            P(("dp", "seq")),
            P(("dp", "seq")),
        ),
        out_specs=(
            P(None, ("dp", "seq"), None),
            P(None, ("dp", "seq"), None),
            P(("dp", "seq"), None),
            P(("dp", "seq"), None),
            P(("dp", "seq"), None),
            P(("dp", "seq"), None),
            P(None, ("dp", "seq")),
            P(("dp", "seq")),
            P(("dp", "seq")),
            P(("dp", "seq")),
            P(("dp", "seq")),
            P(("dp", "seq")),
            P(("dp", "seq")),
        ),
        check_vma=False,
    )
```

```python
import jax
import jax.numpy as jnp
import ml_dtypes
import numpy as np
from jax import lax
from jax.experimental import pallas as pl
from jax.experimental.pallas import tpu as pltpu
from jax.sharding import PartitionSpec as P

H = 16
HD = 64
WINDOW = 128


EPSILON = 1e-05
NEGATIVE = -1e30


def normalize(values, gain, shift):
    center = values - jnp.mean(values, axis=-1, keepdims=True)
    inverse = lax.rsqrt(jnp.mean(center * center, axis=-1, keepdims=True) + EPSILON)
    unit = center * inverse
    return (unit * gain + shift, unit, inverse)


def normalize_back(incoming, unit, inverse, gain):
    scaled = incoming * gain
    middle = (
        scaled
        - jnp.mean(scaled, axis=-1, keepdims=True)
        - unit * jnp.mean(scaled * unit, axis=-1, keepdims=True)
    )
    return (inverse * middle, jnp.sum(incoming * unit, axis=0), jnp.sum(incoming, axis=0))


def angles_of(places, size):
    inverse = 10000.0 ** (-(jnp.arange(size // 2, dtype=jnp.float32) * (2.0 / size)))
    return places.astype(jnp.float32)[:, None] * inverse[None, :]


def rotate(values, angles):
    half = values.shape[-1] // 2
    cosine = jnp.cos(angles)[:, None, :]
    sine = jnp.sin(angles)[:, None, :]
    first_half = values[..., :half]
    second_half = values[..., half:]
    return jnp.concatenate(
        [first_half * cosine - second_half * sine, second_half * cosine + first_half * sine],
        axis=-1,
    )


def unrotate(values, angles):
    half = values.shape[-1] // 2
    cosine = jnp.cos(angles)[:, None, :]
    sine = jnp.sin(angles)[:, None, :]
    first_half = values[..., :half]
    second_half = values[..., half:]
    return jnp.concatenate(
        [first_half * cosine + second_half * sine, second_half * cosine - first_half * sine],
        axis=-1,
    )


def pack_shards(shards):
    return jnp.concatenate([item.reshape(1, -1) for item in shards], axis=1)


def unpack_gathered(whole, shards):
    devices = whole.shape[0]
    result = []
    offset = 0
    for number, item in enumerate(shards):
        count = item.size
        piece = whole[:, offset : offset + count]
        offset = offset + count
        if number == 4:
            rows, cols = item.shape
            result.append(
                piece.reshape(devices, rows, cols).transpose(1, 0, 2).reshape(rows, devices * cols)
            )
        elif item.ndim == 2:
            result.append(piece.reshape(devices * item.shape[0], item.shape[1]))
        else:
            result.append(piece.reshape(-1))
    return tuple(result)


def pack_grads(totals, devices):
    pieces = []
    for number, item in enumerate(totals):
        if number == 4:
            rows, cols = item.shape
            pieces.append(
                item.reshape(rows, devices, cols // devices).transpose(1, 0, 2).reshape(devices, -1)
            )
        else:
            pieces.append(item.reshape(devices, -1))
    return jnp.concatenate(pieces, axis=1)


def unpack_summed(summed, shards):
    flat = summed.reshape(-1)
    result = []
    offset = 0
    for item in shards:
        count = item.size
        result.append(flat[offset : offset + count].reshape(item.shape))
        offset = offset + count
    return tuple(result)


def block_scores(query, keys_padded, values_padded, starts, first, size):
    block_query = lax.dynamic_slice_in_dim(query, first, size, 0)
    block_keys = lax.dynamic_slice_in_dim(keys_padded, first, size + WINDOW, 0)
    block_values = lax.dynamic_slice_in_dim(values_padded, first, size + WINDOW, 0)
    begin = lax.dynamic_slice_in_dim(starts, first, size, 0)
    here = first + jnp.arange(size, dtype=jnp.int32)
    there = first - WINDOW + jnp.arange(size + WINDOW, dtype=jnp.int32)
    allowed = (
        (there[None, :] >= begin[:, None])
        & (there[None, :] <= here[:, None])
        & (here[:, None] - there[None, :] < WINDOW)
    )
    raw = jnp.einsum("qhd,khd->hqk", block_query, block_keys, preferred_element_type=jnp.float32)
    scores = jnp.where(allowed[None], raw * HD ** (-0.5), NEGATIVE)
    return (scores, block_query, block_keys, block_values)


def attend_forward(query, keys_padded, values_padded, starts):
    length = query.shape[0]
    size = min(512, length)
    count = length // size

    def step(carry, index):
        scores, block_query, block_keys, block_values = block_scores(
            query, keys_padded, values_padded, starts, index * size, size
        )
        top = jnp.max(scores, axis=-1, keepdims=True)
        exponent = jnp.exp(scores - top)
        total = jnp.sum(exponent, axis=-1, keepdims=True)
        probs = (exponent / total).astype(jnp.bfloat16)
        outcome = jnp.einsum(
            "hqk,khd->qhd", probs, block_values, preferred_element_type=jnp.float32
        )
        return (carry, (outcome, (top + jnp.log(total))[..., 0]))

    unused, (outcomes, logs) = lax.scan(step, 0, jnp.arange(count, dtype=jnp.int32))
    return (outcomes.reshape(query.shape), logs)


def attend_backward(query, keys_padded, values_padded, starts, logs, grad_out):
    length = query.shape[0]
    size = min(512, length)
    count = length // size

    def step(carry, index):
        grad_query, grad_keys, grad_values = carry
        first = index * size
        scores, block_query, block_keys, block_values = block_scores(
            query, keys_padded, values_padded, starts, first, size
        )
        probs = jnp.exp(scores - logs[index][..., None])
        grad_block = lax.dynamic_slice_in_dim(grad_out, first, size, 0)
        grad_probs = jnp.einsum(
            "qhd,khd->hqk", grad_block, block_values, preferred_element_type=jnp.float32
        )
        inner = jnp.sum(probs * grad_probs, axis=-1, keepdims=True)
        grad_scores = (probs * (grad_probs - inner) * HD ** (-0.5)).astype(jnp.bfloat16)
        query_part = jnp.einsum(
            "hqk,khd->qhd", grad_scores, block_keys, preferred_element_type=jnp.float32
        )
        keys_part = jnp.einsum(
            "hqk,qhd->khd", grad_scores, block_query, preferred_element_type=jnp.float32
        )
        values_part = jnp.einsum(
            "hqk,qhd->khd",
            probs.astype(jnp.bfloat16),
            grad_block,
            preferred_element_type=jnp.float32,
        )
        grad_query = lax.dynamic_update_slice_in_dim(grad_query, query_part, first, 0)
        grad_keys = lax.dynamic_update_slice_in_dim(
            grad_keys,
            lax.dynamic_slice_in_dim(grad_keys, first, size + WINDOW, 0) + keys_part,
            first,
            0,
        )
        grad_values = lax.dynamic_update_slice_in_dim(
            grad_values,
            lax.dynamic_slice_in_dim(grad_values, first, size + WINDOW, 0) + values_part,
            first,
            0,
        )
        return ((grad_query, grad_keys, grad_values), None)

    start_state = (
        jnp.zeros(query.shape, jnp.float32),
        jnp.zeros(keys_padded.shape, jnp.float32),
        jnp.zeros(values_padded.shape, jnp.float32),
    )
    (grad_query, grad_keys, grad_values), unused = lax.scan(
        step, start_state, jnp.arange(count, dtype=jnp.int32)
    )
    return (grad_query, grad_keys, grad_values)


def attention_forward(query, keyset, valueset, places):
    rows, heads, depth = query.shape
    width = heads * depth
    parts = lax.axis_size("seq")
    slab = width // parts
    local = slab // depth
    packed = jnp.stack(
        [query.reshape(rows, width), keyset.reshape(rows, width), valueset], axis=1
    ).reshape(rows, 3, parts, slab)
    moved = lax.all_to_all(packed, "seq", split_axis=2, concat_axis=0, tiled=True)
    group = moved.shape[0]
    every = lax.all_gather(places, "seq", axis=0, tiled=True)
    starts = jnp.maximum(jnp.arange(group, dtype=jnp.int32) - every, 0)
    padding = jnp.zeros((WINDOW, local, depth), jnp.bfloat16)
    head_query = moved[:, 0, 0].reshape(group, local, depth)
    keys_padded = jnp.concatenate([padding, moved[:, 1, 0].reshape(group, local, depth)], axis=0)
    values_padded = jnp.concatenate([padding, moved[:, 2, 0].reshape(group, local, depth)], axis=0)
    outcome, logs = attend_forward(head_query, keys_padded, values_padded, starts)
    sent = outcome.astype(jnp.bfloat16).reshape(group, 1, slab)
    attended = lax.all_to_all(sent, "seq", split_axis=0, concat_axis=1, tiled=True).reshape(
        rows, width
    )
    return (attended, (head_query, keys_padded, values_padded, starts, logs))


def attention_backward(kept, grad_attended, rows, width):
    head_query, keys_padded, values_padded, starts, logs = kept
    depth = head_query.shape[-1]
    parts = lax.axis_size("seq")
    slab = width // parts
    local = slab // depth
    came = lax.all_to_all(
        grad_attended.reshape(rows, parts, slab), "seq", split_axis=1, concat_axis=0, tiled=True
    )
    group = came.shape[0]
    grad_out = came.reshape(group, local, depth)
    grad_query, grad_keys, grad_values = attend_backward(
        head_query, keys_padded, values_padded, starts, logs, grad_out
    )
    packed = (
        jnp.stack([grad_query, grad_keys[WINDOW:], grad_values[WINDOW:]], axis=1)
        .astype(jnp.bfloat16)
        .reshape(group, 3, 1, slab)
    )
    back = lax.all_to_all(packed, "seq", split_axis=0, concat_axis=2, tiled=True).reshape(
        rows, 3, width
    )
    return (back[:, 0], back[:, 1], back[:, 2])


def forward_micro(weights, block, places):
    (
        qkv_weight,
        out_weight,
        gate_weight,
        up_weight,
        down_weight,
        gain1,
        shift1,
        gain2,
        shift2,
        scale1,
        scale2,
    ) = weights
    rows, width = block.shape
    start_in = block.astype(jnp.float32)
    normed1, unit1, inverse1 = normalize(start_in, gain1, shift1)
    acted1 = normed1.astype(jnp.bfloat16)
    projected = jnp.dot(acted1, qkv_weight, preferred_element_type=jnp.float32)
    angles = angles_of(places, HD)
    query = rotate(projected[:, :width].reshape(rows, H, HD), angles).astype(jnp.bfloat16)
    keyset = rotate(projected[:, width : 2 * width].reshape(rows, H, HD), angles).astype(
        jnp.bfloat16
    )
    valueset = projected[:, 2 * width :].astype(jnp.bfloat16)
    attended, kept = attention_forward(query, keyset, valueset, places)
    attn = jnp.dot(attended, out_weight, preferred_element_type=jnp.float32)
    mid = start_in + scale1 * attn
    normed2, unit2, inverse2 = normalize(mid, gain2, shift2)
    acted2 = normed2.astype(jnp.bfloat16)
    gate = jnp.dot(acted2, gate_weight, preferred_element_type=jnp.float32)
    up_value = jnp.dot(acted2, up_weight, preferred_element_type=jnp.float32)
    hidden = (jax.nn.silu(gate) * up_value).astype(jnp.bfloat16)
    branch = jnp.dot(hidden, down_weight, preferred_element_type=jnp.float32)
    result = (mid + scale2 * branch).astype(jnp.bfloat16)
    saved = (
        acted1,
        unit1,
        inverse1,
        angles,
        kept,
        attended,
        attn,
        unit2,
        inverse2,
        acted2,
        gate,
        up_value,
        hidden,
        branch,
    )
    return (result, saved)


def backward_micro(weights, saved, cotangent):
    (
        qkv_weight,
        out_weight,
        gate_weight,
        up_weight,
        down_weight,
        gain1,
        shift1,
        gain2,
        shift2,
        scale1,
        scale2,
    ) = weights
    (
        acted1,
        unit1,
        inverse1,
        angles,
        kept,
        attended,
        attn,
        unit2,
        inverse2,
        acted2,
        gate,
        up_value,
        hidden,
        branch,
    ) = saved
    rows, width = attended.shape
    flow = cotangent.astype(jnp.float32)
    grad_branch = (scale2 * flow).astype(jnp.bfloat16)
    grad_scale2 = jnp.sum(flow * branch, axis=0)
    grad_down = jnp.einsum("rf,rd->fd", hidden, grad_branch, preferred_element_type=jnp.float32)
    grad_hidden = jnp.einsum(
        "rd,fd->rf", grad_branch, down_weight, preferred_element_type=jnp.float32
    )
    sigmoid_gate = jax.nn.sigmoid(gate)
    grad_gate = (
        grad_hidden * up_value * sigmoid_gate * (1.0 + gate * (1.0 - sigmoid_gate))
    ).astype(jnp.bfloat16)
    grad_up = (grad_hidden * gate * sigmoid_gate).astype(jnp.bfloat16)
    grad_gate_w = jnp.einsum("rd,rf->df", acted2, grad_gate, preferred_element_type=jnp.float32)
    grad_up_w = jnp.einsum("rd,rf->df", acted2, grad_up, preferred_element_type=jnp.float32)
    grad_acted2 = jnp.einsum(
        "rf,df->rd", grad_gate, gate_weight, preferred_element_type=jnp.float32
    ) + jnp.einsum("rf,df->rd", grad_up, up_weight, preferred_element_type=jnp.float32)
    grad_mid, grad_gain2, grad_shift2 = normalize_back(grad_acted2, unit2, inverse2, gain2)
    grad_mid = flow + grad_mid
    grad_scale1 = jnp.sum(grad_mid * attn, axis=0)
    grad_attn = (scale1 * grad_mid).astype(jnp.bfloat16)
    grad_out_w = jnp.einsum("rd,re->de", attended, grad_attn, preferred_element_type=jnp.float32)
    grad_attended = jnp.einsum(
        "re,de->rd", grad_attn, out_weight, preferred_element_type=jnp.float32
    ).astype(jnp.bfloat16)
    grad_query, grad_keys, grad_values = attention_backward(kept, grad_attended, rows, width)
    query_plain = unrotate(grad_query.astype(jnp.float32).reshape(rows, H, HD), angles).reshape(
        rows, width
    )
    keys_plain = unrotate(grad_keys.astype(jnp.float32).reshape(rows, H, HD), angles).reshape(
        rows, width
    )
    grad_projected = jnp.concatenate(
        [query_plain, keys_plain, grad_values.astype(jnp.float32)], axis=1
    ).astype(jnp.bfloat16)
    grad_qkv_w = jnp.einsum("rd,re->de", acted1, grad_projected, preferred_element_type=jnp.float32)
    grad_acted1 = jnp.einsum(
        "re,de->rd", grad_projected, qkv_weight, preferred_element_type=jnp.float32
    )
    grad_first, grad_gain1, grad_shift1 = normalize_back(grad_acted1, unit1, inverse1, gain1)
    grad_input = (grad_mid + grad_first).astype(jnp.bfloat16)
    terms = (
        grad_qkv_w,
        grad_out_w,
        grad_gate_w,
        grad_up_w,
        grad_down,
        grad_gain1,
        grad_shift1,
        grad_gain2,
        grad_shift2,
        grad_scale1,
        grad_scale2,
    )
    return (grad_input, terms)


def body(
    block_input,
    positions,
    out_grad,
    qkv_weight,
    out_weight,
    gate_weight,
    up_weight,
    down_weight,
    norm1_gain,
    norm1_shift,
    norm2_gain,
    norm2_shift,
    attn_scale,
    mlp_scale,
):
    shards = (
        qkv_weight,
        out_weight,
        gate_weight,
        up_weight,
        down_weight,
        norm1_gain,
        norm1_shift,
        norm2_gain,
        norm2_shift,
        attn_scale,
        mlp_scale,
    )
    devices = lax.axis_size(("dp", "seq"))
    outer = lax.axis_size("dp")
    inner = lax.axis_size("seq")
    packed = pack_shards(shards)
    totals = None
    results = []
    grads_in = []
    for index in range(block_input.shape[0]):
        weights = unpack_gathered(lax.all_gather(packed, ("dp", "seq"), axis=0, tiled=True), shards)
        result, saved = forward_micro(weights, block_input[index], positions[index])
        backward_weights = unpack_gathered(
            lax.all_gather(packed, ("dp", "seq"), axis=0, tiled=True), shards
        )
        grad_input, terms = backward_micro(backward_weights, saved, out_grad[index])
        if totals is None:
            totals = terms
        else:
            totals = tuple(
                (first_term + second_term for first_term, second_term in zip(totals, terms))
            )
        results.append(result)
        grads_in.append(grad_input)
    laid = pack_grads(totals, devices)
    laid = laid.reshape(outer, inner, laid.shape[1])
    partial_sum = lax.psum_scatter(laid.astype(jnp.bfloat16), "dp", scatter_dimension=0, tiled=True)
    summed = lax.psum_scatter(partial_sum, "seq", scatter_dimension=1, tiled=True).astype(
        jnp.float32
    )
    return (jnp.stack(results), jnp.stack(grads_in)) + unpack_summed(summed, shards)


VMEM_BYTES = 64 * 1024 * 1024
BF = jnp.bfloat16
F32 = jnp.float32
MESH = pl.DeviceIdType.MESH
TEAM = 8
PLACES = 256
RELATIONS = [(1, 0, 0), (0, 1, 0), (1, 1, 0), (0, 0, 1), (1, 0, 1), (0, 1, 1), (1, 1, 1)]
ROW_TEAM = (1, 3, 5)
LEG = (None, 0)


def trig_table():
    inverse = 10000.0 ** (-(np.arange(HD // 2, dtype=np.float64) * (2.0 / HD)))
    angles = np.arange(PLACES, dtype=np.float64)[:, None] * inverse[None, :]
    values = np.concatenate([np.cos(angles), np.sin(angles)] * 2, axis=1).astype(np.float32)
    high = values.astype(ml_dtypes.bfloat16)
    rest = (values - high.astype(np.float32)).astype(ml_dtypes.bfloat16)
    return np.concatenate([high, rest], axis=1)


def dot(a, b):
    return lax.dot_general(a, b, (((1,), (0,)), ((), ())), preferred_element_type=F32)


def dot_rows(a, b):
    return lax.dot_general(a, b, (((1,), (1,)), ((), ())), preferred_element_type=F32)


def dot_cols(a, b):
    return lax.dot_general(a, b, (((0,), (0,)), ((), ())), preferred_element_type=F32)


def sigmoid(v):
    return 0.5 * jnp.tanh(0.5 * v) + 0.5


def unit_of(values):
    center = values - jnp.mean(values, axis=-1, keepdims=True)
    inverse = lax.rsqrt(jnp.mean(center * center, axis=-1, keepdims=True) + EPSILON)
    return center * inverse, inverse


def layer_kernel(
    x_ref, g_ref, vec_ref, table_ref, qkv_ref, out_ref, gate_ref, up_ref, down_ref,
    y_ref, dx_ref, vg_ref, fin_a, fin_m, zq_ref, zo_ref, zg_ref, zd_ref,
    vec_all, vecs, gacc, gv_in, gv_z, gv_send, gv_all,
    pack_a, pack_m, w0, w1, w2, outw,
    n1, n2, db, da, qkv, att, probs, dqs, dkv, hid, dgu,
    send_a, recv_c, recv_d, send_b, send_a0, recv_c0, recv_d0,
    stage_q, stage_o, stage_g, stage_d, own_q, own_o, own_g, own_d, gout, gsend,
    side_q, side_o, keep_q, send_q, relay_g, relay_d, relay_q, relay_o,
    mid, attn, trig, pos,
    vec_ss, vec_rs, wr_ss, wr_rs, wa_ss, wa_rs, w_ss, w_rs, o_ss, o_rs, ga_ss, ga_rs, ag_ss, ag_rs,
    ra_ss, ra_rs, rs_ss, rs_rs, go_ss, go_rs, sx_ss, sx_rs, z_ss, z_rs, f_ss, f_rs,
    gv_ss, gv_rs, loc_sem,
):
    dp = lax.axis_index("dp")
    sq = lax.axis_index("seq")
    z, xi, y, c = dp // 2, dp % 2, sq // 2, sq % 2
    me = xi * 4 + sq
    chip = xi * 2 + y

    def copy(src, dst, ss, rs, device):
        return pltpu.make_async_remote_copy(
            src_ref=src, dst_ref=dst, send_sem=ss, recv_sem=rs,
            device_id=device, device_id_type=MESH,
        )

    def span(start, size):
        return pl.ds(pl.multiple_of(start, size), size)

    def team(k):
        kx, ky, kc = RELATIONS[k]
        xx, yy, cc = (xi + kx) % 2, (y + ky) % 2, (c + kc) % 2
        return (z * 2 + xx, yy * 2 + cc), xx * 4 + yy * 2 + cc

    def level(j):
        zz = (z + j) % 4
        return (zz * 2 + xi, sq), zz

    teams = [team(k) for k in range(7)]
    levels = [level(j) for j in range(1, 4)]
    sources = [(z + 4 - j) % 4 for j in range(1, 4)]
    across, beside, sibling = teams[0][0], teams[1][0], teams[3][0]
    chips = [(1 - xi) * 2 + y, xi * 2 + (1 - y), (1 - xi) * 2 + (1 - y)]

    pending = []
    pack_sends = []
    barrier = pltpu.get_barrier_semaphore()
    for device, _ in teams + levels:
        pl.semaphore_signal(barrier, inc=1, device_id=device, device_id_type=MESH)

    for t in range(4):
        for b in range(3):
            pack_a[32 * t : 32 * t + 32, 256 * b : 256 * b + 256] = qkv_ref[
                :, 1024 * b + 256 * t : 1024 * b + 256 * t + 256
            ]
        pack_a[32 * t : 32 * t + 32, 768:1024] = out_ref[:, 256 * t : 256 * t + 256]
    lane = lax.broadcasted_iota(jnp.int32, (8, 128), 1)
    sub = lax.broadcasted_iota(jnp.int32, (8, 128), 0)
    vec_all[z, me] = jnp.where((sub >= 6) | (lane // 32 == me % 4), vec_ref[...], 0.0)
    gacc[...] = jnp.zeros_like(gacc)
    pl.semaphore_wait(barrier, 10)

    def begin(item):
        item.start()
        pending.append(item)

    for k, (device, _) in enumerate(teams):
        begin(copy(vec_all.at[z, me], vec_all.at[z, me], vec_ss.at[k], vec_rs.at[k], device))

    my_rows = span((z * 8 + me) * 32, 32)
    w0[my_rows, :] = pack_a[span(sq * 32, 32), :]
    for i, k in enumerate(ROW_TEAM):
        device, g = teams[k]
        begin(
            copy(pack_a.at[span((g % 4) * 32, 32), :], w0.at[my_rows, :], wr_ss.at[i], wr_rs.at[i],
                 device)
        )
    for t in range(TEAM):
        pack_m[32 * t : 32 * t + 32, 0:512] = gate_ref[:, 512 * t : 512 * t + 512]
        pack_m[32 * t : 32 * t + 32, 512:1024] = up_ref[:, 512 * t : 512 * t + 512]
        pack_m[32 * t : 32 * t + 32, 1024:1536] = down_ref[:, 512 * t : 512 * t + 512]

    jumps = [z == 3, None, z == 0]
    passes = (z == 1) | (z == 2)

    def rise(ref, piece, ss, rs, base):
        for j in (1, 0, 2):
            item = copy(
                ref.at[piece(z)], ref.at[piece(z)], ss.at[base + j], rs.at[base + j], levels[j][0]
            )
            if jumps[j] is None:
                begin(item)
            else:
                pl.when(jnp.logical_not(jumps[j]))(item.start)
                pending.append((jumps[j], item))

    def rise_pass(ref, piece, ss, rs, base):
        arrived = ref.at[piece(sources[1])]
        copy(arrived, arrived, ss.at[base + 1], rs.at[base + 1], levels[1][0]).wait_recv()
        slot = jnp.where(z == 1, 0, 2)
        end = jnp.where(z == 1, 0, 3)
        item = copy(arrived, arrived, ss.at[base + 3], rs.at[base + slot], (end * 2 + xi, sq))
        pl.when(passes)(item.start)
        pending.append((jnp.logical_not(passes), item))

    def rise_wait(ref, piece, ss, rs, base, j):
        arrived = ref.at[piece(sources[j])]
        copy(arrived, arrived, ss.at[base + j], rs.at[base + j], levels[j][0]).wait_recv()

    groups = [(w1, 0, 1024), (w2, 1024, 512)]

    def level_rows(zz):
        return span(zz * 256, 256)

    def weights_out(n):
        ref, first, width = groups[n]
        ref[my_rows, :] = pack_m[span(me * 32, 32), first : first + width]
        for k, (device, g) in enumerate(teams):
            item = copy(
                pack_m.at[span(g * 32, 32), pl.ds(first, width)],
                ref.at[my_rows, :], w_ss.at[n, k], w_rs.at[n, k], device,
            )
            item.start()
            pack_sends.append(item)

    def weights_up(n):
        ref = groups[n][0]
        for k, (device, g) in enumerate(teams):
            rows = span((z * 8 + g) * 32, 32)
            copy(ref.at[rows, :], ref.at[rows, :], w_ss.at[n, k], w_rs.at[n, k], device).wait_recv()
        rise(ref, level_rows, w_ss.at[n], w_rs.at[n], 7)

    def weights_pass(n):
        rise_pass(groups[n][0], level_rows, w_ss.at[n], w_rs.at[n], 7)

    def weights_in(n):
        for j in (0, 2):
            rise_wait(groups[n][0], level_rows, w_ss.at[n], w_rs.at[n], 7, j)

    halves = [pl.ds(0, 768), pl.ds(768, 256)]

    def slab(n, zz, xx):
        return span((zz * 2 + xx) * 128, 128), halves[n]

    def slab_up(n):
        rise(w0, lambda zz: slab(n, zz, xi), wa_ss.at[n], wa_rs.at[n], 0)
        mine = w0.at[slab(n, z, xi)]
        begin(copy(mine, mine, wa_ss.at[n, 4], wa_rs.at[n, 4], across))

    def slab_pass(n):
        rise_pass(w0, lambda zz: slab(n, zz, xi), wa_ss.at[n], wa_rs.at[n], 0)
        for j in (1, 0, 2):
            if j != 1:
                rise_wait(w0, lambda zz: slab(n, zz, xi), wa_ss.at[n], wa_rs.at[n], 0, j)
            block = w0.at[slab(n, sources[j], xi)]
            begin(copy(block, block, wa_ss.at[n, 5 + j], wa_rs.at[n, 5 + j], across))

    def slab_in(n):
        for j in range(4):
            block = w0.at[slab(n, z if j == 0 else sources[j - 1], 1 - xi)]
            copy(block, block, wa_ss.at[n, 4 + j], wa_rs.at[n, 4 + j], across).wait_recv()

    for k, (device, g) in enumerate(teams):
        copy(vec_all.at[z, g], vec_all.at[z, g], vec_ss.at[k], vec_rs.at[k], device).wait_recv()
    for j, (device, _) in enumerate(levels):
        begin(copy(vec_all.at[z], vec_all.at[z], vec_ss.at[7 + j], vec_rs.at[7 + j], device))
    for i, k in enumerate(ROW_TEAM):
        device, g = teams[k]
        rows = w0.at[span((z * 8 + g) * 32, 32), :]
        copy(rows, rows, wr_ss.at[i], wr_rs.at[i], device).wait_recv()
    slab_up(0)
    weights_out(0)
    for j in range(3):
        block = vec_all.at[sources[j]]
        copy(block, block, vec_ss.at[7 + j], vec_rs.at[7 + j], levels[j][0]).wait_recv()
    for k in range(8):
        total = vec_all[k // 2, 4 * (k % 2)]
        for j in range(1, 4):
            total = total + vec_all[k // 2, 4 * (k % 2) + j]
        vecs[:, 128 * k : 128 * k + 128] = total

    def vector(n):
        return vecs[n : n + 1, :]

    def row_rows(m, cc, yy):
        return span(m * 512 + cc * 256 + yy * 128, 128)

    def row_start(ref, e, m):
        block = ref.at[row_rows(m, c, y), :]
        begin(copy(block, block, ga_ss.at[e, m, 0], ga_rs.at[e, m, 0], beside))
        begin(copy(block, block, ga_ss.at[e, m, 1], ga_rs.at[e, m, 1], sibling))

    def row_pass(ref, e, m):
        block = ref.at[row_rows(m, c, 1 - y), :]
        copy(block, block, ga_ss.at[e, m, 0], ga_rs.at[e, m, 0], beside).wait_recv()
        begin(copy(block, block, ga_ss.at[e, m, 2], ga_rs.at[e, m, 2], sibling))

    def row_end(ref, e, m):
        for which, yy in ((1, y), (2, 1 - y)):
            block = ref.at[row_rows(m, 1 - c, yy), :]
            copy(block, block, ga_ss.at[e, m, which], ga_rs.at[e, m, which], sibling).wait_recv()

    def slot_rows(m, cc, place):
        return span(m * 1024 + cc * 512 + place * 128, 128)

    def gather_start(ref, e, m):
        block = ref.at[slot_rows(m, c, chip), :]
        for r in (0, 1, 3):
            begin(copy(block, block, ag_ss.at[e, m, r], ag_rs.at[e, m, r], teams[r][0]))

    def gather_hand(ref, e, m, r):
        block = ref.at[slot_rows(m, c, chips[r]), :]
        copy(block, block, ag_ss.at[e, m, r], ag_rs.at[e, m, r], teams[r][0]).wait_recv()
        begin(copy(block, block, ag_ss.at[e, m, 4 + r], ag_rs.at[e, m, 4 + r], sibling))

    def gather_pass(ref, e, m, last):
        first = 1 - last
        gather_hand(ref, e, m, first)
        block = ref.at[slot_rows(m, c, chips[first]), :]
        begin(copy(block, block, ag_ss.at[e, m, 2], ag_rs.at[e, m, 2], teams[last][0]))
        gather_hand(ref, e, m, last)

    def gather_far(ref, e, m):
        gather_hand(ref, e, m, 2)

    def gather_end(ref, e, m):
        for r in range(4):
            place = chip if r == 3 else chips[r]
            which = 3 if r == 3 else 4 + r
            block = ref.at[slot_rows(m, 1 - c, place), :]
            copy(block, block, ag_ss.at[e, m, which], ag_rs.at[e, m, which], sibling).wait_recv()

    for m in range(2):
        unit, _ = unit_of(x_ref[m].astype(F32))
        n1[row_rows(m, c, y), :] = (unit * vector(0) + vector(1)).astype(BF)
        row_start(n1, 0, m)
    for m in range(2):
        db[slot_rows(m, c, chip), :] = (g_ref[m].astype(F32) * vector(5)).astype(BF)
    gather_start(db, 0, 0)

    def make_trig(index, carry):
        m, slot = index // 4, index % 4
        cc, yy = slot // 2, slot % 2
        row = vec_all[z, xi * 4 + yy * 2 + cc, pl.ds(6 + m, 1), :]
        places = jnp.transpose(jnp.broadcast_to(row, (128, 128)))
        rows = span(index * 128, 128)
        pos[rows, :] = places
        hits = lax.broadcasted_iota(jnp.int32, (128, PLACES), 1).astype(F32) == jnp.concatenate(
            [places, places], axis=1
        )
        both = dot(hits.astype(F32).astype(BF), table_ref[...])
        trig[rows, :] = both[:, :128] + both[:, 128:]
        return carry

    lax.fori_loop(0, 8, make_trig, 0)

    def expand(rows, count):
        both = trig[rows, :]
        front = lax.broadcasted_iota(jnp.int32, (count, 128), 1) % 64 < 32
        cosine = jnp.where(front, both, pltpu.roll(both, 32, 1))
        sine = jnp.where(front, -pltpu.roll(both, 96, 1), both)
        return front, cosine, sine

    def swap(values, front):
        return jnp.where(front, pltpu.roll(values, 96, 1), pltpu.roll(values, 32, 1))

    slab_pass(0)
    slab_up(1)
    weights_up(0)
    row_pass(n1, 0, 0)
    row_pass(n1, 0, 1)
    gather_pass(db, 0, 0, 1)
    weights_out(1)
    slab_in(0)

    first_head = lax.broadcasted_iota(jnp.int32, (128, 128), 1) < 64

    def split_heads(values):
        zero = jnp.zeros_like(values)
        return jnp.concatenate(
            [jnp.where(first_head, values, zero), jnp.where(first_head, zero, values)], axis=0
        )

    def join_heads(values):
        return jnp.where(first_head, values[:128], values[128:])

    def project(m):
        def step(i, carry):
            rows = span(m * 512 + i * 256, 256)
            raw = dot(n1[rows, :], w0[:, 0:768])
            front, cosine, sine = expand(rows, 256)
            for b in range(4):
                part = raw[:, 128 * b : 128 * b + 128]
                qkv[rows, 128 * b : 128 * b + 128] = (
                    part * cosine + swap(part, front) * sine
                ).astype(BF)
            qkv[rows, 512:768] = raw[:, 512:768].astype(BF)
            return carry

        lax.fori_loop(0, 2, step, 0)

    def block_rows(m, s):
        return span(m * 512 + (s % 2) * 256 + (s // 2) * 128, 128)

    def pair(b, p):
        return slice(256 * b + 128 * p, 256 * b + 128 * p + 128)

    def attend(m):
        def step(s, carry):
            rows = block_rows(m, s)
            before = block_rows(m, jnp.maximum(s - 1, 0))
            r = lax.broadcasted_iota(jnp.int32, (128, 256), 0)
            k = lax.broadcasted_iota(jnp.int32, (128, 256), 1)
            back = r + 128 - k
            places = pos[rows, :]
            limit = jnp.minimum(jnp.concatenate([places, places], axis=1).astype(jnp.int32), 127)
            limit = jnp.minimum(limit, s * 128 + r)
            allowed = (back >= 0) & (back <= limit)
            allowed = jnp.concatenate([allowed, allowed], axis=0)
            for p in range(2):
                query = split_heads(qkv[rows, pair(0, p)])
                keys = jnp.concatenate([qkv[before, pair(1, p)], qkv[rows, pair(1, p)]], axis=0)
                held = jnp.concatenate([qkv[before, pair(2, p)], qkv[rows, pair(2, p)]], axis=0)
                scores = dot_rows(query, keys) * (HD ** -0.5)
                scores = jnp.where(allowed, scores, NEGATIVE)
                top = jnp.max(scores, axis=-1, keepdims=True)
                exponent = jnp.exp(scores - top)
                total = jnp.sum(exponent, axis=-1, keepdims=True)
                share = (exponent / total).astype(BF)
                probs[(m * 4 + s) * 2 + p] = share
                att[rows, pair(0, p)] = join_heads(dot(share, held)).astype(BF)
            return carry

        lax.fori_loop(0, 4, step, 0)

    def row_send(e, m):
        return copy(
            send_a0.at[m, span((1 - y) * 128, 128), :], recv_d0.at[m], ra_ss.at[e, m, 1],
            ra_rs.at[e, m, 1], beside,
        )

    def row_scatter(e, m, compute):
        hand = copy(send_b.at[m], recv_c0.at[m], ra_ss.at[e, m, 0], ra_rs.at[e, m, 0], sibling)

        def step(j, carry):
            part = compute(pl.multiple_of(m * 512 + ((c + 1 + j) % 2) * 256, 256))

            @pl.when(j == 0)
            def _():
                send_b[m] = part.astype(BF)
                hand.start()

            @pl.when(j == 1)
            def _():
                hand.wait_recv()
                send_a0[m] = (part + recv_c0[m].astype(F32)).astype(BF)
                row_send(e, m).start()

            return carry

        lax.fori_loop(0, 2, step, 0)
        hand.wait_send()

    def row_scatter_end(e, m):
        row_send(e, m).wait()
        return send_a0[m, span(y * 128, 128), :].astype(F32) + recv_d0[m].astype(F32)

    def scatter(e, m, compute):
        def step(j, carry):
            cc = (c + 1 + j // 2) % 2
            xx = (xi + 1 + j % 2) % 2
            part = compute(pl.multiple_of(m * 1024 + cc * 512 + xx * 256, 256))
            there = span(xx * 256, 256)

            @pl.when(j < 2)
            def _():
                send_b[j] = part.astype(BF)
                copy(
                    send_b.at[j], recv_c.at[e, m, there, :], rs_ss.at[e, m, j], rs_rs.at[e, m, j],
                    sibling,
                ).start()

            @pl.when(j >= 2)
            def _():
                copy(
                    send_b.at[j - 2], recv_c.at[e, m, there, :], rs_ss.at[e, m, j - 2],
                    rs_rs.at[e, m, j - 2], sibling,
                ).wait_recv()
                send_a[m, there, :] = (
                    part + recv_c[e, m, there, :].astype(F32)
                ).astype(BF)

            @pl.when(j == 2)
            def _():
                scatter_send(e, m, 2).start()
                if LEG[e] != 1:
                    scatter_send(e, m, 0).start()

            @pl.when(j == 3)
            def _():
                if LEG[e] != 0:
                    scatter_send(e, m, 1).start()

            return carry

        lax.fori_loop(0, 4, step, 0)
        for j in range(2):
            copy(
                send_b.at[j], recv_c.at[e, m, pl.ds(0, 256), :], rs_ss.at[e, m, j],
                rs_rs.at[e, m, j], sibling,
            ).wait_send()

    def scatter_send(e, m, r):
        rows = span(chips[r] * 128, 128)
        return copy(
            send_a.at[m, rows, :], recv_d.at[e, m, r], rs_ss.at[e, m, 2 + r],
            rs_rs.at[e, m, 2 + r], teams[r if r < 2 or LEG[e] is None else LEG[e]][0],
        )

    def scatter_pass(e, m):
        r = 1 - LEG[e]
        rows = span(chips[r] * 128, 128)
        scatter_send(e, m, 2).wait_recv()
        send_a[m, rows, :] = (
            send_a[m, rows, :].astype(F32) + recv_d[e, m, 2].astype(F32)
        ).astype(BF)
        scatter_send(e, m, r).start()

    def scatter_end(e, m):
        direct = LEG[e] is None
        for r in range(3):
            if r < 2 or direct:
                scatter_send(e, m, r).wait()
            else:
                scatter_send(e, m, r).wait_send()
        total = send_a[m, span(chip * 128, 128), :].astype(F32)
        for r in range(3 if direct else 2):
            total = total + recv_d[e, m, r].astype(F32)
        return total

    def outwards(row):
        return dot(att[pl.ds(row, 256), :], outw[...])

    row_end(n1, 0, 0)
    project(0)
    slab_pass(1)
    attend(0)
    slab_in(1)
    for i, k in enumerate(ROW_TEAM):
        device, g = teams[k]
        begin(
            copy(
                w0.at[span((g % 4) * 256, 256), pl.ds(768, 256)],
                outw.at[:, span(sq * 256, 256)], o_ss.at[i], o_rs.at[i], device,
            )
        )
    outw[:, span(sq * 256, 256)] = w0[span(sq * 256, 256), 768:1024]
    row_end(n1, 0, 1)
    project(1)
    for i, k in enumerate(ROW_TEAM):
        device, g = teams[k]
        copy(
            w0.at[span((g % 4) * 256, 256), pl.ds(768, 256)],
            outw.at[:, span((g % 4) * 256, 256)], o_ss.at[i], o_rs.at[i], device,
        ).wait_recv()
    row_scatter(0, 0, outwards)
    gather_start(db, 0, 1)
    weights_up(1)
    attend(1)
    row_scatter(0, 1, outwards)

    def second_norm(m):
        total = row_scatter_end(0, m)
        attn[m] = total
        middle = x_ref[m].astype(F32) + vector(4) * total
        mid[m] = middle
        unit, _ = unit_of(middle)
        n2[slot_rows(m, c, chip), :] = (unit * vector(2) + vector(3)).astype(BF)

    gather_far(db, 0, 0)
    second_norm(0)
    gather_start(n2, 1, 0)
    gather_pass(db, 0, 1, 0)
    weights_pass(0)
    second_norm(1)
    gather_start(n2, 1, 1)
    gather_pass(n2, 1, 0, 0)
    gather_far(db, 0, 1)
    gather_far(n2, 1, 0)
    gather_pass(n2, 1, 1, 1)
    weights_pass(1)

    def mlp(row):
        rows = pl.ds(row, 256)
        both = dot(n2[rows, :], w1[...])
        d_hidden = dot(db[rows, :], w2[...])
        gate, up = both[:, :512], both[:, 512:]
        sig = sigmoid(gate)
        silu = gate * sig
        hid[rows, :] = (silu * up).astype(BF)
        dgu[rows, 0:512] = (d_hidden * up * sig * (1.0 + gate * (1.0 - sig))).astype(BF)
        dgu[rows, 512:1024] = (d_hidden * silu).astype(BF)
        return dot_rows(dgu[rows, :], w1[...])

    weights_in(0)
    weights_in(1)
    gather_end(db, 0, 0)
    gather_end(n2, 1, 0)
    scatter(0, 0, mlp)
    gather_far(n2, 1, 1)
    gather_end(db, 0, 1)
    gather_end(n2, 1, 1)
    scatter(0, 1, mlp)

    turned = (z == 0) | (z == 2)
    at_end = (z == 0) | (z == 3)

    def target(i):
        inner = jnp.where(i == 3, 1, jnp.where(i == 0, 0, i + 1))
        plain = jnp.where(at_end, i, inner)
        return jnp.where(turned, 3 - plain, plain)

    def descend(n, i, stage, arrive, relay):
        zz = target(i)

        @pl.when(at_end & (i == 0))
        def _():
            via = jnp.where(z == 0, 1, 2)
            copy(stage.at[i], relay, z_ss.at[n, i], z_rs.at[n, 3], (via * 2 + xi, sq)).start()

        @pl.when(jnp.logical_not(at_end & (i == 0)) & (at_end | (i < 2)))
        def _():
            slot = (zz + 3 - z) % 4
            copy(
                stage.at[i], arrive.at[slot], z_ss.at[n, i], z_rs.at[n, slot], (zz * 2 + xi, sq)
            ).start()

    def descend_pass(n, stage, arrive, relay):
        @pl.when(passes)
        def _():
            zz = target(2)
            slot = (zz + 3 - z) % 4
            copy(stage.at[2], relay, z_ss.at[n, 2], z_rs.at[n, 3], levels[0][0]).wait_recv()
            stage[2] = (stage[2].astype(F32) + relay[...].astype(F32)).astype(BF)
            copy(
                stage.at[2], arrive.at[slot], z_ss.at[n, 2], z_rs.at[n, slot], (zz * 2 + xi, sq)
            ).start()

    def weight_grad(n, left, right, stage, own, arrive, relay):
        def step(i, carry):
            part = dot_cols(left[:, span(target(i) * 256, 256)], right[...])

            @pl.when(i < 3)
            def _():
                stage[i] = part.astype(BF)
                descend(n, i, stage, arrive, relay)

            @pl.when(i == 3)
            def _():
                own[...] = part.astype(own.dtype)

            return carry

        lax.fori_loop(0, 4, step, 0)

    weight_grad(0, n2, dgu, stage_g, own_g, zg_ref, relay_g)

    def norm_back(grad, values, gain, row):
        unit, inverse = unit_of(values)
        gacc[row : row + 1, :] += jnp.sum(grad * unit, axis=0, keepdims=True)
        gacc[row + 1 : row + 2, :] += jnp.sum(grad, axis=0, keepdims=True)
        scaled = grad * gain
        return inverse * (
            scaled
            - jnp.mean(scaled, axis=-1, keepdims=True)
            - unit * jnp.mean(scaled * unit, axis=-1, keepdims=True)
        )

    def second_norm_back(m):
        grad = scatter_end(0, m)
        d_mid = g_ref[m].astype(F32) + norm_back(grad, mid[m], vector(2), 2)
        gacc[4:5, :] += jnp.sum(d_mid * attn[m], axis=0, keepdims=True)
        attn[m] = d_mid
        da[row_rows(m, c, y), :] = (vector(4) * d_mid).astype(BF)
        row_start(da, 1, m)

    second_norm_back(0)
    weight_grad(1, db, hid, stage_d, own_d, zd_ref, relay_d)

    def downwards(row):
        return dot_rows(hid[pl.ds(row, 256), :], w2[...])

    def attend_back(m):
        def step(s, carry):
            rows = block_rows(m, s)
            before = block_rows(m, jnp.maximum(s - 1, 0))
            d_att = dot_rows(da[rows, :], outw[...]).astype(BF)
            here = span(s * 128, 128)
            prior = span(jnp.maximum(s - 1, 0) * 128, 128)
            for p in range(2):
                d_heads = split_heads(d_att[:, 128 * p : 128 * p + 128])
                query = split_heads(qkv[rows, pair(0, p)])
                keys = jnp.concatenate([qkv[before, pair(1, p)], qkv[rows, pair(1, p)]], axis=0)
                held = jnp.concatenate([qkv[before, pair(2, p)], qkv[rows, pair(2, p)]], axis=0)
                share = probs[(m * 4 + s) * 2 + p]
                weights = share.astype(F32)
                d_probs = dot_rows(d_heads, held)
                inner = jnp.sum(weights * d_probs, axis=-1, keepdims=True)
                d_scores = (weights * (d_probs - inner) * (HD ** -0.5)).astype(BF)
                dqs[here, pair(0, p)] = join_heads(dot(d_scores, keys))
                d_keys = dot_cols(d_scores, query)
                d_held = dot_cols(share, d_heads)
                dkv[prior, pair(0, p)] += d_keys[:128]
                dkv[prior, pair(1, p)] += d_held[:128]
                dkv[here, pair(0, p)] = d_keys[128:]
                dkv[here, pair(1, p)] = d_held[128:]
            return carry

        lax.fori_loop(0, 4, step, 0)

        def finish(s, carry):
            rows = block_rows(m, s)
            here = span(s * 128, 128)
            front, cosine, sine = expand(rows, 128)
            for b in range(4):
                part = dqs[here, 128 * b : 128 * b + 128] if b < 2 else dkv[here, pair(0, b - 2)]
                qkv[rows, 128 * b : 128 * b + 128] = (
                    part * cosine - swap(part, front) * sine
                ).astype(BF)
            qkv[rows, 512:768] = dkv[here, 256:512].astype(BF)
            return carry

        lax.fori_loop(0, 4, finish, 0)

    def inwards(row):
        return dot_rows(qkv[pl.ds(row, 256), :], w0[:, 0:768])

    dkv[...] = jnp.zeros_like(dkv)
    scatter(1, 0, downwards)
    row_pass(da, 1, 0)
    second_norm_back(1)
    row_end(da, 1, 0)
    attend_back(0)
    row_scatter(1, 0, inwards)
    scatter_pass(1, 0)
    descend_pass(0, stage_g, zg_ref, relay_g)
    scatter(1, 1, downwards)
    row_pass(da, 1, 1)
    row_end(da, 1, 1)
    part = dot_cols(att[...], da[...])
    for u in range(4):
        gsend[u] = part[:, 256 * u : 256 * u + 256].astype(BF)
    gout[span(sq * 256, 256), :] = gsend[sq]
    for i, k in enumerate(ROW_TEAM):
        device, g = teams[k]
        begin(
            copy(gsend.at[g % 4], gout.at[span(sq * 256, 256), :], go_ss.at[i], go_rs.at[i], device)
        )

    attend_back(1)
    row_scatter(1, 1, inwards)
    def mine_of(values):
        return jnp.where(xi == 0, values[:128], values[128:])

    def other_of(values):
        return jnp.where(xi == 0, values[128:], values[:128])

    for i, k in enumerate(ROW_TEAM):
        device, g = teams[k]
        theirs = span((g % 4) * 256, 256)
        copy(gsend.at[g % 4], gout.at[theirs, :], go_ss.at[i], go_rs.at[i], device).wait_recv()
    for j in range(4):
        zz = target(j)
        begin(
            copy(
                gout.at[span((zz * 2 + 1 - xi) * 128, 128), :], side_o.at[j], sx_ss.at[1, j],
                sx_rs.at[1, j], across,
            )
        )

    def qkv_grad(j, carry):
        part = dot_cols(n1[:, span(target(j) * 256, 256)], qkv[...])
        send_q[j] = other_of(part).astype(BF)
        copy(send_q.at[j], side_q.at[j], sx_ss.at[0, j], sx_rs.at[0, j], across).start()
        keep_q[j] = mine_of(part).astype(BF)
        return carry

    lax.fori_loop(0, 4, qkv_grad, 0)


    def summed(n, i, mine, side, stage, own, arrive, relay):
        copy(side.at[i], side.at[i], sx_ss.at[n, i], sx_rs.at[n, i], across).wait_recv()
        total = mine + side[i].astype(F32)
        if i < 3:
            stage[i] = total.astype(BF)
            descend(2 + n, i, stage, arrive, relay)
        else:
            own[...] = total

    def sum_q(i):
        summed(0, i, keep_q[i].astype(F32), side_q, stage_q, own_q, zq_ref, relay_q)

    def sum_o(i):
        part = gout[span((target(i) * 2 + xi) * 128, 128), :].astype(F32)
        summed(1, i, part, side_o, stage_o, own_o, zo_ref, relay_o)

    def summed_levels(n, stage, own, arrive):
        for i in range(3):
            copy(stage.at[i], arrive.at[i], z_ss.at[n, i], z_rs.at[n, i], levels[0][0]).wait_send()
        loads = [pltpu.make_async_copy(arrive.at[j], stage.at[j], loc_sem.at[j]) for j in range(3)]
        absent = [z == 0, None, z == 3]
        for j in range(3):
            def load(j=j):
                copy(
                    stage.at[j], arrive.at[j], z_ss.at[n, j], z_rs.at[n, j], levels[0][0]
                ).wait_recv()
                loads[j].start()

            def clear(j=j):
                stage[j] = jnp.zeros(stage.shape[1:], BF)

            if absent[j] is None:
                load()
            else:
                pl.when(jnp.logical_not(absent[j]))(load)
                pl.when(absent[j])(clear)
        for j in range(3):
            if absent[j] is None:
                loads[j].wait()
            else:
                pl.when(jnp.logical_not(absent[j]))(loads[j].wait)
        total = own[...].astype(F32)
        for j in range(3):
            total = total + stage[j].astype(F32)
        return total.astype(BF)

    def last_copies(n, pack, first, width, fin, people, who):
        found = []
        for i, k in enumerate(people):
            device, g = teams[k]
            found.append(
                copy(
                    pack.at[span((g % who) * 32, 32), pl.ds(first, width)],
                    fin.at[me % who, :, pl.ds(first, width)], f_ss.at[n, i], f_rs.at[n, i], device,
                )
            )
        return found

    def finals(n, first, width, stage, own, arrive, pack, fin, people, who):
        pack[:, first : first + width] = summed_levels(n, stage, own, arrive)
        stay = pltpu.make_async_copy(
            pack.at[span((me % who) * 32, 32), pl.ds(first, width)],
            fin.at[me % who, :, pl.ds(first, width)], loc_sem.at[3],
        )
        stay.start()
        for item in last_copies(n, pack, first, width, fin, people, who):
            item.start()
        stay.wait()

    plans = [
        (0, 0, 1024, stage_g, own_g, zg_ref, pack_m, fin_m, range(7), 8),
        (1, 1024, 512, stage_d, own_d, zd_ref, pack_m, fin_m, range(7), 8),
        (3, 768, 256, stage_o, own_o, zo_ref, pack_a, fin_a, ROW_TEAM, 4),
        (2, 0, 768, stage_q, own_q, zq_ref, pack_a, fin_a, ROW_TEAM, 4),
    ]
    def first_norm_back(m):
        grad = row_scatter_end(1, m)
        back = norm_back(grad, x_ref[m].astype(F32), vector(0), 0)
        dx_ref[m] = (attn[m] + back).astype(BF)

    def result(m):
        branch = scatter_end(1, m)
        gacc[5:6, :] += jnp.sum(g_ref[m].astype(F32) * branch, axis=0, keepdims=True)
        y_ref[m] = (mid[m] + vector(5) * branch).astype(BF)

    for i in range(4):
        sum_o(i)
    descend_pass(1, stage_d, zd_ref, relay_d)
    sum_q(0)
    scatter_pass(1, 1)
    sum_q(1)
    first_norm_back(0)
    sum_q(2)
    descend_pass(2, stage_q, zq_ref, relay_q)
    descend_pass(3, stage_o, zo_ref, relay_o)
    first_norm_back(1)
    sum_q(3)
    result(0)
    result(1)
    for k in range(8):
        gv_send[k] = gacc[:, 128 * k : 128 * k + 128]
    for k, (device, g) in enumerate(teams):
        begin(copy(gv_send.at[g], gv_in.at[k], gv_ss.at[k], gv_rs.at[k], device))

    for item in pack_sends:
        item.wait_send()
    finals(*plans[0])
    for item in pending:
        if isinstance(item, tuple):
            pl.when(jnp.logical_not(item[0]))(item[1].wait_send)
        else:
            item.wait_send()
    for j in range(4):
        copy(send_q.at[j], side_q.at[j], sx_ss.at[0, j], sx_rs.at[0, j], across).wait_send()
    for k, (device, g) in enumerate(teams):
        copy(gv_send.at[g], gv_in.at[k], gv_ss.at[k], gv_rs.at[k], device).wait_recv()
    total = gv_send[me]
    for k in range(7):
        total = total + gv_in[k]
    gv_z[0] = total
    level_sends = []
    for j, (device, _) in enumerate(levels):
        item = copy(gv_z.at[0], gv_z.at[1 + j], gv_ss.at[7 + j], gv_rs.at[7 + j], device)
        item.start()
        level_sends.append(item)
    finals(*plans[1])
    for item in level_sends:
        item.wait()
    gv_all[me] = gv_z[0] + gv_z[1] + gv_z[2] + gv_z[3]
    for k, (device, g) in enumerate(teams):
        copy(gv_all.at[me], gv_all.at[me], gv_ss.at[10 + k], gv_rs.at[10 + k], device).start()
    finals(*plans[2])
    finals(*plans[3])
    for k, (device, g) in enumerate(teams):
        copy(gv_all.at[g], gv_all.at[g], gv_ss.at[10 + k], gv_rs.at[10 + k], device).wait()
    vg_ref[...] = gv_all[z * 2 + me // 4]
    for n, first, width, _, _, _, pack, fin, people, who in plans:
        for item in last_copies(n, pack, first, width, fin, people, who):
            item.wait()


def layer_fast(
    block_input,
    positions,
    out_grad,
    qkv_weight,
    out_weight,
    gate_weight,
    up_weight,
    down_weight,
    norm1_gain,
    norm1_shift,
    norm2_gain,
    norm2_shift,
    attn_scale,
    mlp_scale,
):
    vectors = jnp.stack(
        [norm1_gain, norm1_shift, norm2_gain, norm2_shift, attn_scale, mlp_scale]
    ).astype(F32)
    packed = jnp.concatenate([jnp.tile(vectors, (1, 4)), positions.astype(F32)], axis=0)
    vmem, anywhere = pl.BlockSpec(memory_space=pltpu.VMEM), pl.BlockSpec(memory_space=pl.ANY)
    dma = pltpu.SemaphoreType.DMA
    scratch = [
        pltpu.VMEM((4, 8, 8, 128), F32), pltpu.VMEM((8, 1024), F32), pltpu.VMEM((8, 1024), F32),
        pltpu.VMEM((7, 8, 128), F32), pltpu.VMEM((4, 8, 128), F32), pltpu.VMEM((8, 8, 128), F32),
        pltpu.VMEM((8, 8, 128), F32),
        pltpu.VMEM((128, 1024), BF), pltpu.VMEM((256, 1536), BF), pltpu.VMEM((1024, 1024), BF),
        pltpu.VMEM((1024, 1024), BF), pltpu.VMEM((1024, 512), BF), pltpu.VMEM((256, 1024), BF),
        pltpu.VMEM((1024, 1024), BF), pltpu.VMEM((2048, 1024), BF), pltpu.VMEM((2048, 1024), BF),
        pltpu.VMEM((1024, 1024), BF),
        pltpu.VMEM((1024, 768), BF), pltpu.VMEM((1024, 256), BF), pltpu.VMEM((16, 256, 256), BF),
        pltpu.VMEM((512, 256), F32), pltpu.VMEM((512, 512), F32),
        pltpu.VMEM((2048, 512), BF), pltpu.VMEM((2048, 1024), BF),
        pltpu.VMEM((2, 512, 1024), BF), pltpu.VMEM((2, 2, 512, 1024), BF),
        pltpu.VMEM((2, 2, 3, 128, 1024), BF), pltpu.VMEM((2, 256, 1024), BF),
        pltpu.VMEM((2, 256, 1024), BF), pltpu.VMEM((2, 256, 1024), BF),
        pltpu.VMEM((2, 128, 1024), BF),
        pltpu.VMEM((3, 128, 768), BF), pltpu.VMEM((3, 128, 256), BF),
        pltpu.VMEM((3, 256, 1024), BF), pltpu.VMEM((3, 256, 512), BF),
        pltpu.VMEM((128, 768), F32), pltpu.VMEM((128, 256), F32),
        pltpu.VMEM((256, 1024), BF), pltpu.VMEM((256, 512), BF),
        pltpu.VMEM((1024, 256), BF), pltpu.VMEM((4, 256, 256), BF),
        pltpu.VMEM((4, 128, 768), BF), pltpu.VMEM((4, 128, 256), BF),
        pltpu.VMEM((4, 128, 768), BF), pltpu.VMEM((4, 128, 768), BF),
        pltpu.VMEM((256, 1024), BF), pltpu.VMEM((256, 512), BF), pltpu.VMEM((128, 768), BF),
        pltpu.VMEM((128, 256), BF),
        pltpu.VMEM((2, 128, 1024), F32), pltpu.VMEM((2, 128, 1024), F32),
        pltpu.VMEM((1024, 128), F32), pltpu.VMEM((1024, 128), F32),
        dma((10,)), dma((10,)), dma((3,)), dma((3,)), dma((2, 8)), dma((2, 8)), dma((2, 11)), dma((2, 11)),
        dma((3,)), dma((3,)), dma((2, 2, 3)), dma((2, 2, 3)), dma((2, 2, 7)), dma((2, 2, 7)),
        dma((2, 2, 2)), dma((2, 2, 2)), dma((2, 2, 5)), dma((2, 2, 5)), dma((3,)), dma((3,)),
        dma((2, 4)), dma((2, 4)), dma((4, 4)), dma((4, 4)), dma((4, 7)), dma((4, 7)),
        dma((17,)), dma((17,)), dma((4,)),
    ]
    y, dx, vg, fin_a, fin_m = pl.pallas_call(
        layer_kernel,
        out_shape=(
            jax.ShapeDtypeStruct((2, 128, 1024), BF),
            jax.ShapeDtypeStruct((2, 128, 1024), BF),
            jax.ShapeDtypeStruct((8, 128), F32),
            jax.ShapeDtypeStruct((4, 32, 1024), BF),
            jax.ShapeDtypeStruct((8, 32, 1536), BF),
            jax.ShapeDtypeStruct((3, 128, 768), BF),
            jax.ShapeDtypeStruct((3, 128, 256), BF),
            jax.ShapeDtypeStruct((3, 256, 1024), BF),
            jax.ShapeDtypeStruct((3, 256, 512), BF),
        ),
        in_specs=[vmem] * 9,
        out_specs=(vmem, vmem, vmem) + (anywhere,) * 6,
        scratch_shapes=scratch,
        compiler_params=pltpu.CompilerParams(
            collective_id=0, has_side_effects=True, vmem_limit_bytes=VMEM_BYTES
        ),
        cost_estimate=pl.CostEstimate(
            flops=26_000_000_000, bytes_accessed=8_000_000, transcendentals=4_000_000
        ),
        name="layer",
    )(
        block_input, out_grad, packed, jnp.asarray(trig_table()), qkv_weight, out_weight,
        gate_weight, up_weight, down_weight.T,
    )[:5]
    fin_a, fin_m = fin_a.astype(F32), fin_m.astype(F32)
    grad_qkv = (
        fin_a[:, :, 0:768].reshape(4, 32, 3, 256).transpose(1, 2, 0, 3).reshape(32, 3072)
    )
    grad_out = fin_a[:, :, 768:1024].transpose(1, 0, 2).reshape(32, 1024)
    grad_gate = fin_m[:, :, 0:512].transpose(1, 0, 2).reshape(32, 4096)
    grad_up = fin_m[:, :, 512:1024].transpose(1, 0, 2).reshape(32, 4096)
    grad_down = fin_m[:, :, 1024:1536].transpose(0, 2, 1).reshape(4096, 32)
    part = lax.axis_index(("dp", "seq")) % 4
    vg = lax.dynamic_index_in_dim(vg.reshape(8, 4, 32), part, 1, keepdims=False)
    return (y, dx, grad_qkv, grad_out, grad_gate, grad_up, grad_down) + tuple(
        vg[i] for i in range(6)
    )


def fits(mesh):
    return mesh.shape["dp"] == 8 and mesh.shape["seq"] == 4


def solution(mesh):
    return jax.shard_map(
        layer_fast if fits(mesh) else body,
        mesh=mesh,
        in_specs=(
            P(None, ("dp", "seq"), None),
            P(None, ("dp", "seq")),
            P(None, ("dp", "seq"), None),
            P(("dp", "seq"), None),
            P(("dp", "seq"), None),
            P(("dp", "seq"), None),
            P(("dp", "seq"), None),
            P(None, ("dp", "seq")),
            P(("dp", "seq")),
            P(("dp", "seq")),
            P(("dp", "seq")),
            P(("dp", "seq")),
            P(("dp", "seq")),
            P(("dp", "seq")),
        ),
        out_specs=(
            P(None, ("dp", "seq"), None),
            P(None, ("dp", "seq"), None),
            P(("dp", "seq"), None),
            P(("dp", "seq"), None),
            P(("dp", "seq"), None),
            P(("dp", "seq"), None),
            P(None, ("dp", "seq")),
            P(("dp", "seq")),
            P(("dp", "seq")),
            P(("dp", "seq")),
            P(("dp", "seq")),
            P(("dp", "seq")),
            P(("dp", "seq")),
        ),
        check_vma=False,
    )
```
